512 devices in a mesh: band: 64 (over x, z_hi, y), plane: 8 (over z_lo, core).
Axes of the slice: x: 4, y: 8, z: 8 (z_hi: 2, z_lo: 4; z = z_hi * 4 + z_lo), core: 2. Of those that a mesh axis runs over, the one named last changes fastest.
Arguments:
- orbitals: float32 [64, 128, 128, 128], P('band', 'plane'), may hold values from -6 to 6
- coulomb: bfloat16 [128, 21504], P(None, 'plane'), may hold values from 0.049804688 to 2
- stick_lists: int32 [8, 2688], replicated, may hold values from -1 to 16383, as said below
- roots: int32 [2], replicated, may hold values from 0 to 63
Outputs:
- exchange_field: bfloat16 [64, 128, 128, 128], P('band', 'plane')
The draws below stay inside these ranges and needn't reach their ends.
Inputs may be any that keep to these rules, and one draw needn't show every extreme that they name: `stick_lists`: row o lists, slot by slot, the stick columns h * 128 + g that plane owner o holds, then -1 in its unused slots. The 12288 listed columns are distinct and are those with the smallest sum of squared signed frequencies. Every owner holds at least one stick; one owner holds exactly 2688.
All inputs are finite; a program needn't handle non-finite values.
Results may differ from the reference program's by a relative error of at most 0.0096.
Values may be sent and summed in bfloat16 or wider, within the bound.
A program may use at most 64 MiB of HBM per device.

```python
import math
import jax
import jax.numpy as jnp
from jax import lax

N = 128
BL = 1
STEPS = 2
NB = 64
STICKS = 12288
SLOTS = 2688
N_BAND = 64
N_PLANE = 8


def draw_stick_lists(key, part):
    key = jax.random.fold_in(key, 7)
    key_order, key_mix, key_heavy, key_jitter = jax.random.split(key, 4)
    frequency = jnp.arange(N, dtype=jnp.int32)
    signed_freq = jnp.minimum(frequency, N - frequency)
    radius_sq = (signed_freq[:, None] * signed_freq[:, None] + signed_freq[None, :] * signed_freq[None, :]).reshape(-1)
    shuffled = jax.random.permutation(key_order, N * N).astype(jnp.int32)
    by_radius = shuffled[jnp.argsort(radius_sq[shuffled], stable=True)]
    kept_ids = by_radius[:STICKS]
    kept_ids = kept_ids[jax.random.permutation(key_mix, STICKS)]
    others = N_PLANE - 1
    even_share = (STICKS - SLOTS) // others
    remainder = (STICKS - SLOTS) % others
    offsets_draw = jax.random.randint(key_jitter, (others,), 0, even_share // 4 + 1).astype(jnp.int32)
    jitter = offsets_draw - jnp.roll(offsets_draw, 1)
    other_counts = even_share + jitter + (jnp.arange(others, dtype=jnp.int32) < remainder).astype(jnp.int32)
    heavy_owner = jax.random.randint(key_heavy, (), 0, N_PLANE).astype(jnp.int32)
    owner_ids = jnp.arange(N_PLANE, dtype=jnp.int32)
    other_slot = jnp.clip(jnp.where(owner_ids < heavy_owner, owner_ids, owner_ids - 1), 0, others - 1)
    counts = jnp.where(owner_ids == heavy_owner, SLOTS, other_counts[other_slot]).astype(jnp.int32)
    starts = jnp.cumsum(counts) - counts
    slot_ids = jnp.arange(SLOTS, dtype=jnp.int32)
    gather_at = jnp.clip(starts[:, None] + slot_ids[None, :], 0, STICKS - 1)
    return jnp.where(slot_ids[None, :] < counts[:, None], kept_ids[gather_at], -1).astype(jnp.int32)


def block_levels(key, shape, cuts, least, largest):
    level, own = 1.0, jax.random.fold_in(key, 6)
    for position, parts in cuts:
        heights = jnp.exp(jax.random.uniform(jax.random.fold_in(own, position), (parts,), jnp.float32, least / len(cuts), largest / len(cuts)))
        level = level * jnp.repeat(heights, shape[position] // parts).reshape([-1 if axis == position else 1 for axis in range(len(shape))])
    return level


def bell_draw(own_key, extent, scale, most, pieces=(), held_as=jnp.bfloat16):
    drawn = scale * jax.random.normal(own_key, extent, jnp.float32)
    if pieces:
        drawn = drawn * block_levels(own_key, extent, pieces, -0.22, 0.18)
    return jnp.clip(drawn, -most, most).astype(held_as)


def setup_inputs(seed: int = 0) -> dict:
    splits = jax.random.split(jax.random.key(seed), 5)
    return {
        "orbitals": bell_draw(splits[0], (NB, N, N, N), 1.0, 6.0, ((0, 64), (1, 8)), jnp.float32),
        "coulomb": jnp.clip(jnp.exp(math.log(2.0) - 3.6927934 * jax.random.uniform(splits[1], (N, N_PLANE * SLOTS), jnp.float32) ** block_levels(splits[1], (N, N_PLANE * SLOTS), ((1, 8),), -0.2, 0.2)), 0.049804688, 2.0).astype(jnp.bfloat16),
        "stick_lists": draw_stick_lists(jax.random.fold_in(splits[4], 71), 0),
        "roots": jax.random.randint(splits[3], (STEPS,), 0, N_BAND).astype(jnp.int32),
    }


def cas_table(grid_size):
    row_index = lax.broadcasted_iota(jnp.int32, (grid_size, grid_size), 0)
    col_index = lax.broadcasted_iota(jnp.int32, (grid_size, grid_size), 1)
    angles = (2.0 * math.pi / grid_size) * ((row_index * col_index) % grid_size).astype(jnp.float32)
    return (jnp.cos(angles) + jnp.sin(angles)).astype(jnp.bfloat16)


def reference(orbitals, coulomb, stick_lists, roots):
    grid_size = orbitals.shape[1]
    highest = lax.Precision.HIGHEST
    cas = cas_table(grid_size).astype(jnp.float32)
    flat_ids = stick_lists.reshape(-1)
    is_valid = flat_ids >= 0
    safe_ids = jnp.where(is_valid, flat_ids, 0).astype(jnp.int32)
    target = jnp.where(is_valid, flat_ids, grid_size * grid_size).astype(jnp.int32)
    kernel = coulomb.astype(jnp.float32)
    blocks = [lax.dynamic_slice_in_dim(orbitals, (roots[window_step] * BL).astype(jnp.int32), BL, 0) for window_step in range(STEPS)]
    partners = jnp.concatenate(blocks, 0)

    def potential(pair_grid):
        along_z = jnp.einsum("xyz,gz->xyg", pair_grid, cas, precision=highest).astype(jnp.bfloat16).astype(jnp.float32)
        spectrum = jnp.einsum("xyg,hy->xhg", along_z, cas, precision=highest).astype(jnp.bfloat16)
        spectrum = spectrum.reshape(grid_size, grid_size * grid_size)
        taken = jnp.take(spectrum, safe_ids, axis=1)
        taken = jnp.where(is_valid[None, :], taken, jnp.zeros_like(taken)).astype(jnp.float32)
        scaled = (jnp.dot(cas, taken, precision=highest) * kernel).astype(jnp.bfloat16).astype(jnp.float32)
        returned = (jnp.dot(cas, scaled, precision=highest) / grid_size).astype(jnp.bfloat16)
        field_grid = jnp.zeros((grid_size, grid_size * grid_size), jnp.bfloat16).at[:, target].set(returned, mode="drop")
        field_grid = field_grid.reshape(grid_size, grid_size, grid_size).astype(jnp.float32)
        inverse_y = (jnp.einsum("xhg,yh->xyg", field_grid, cas, precision=highest) / grid_size).astype(jnp.bfloat16).astype(jnp.float32)
        return jnp.einsum("xyg,zg->xyz", inverse_y, cas, precision=highest) / grid_size

    def one_band(orbital):
        accumulated = jnp.zeros(orbital.shape, jnp.float32)
        for member in range(STEPS * BL):
            pair_grid = (orbital * partners[member]).astype(jnp.bfloat16).astype(jnp.float32)
            accumulated = accumulated + partners[member] * potential(pair_grid)
        return accumulated.astype(jnp.bfloat16)

    return lax.map(one_band, orbitals)
```

```python
import functools
import math

import jax
import jax.numpy as jnp
import numpy as np
from jax import lax
from jax.experimental import pallas as pl
from jax.experimental.pallas import tpu as pltpu
from jax.sharding import PartitionSpec as P

NX, NZ, NY = 4, 2, 8
MESH = pl.DeviceIdType.MESH
F32, BF16 = jnp.float32, jnp.bfloat16


def cas_table(n):
    k = np.arange(n)
    angles = 2.0 * math.pi / n * ((k[:, None] * k[None, :]) % n)
    return jnp.asarray(np.cos(angles) + np.sin(angles), F32).astype(BF16)


def dot(a, b):
    return jnp.dot(a, b, preferred_element_type=F32)


def remote(src, dst, send_sem, recv_sem, device):
    return pltpu.make_async_remote_copy(
        src_ref=src, dst_ref=dst, send_sem=send_sem, recv_sem=recv_sem,
        device_id=device, device_id_type=MESH,
    )


def kernel(
    n, n_plane,
    roots_ref, orb_ref, cas_ref, coulomb_ref, ids_ref, out_ref,
    orb16, in_x, sel, in_y, cand, in_z, shared,
    part, in_part, dense, grid_a, grid_b, send_f, recv_f, send_b, recv_b, total,
    s_x, r_x, s_y, r_y, s_z, r_z, s_gy, r_gy, s_gx, r_gx, s_p, r_p, s_f, r_f, s_b, r_b,
):
    width = n // n_plane
    rows = width * n
    chunk_x, chunk_y = rows // NX, rows // (NX * NY)
    band, plane = lax.axis_index("band"), lax.axis_index("plane")
    y = lax.rem(band, NY)
    zh = lax.rem(band // NY, NZ)
    x = band // (NY * NZ)

    def at_band(bx, bz, by):
        return {"band": (bx * NZ + bz) * NY + by}

    def x_peer(d):
        return lax.rem(x + d, NX)

    def y_peer(d):
        return lax.rem(y + d, NY)

    def p_peer(d):
        return lax.rem(plane + d, n_plane)

    barrier = pltpu.get_barrier_semaphore()
    peers = [at_band(x_peer(d), zh, y) for d in range(1, NX)]
    peers += [at_band(x, zh, y_peer(d)) for d in range(1, NY)]
    peers += [at_band(x, lax.rem(zh + d, NZ), y) for d in range(1, NZ)]
    peers += [{"plane": p_peer(d)} for d in range(1, n_plane)]
    for peer in peers:
        pl.semaphore_signal(barrier, inc=1, device_id=peer, device_id_type=MESH)
    orb16[...] = orb_ref[...].astype(BF16)
    pl.semaphore_wait(barrier, len(peers))

    copies = []

    def start(copy):
        copy.start()
        copies.append(copy)
        return copy

    def x_copy(d, target, slot):
        return remote(
            orb16.at[pl.ds(target * chunk_x, chunk_x)], in_x.at[slot],
            s_x.at[d], r_x.at[d], at_band(target, zh, y),
        )

    for d in range(1, NX):
        start(x_copy(d, x_peer(d), x))
    in_x[x] = orb16[pl.ds(x * chunk_x, chunk_x), :]

    ids = ids_ref[...]
    valid = ids >= 0
    id_h = jnp.where(valid, ids // n, -1)
    id_g = jnp.where(valid, lax.rem(ids, n), -1)
    iota = lax.broadcasted_iota(jnp.int32, (n, ids.shape[1]), 0)
    hot_h = iota == id_h
    hot_g = jnp.where(iota == id_g, 1.0, 0.0).astype(BF16)
    coul_rows = coulomb_ref.shape[0]
    for k in range(coul_rows):
        left = jnp.where(hot_h, coulomb_ref[k : k + 1, :], 0.0).astype(BF16)
        flat = lax.dot_general(
            left, hot_g, (((1,), (1,)), ((), ())), preferred_element_type=F32
        ).astype(BF16)
        for o in range(n_plane):
            part[o, k * width : (k + 1) * width, :] = flat[o * width : (o + 1) * width]

    def p_copy(d, target, slot):
        return remote(part.at[target], in_part.at[slot], s_p.at[d], r_p.at[d], {"plane": target})

    for d in range(1, n_plane):
        start(p_copy(d, p_peer(d), plane))
    in_part[plane] = part[plane]

    for d in range(1, NX):
        x_copy(d, x_peer(d), x_peer(NX - d)).wait_recv()
    root = [roots_ref[s] for s in range(2)]
    root_y = [lax.rem(r, NY) for r in root]
    root_z = [lax.rem(r // NY, NZ) for r in root]
    root_x = [r // (NY * NZ) for r in root]
    for s in range(2):
        sel[s] = in_x[root_x[s]]

    def y_copy(d, target, slot):
        return remote(
            sel.at[:, pl.ds(target * chunk_y, chunk_y)], in_y.at[slot],
            s_y.at[d], r_y.at[d], at_band(x, zh, target),
        )

    for d in range(1, NY):
        start(y_copy(d, y_peer(d), y))
    in_y[y] = sel[:, pl.ds(y * chunk_y, chunk_y), :]

    for d in range(1, n_plane):
        p_copy(d, p_peer(d), p_peer(n_plane - d)).wait_recv()
    summed = in_part[0].astype(F32)
    for o in range(1, n_plane):
        summed = summed + in_part[o].astype(F32)
    mine = x * chunk_x + y * chunk_y
    shared[2, pl.ds(mine, chunk_y), :] = summed.astype(BF16)

    for d in range(1, NY):
        y_copy(d, y_peer(d), y_peer(NY - d)).wait_recv()
    for s in range(2):
        cand[s] = in_y[root_y[s], s]
    z_copy = start(remote(cand, in_z, s_z.at[0], r_z.at[0], at_band(x, lax.rem(zh + 1, NZ), y)))
    z_copy.wait_recv()
    for s in range(2):
        shared[s, pl.ds(mine, chunk_y), :] = jnp.where(root_z[s] == zh, cand[s], in_z[s])

    def gy_copy(d, target, owner):
        block = shared.at[:, pl.ds(x * chunk_x + owner * chunk_y, chunk_y)]
        return remote(block, block, s_gy.at[d], r_gy.at[d], at_band(x, zh, target))

    for d in range(1, NY):
        start(gy_copy(d, y_peer(d), y))
    for d in range(1, NY):
        gy_copy(d, y_peer(d), y_peer(NY - d)).wait_recv()

    def gx_copy(d, target, owner):
        block = shared.at[:, pl.ds(owner * chunk_x, chunk_x)]
        return remote(block, block, s_gx.at[d], r_gx.at[d], at_band(target, zh, y))

    for d in range(1, NX):
        start(gx_copy(d, x_peer(d), x))
    for d in range(1, NX):
        gx_copy(d, x_peer(d), x_peer(NX - d)).wait_recv()

    dense[...] = shared[2].astype(F32)
    cas = cas_ref[...]
    group = 4
    block = width * width

    def f_copy(s, d, target, slot):
        return remote(
            send_f.at[s, target], recv_f.at[s, slot], s_f.at[s, d], r_f.at[s, d], {"plane": target}
        )

    def b_copy(s, d, target, slot):
        return remote(
            send_b.at[s, target], recv_b.at[s, slot], s_b.at[s, d], r_b.at[s, d], {"plane": target}
        )

    def forward(s):
        def step(i, _):
            at = pl.ds(pl.multiple_of(i * (group * n), group * n), group * n)
            pair = (orb_ref[at, :] * shared[s, at, :].astype(F32)).astype(BF16)
            along = dot(pair, cas).astype(BF16)
            for k in range(group):
                plane_k = dot(cas, along[k * n : (k + 1) * n])
                grid_a[pl.ds(i * group + k, n, stride=width), :] = plane_k
            return 0

        lax.fori_loop(0, width // group, step, 0)
        for d in range(1, n_plane):
            t = p_peer(d)
            send_f[s, t] = grid_a[pl.ds(pl.multiple_of(t * block, block), block), :].astype(BF16)
            start(f_copy(s, d, t, plane))
        recv_f[s, plane] = grid_a[pl.ds(pl.multiple_of(plane * block, block), block), :].astype(BF16)

    def middle(s):
        for d in range(1, n_plane):
            f_copy(s, d, p_peer(d), p_peer(n_plane - d)).wait_recv()

        def step(i, _):
            for k in range(group):
                h = i * group + k
                sticks = recv_f[s, :, pl.ds(pl.multiple_of(h * width, width), width), :].reshape(n, n)
                scaled = (dot(cas, sticks) * dense[pl.ds(h, n, stride=width), :]).astype(BF16)
                grid_b[pl.ds(h, n, stride=width), :] = dot(cas, scaled) * (1.0 / n)
            return 0

        lax.fori_loop(0, width // group, step, 0)
        for d in range(1, n_plane):
            t = p_peer(d)
            send_b[s, t] = grid_b[pl.ds(pl.multiple_of(t * block, block), block), :].astype(BF16)
            start(b_copy(s, d, t, plane))
        recv_b[s, plane] = grid_b[pl.ds(pl.multiple_of(plane * block, block), block), :].astype(BF16)

    def inverse(s):
        for d in range(1, n_plane):
            b_copy(s, d, p_peer(d), p_peer(n_plane - d)).wait_recv()

        def step(i, _):
            for k in range(group):
                xi = i * group + k
                field = recv_b[s, :, pl.ds(pl.multiple_of(xi * width, width), width), :].reshape(n, n)
                inverse_y = (dot(cas, field) * (1.0 / n)).astype(BF16)
                at = pl.ds(pl.multiple_of(xi * n, n), n)
                term = dot(inverse_y, cas) * (1.0 / n) * shared[s, at, :].astype(F32)
                if s == 0:
                    total[at, :] = term
                else:
                    out_ref[at, :] = (total[at, :] + term).astype(BF16)
            return 0

        lax.fori_loop(0, width // group, step, 0)

    forward(0)
    forward(1)
    middle(0)
    middle(1)
    inverse(0)
    inverse(1)
    for copy in copies:
        copy.wait_send()


def on_device(orbitals, coulomb, stick_lists, roots):
    _, width, n, _ = orbitals.shape
    n_plane = n // width
    rows = width * n
    band = lax.axis_index("band")
    coul_rows = n // (NX * NY)
    place = band // (NY * NZ) * NY + lax.rem(band, NY)
    coul = lax.dynamic_slice_in_dim(coulomb, place * coul_rows, coul_rows, 0).astype(F32)
    ids = lax.dynamic_slice_in_dim(stick_lists, lax.axis_index("plane"), 1, 0)
    chunk_x, chunk_y = rows // NX, rows // (NX * NY)
    block = width * width
    vmem = pl.BlockSpec(memory_space=pltpu.VMEM)
    dma = pltpu.SemaphoreType.DMA
    out = pl.pallas_call(
        functools.partial(kernel, n, n_plane),
        out_shape=jax.ShapeDtypeStruct((rows, n), BF16),
        in_specs=[pl.BlockSpec(memory_space=pltpu.SMEM)] + [vmem] * 4,
        out_specs=vmem,
        scratch_shapes=[
            pltpu.VMEM((rows, n), BF16),
            pltpu.VMEM((NX, chunk_x, n), BF16),
            pltpu.VMEM((2, chunk_x, n), BF16),
            pltpu.VMEM((NY, 2, chunk_y, n), BF16),
            pltpu.VMEM((2, chunk_y, n), BF16),
            pltpu.VMEM((2, chunk_y, n), BF16),
            pltpu.VMEM((3, rows, n), BF16),
            pltpu.VMEM((n_plane, coul_rows * width, n), BF16),
            pltpu.VMEM((n_plane, coul_rows * width, n), BF16),
            pltpu.VMEM((rows, n), F32),
            pltpu.VMEM((rows, n), F32),
            pltpu.VMEM((rows, n), F32),
            pltpu.VMEM((2, n_plane, block, n), BF16),
            pltpu.VMEM((2, n_plane, block, n), BF16),
            pltpu.VMEM((2, n_plane, block, n), BF16),
            pltpu.VMEM((2, n_plane, block, n), BF16),
            pltpu.VMEM((rows, n), F32),
            dma((NX,)), dma((NX,)),
            dma((NY,)), dma((NY,)),
            dma((1,)), dma((1,)),
            dma((NY,)), dma((NY,)),
            dma((NX,)), dma((NX,)),
            dma((n_plane,)), dma((n_plane,)),
            dma((2, n_plane)), dma((2, n_plane)),
            dma((2, n_plane)), dma((2, n_plane)),
        ],
        compiler_params=pltpu.CompilerParams(
            collective_id=0, has_side_effects=True, vmem_limit_bytes=40 * 1024 * 1024
        ),
        name="exchange",
    )(roots, orbitals.reshape(rows, n), cas_table(n), coul, ids)
    return out.reshape(1, width, n, n)


def solution(mesh):
    in_specs = (P("band", "plane", None, None), P(None, "plane"), P(), P())
    out_specs = P("band", "plane", None, None)
    return jax.shard_map(
        on_device, mesh=mesh, in_specs=in_specs, out_specs=out_specs, check_vma=False
    )
```

```python
import functools
import math

import jax
import jax.numpy as jnp
import numpy as np
from jax import lax
from jax.experimental import pallas as pl
from jax.experimental.pallas import tpu as pltpu
from jax.sharding import PartitionSpec as P

NX, NZ, NY = 4, 2, 8
GROUPS = 2
STEPS = 2
MESH = pl.DeviceIdType.MESH
F32, BF16 = jnp.float32, jnp.bfloat16


def cas_table(n):
    k = np.arange(n)
    angles = 2.0 * math.pi / n * ((k[:, None] * k[None, :]) % n)
    return np.asarray(np.cos(angles) + np.sin(angles), np.float32)


def pair_table(n, width):
    cas = cas_table(n)
    half = width // GROUPS
    table = np.zeros((2, n, GROUPS, n // width, 2, half), np.float32)
    by_x = cas.reshape(n, n // width, GROUPS, half).transpose(0, 2, 1, 3)
    for h in range(2):
        table[h, :, :, :, h, :] = by_x
    return table.reshape(2 * n, 2 * n)


def dot(a, b):
    return jnp.dot(a, b, preferred_element_type=F32)


def pick(index, values):
    out = values[0]
    for k in range(1, len(values)):
        out = jnp.where(index == k, values[k], out)
    return out


def remote(src, dst, send_sem, recv_sem, device):
    return pltpu.make_async_remote_copy(
        src_ref=src, dst_ref=dst, send_sem=send_sem, recv_sem=recv_sem,
        device_id=device, device_id_type=MESH,
    )


def kernel(
    n, n_plane,
    roots_ref, orb_hbm, cas_hbm, twin_hbm, coulomb_hbm, ids_hbm, out_ref,
    orb, cas_ref, twin_ref, coulomb, ids_ref,
    orb16, in_x, sel, in_y, cand, in_z, shared,
    part, in_part, coul16, dense, grid_a, grid_b, send_f, recv_f, send_b, recv_b, total,
    s_in, s_x, r_x, s_y, r_y, s_z, r_z, s_gy, r_gy, s_gx, r_gx,
    s_p, r_p, s_dy, r_dy, s_dx, r_dx, s_f, r_f, s_b, r_b,
):
    width = n // n_plane
    rows = width * n
    rows_g = rows // GROUPS
    chunk_x, chunk_y = rows_g // NX, rows_g // (NX * NY)
    band, plane = lax.axis_index("band"), lax.axis_index("plane")
    y = lax.rem(band, NY)
    zh = lax.rem(band // NY, NZ)
    x = band // (NY * NZ)

    def at_band(bx, bz, by):
        return {"band": (bx * NZ + bz) * NY + by}

    def x_peer(d):
        return lax.rem(x + d, NX)

    def y_peer(d):
        return lax.rem(y + d, NY)

    def p_peer(d):
        return lax.rem(plane + d, n_plane)

    barrier = pltpu.get_barrier_semaphore()
    peers = [at_band(x_peer(d), zh, y) for d in range(1, NX)]
    peers += [at_band(x, zh, y_peer(d)) for d in range(1, NY)]
    peers += [at_band(x, lax.rem(zh + d, NZ), y) for d in range(1, NZ)]
    peers += [{"plane": p_peer(d)} for d in range(1, n_plane)]
    for peer in peers:
        pl.semaphore_signal(barrier, inc=1, device_id=peer, device_id_type=MESH)

    coul_rows = n // (NX * NY)
    first_row = (x * NY + y) * coul_rows
    coul_tile = pl.multiple_of(first_row // 16 * 16, 16)
    loads = [
        pltpu.make_async_copy(orb_hbm, orb, s_in.at[0]),
        pltpu.make_async_copy(coulomb_hbm.at[pl.ds(coul_tile, 16)], coulomb, s_in.at[1]),
        pltpu.make_async_copy(ids_hbm, ids_ref, s_in.at[2]),
        pltpu.make_async_copy(cas_hbm, cas_ref, s_in.at[3]),
        pltpu.make_async_copy(twin_hbm, twin_ref, s_in.at[4]),
    ]
    for load in loads:
        load.start()
    loads[0].wait()
    orb16[...] = orb[...].astype(BF16)
    pl.semaphore_wait(barrier, len(peers))

    copies = []

    def start(copy):
        copy.start()
        copies.append(copy)
        return copy

    def x_copy(g, d, target, slot):
        return remote(
            orb16.at[pl.ds(g * rows_g + target * chunk_x, chunk_x)], in_x.at[g, slot],
            s_x.at[g, d], r_x.at[g, d], at_band(target, zh, y),
        )

    def send_x(g):
        for d in range(1, NX):
            start(x_copy(g, d, x_peer(d), x))
        in_x[g, x] = orb16[pl.ds(g * rows_g + x * chunk_x, chunk_x), :]

    def wait_x(g):
        for d in range(1, NX):
            x_copy(g, d, x_peer(d), x_peer(NX - d)).wait_recv()

    root = [roots_ref[s] for s in range(STEPS)]
    root_y = [lax.rem(r, NY) for r in root]
    root_z = [lax.rem(r // NY, NZ) for r in root]
    root_x = [r // (NY * NZ) for r in root]

    def y_copy(g, s, d, target, slot):
        return remote(
            sel.at[g, s, pl.ds(target * chunk_y, chunk_y)], in_y.at[g, s, slot],
            s_y.at[g, s, d], r_y.at[g, s, d], at_band(x, zh, target),
        )

    def send_y(g, s):
        sel[g, s] = pick(root_x[s], [in_x[g, k] for k in range(NX)])
        for d in range(1, NY):
            start(y_copy(g, s, d, y_peer(d), y))
        in_y[g, s, y] = sel[g, s, pl.ds(y * chunk_y, chunk_y), :]

    def z_copy(g, s):
        return remote(
            cand.at[g, s], in_z.at[g, s], s_z.at[g, s], r_z.at[g, s],
            at_band(x, lax.rem(zh + 1, NZ), y),
        )

    def send_z(g, s):
        for d in range(1, NY):
            y_copy(g, s, d, y_peer(d), y_peer(NY - d)).wait_recv()
        cand[g, s] = pick(root_y[s], [in_y[g, s, k] for k in range(NY)])
        start(z_copy(g, s))

    def gy_copy(g, s, d, target, owner):
        block = shared.at[s, pl.ds(g * rows_g + x * chunk_x + owner * chunk_y, chunk_y)]
        return remote(block, block, s_gy.at[g, s, d], r_gy.at[g, s, d], at_band(x, zh, target))

    def send_gy(g, s):
        z_copy(g, s).wait_recv()
        at = pl.ds(g * rows_g + x * chunk_x + y * chunk_y, chunk_y)
        shared[s, at, :] = jnp.where(root_z[s] == zh, cand[g, s], in_z[g, s])
        for d in range(1, NY):
            start(gy_copy(g, s, d, y_peer(d), y))

    def gx_copy(g, s, d, target, owner):
        block = shared.at[s, pl.ds(g * rows_g + owner * chunk_x, chunk_x)]
        return remote(block, block, s_gx.at[g, s, d], r_gx.at[g, s, d], at_band(target, zh, y))

    def send_gx(g, s):
        for d in range(1, NY):
            gy_copy(g, s, d, y_peer(d), y_peer(NY - d)).wait_recv()
        for d in range(1, NX):
            start(gx_copy(g, s, d, x_peer(d), x))

    def p_copy(d, target, slot):
        return remote(part.at[target], in_part.at[slot], s_p.at[d], r_p.at[d], {"plane": target})

    def send_part():
        loads[1].wait()
        loads[2].wait()
        ids = ids_ref[pl.ds(plane, 1), :]
        valid = ids >= 0
        id_h = jnp.where(valid, ids // n, -1)
        id_g = jnp.where(valid, lax.rem(ids, n), -1)
        iota = lax.broadcasted_iota(jnp.int32, (n, ids.shape[1]), 0)
        hot_h = iota == id_h
        hot_g = jnp.where(iota == id_g, 1.0, 0.0).astype(BF16)
        tile = coulomb[...].astype(F32)
        own = tile[:coul_rows]
        for k in range(1, 16 // coul_rows):
            inside = first_row - coul_tile == k * coul_rows
            own = jnp.where(inside, tile[k * coul_rows : (k + 1) * coul_rows], own)
        for k in range(coul_rows):
            left = jnp.where(hot_h, own[k : k + 1], 0.0).astype(BF16)
            flat = lax.dot_general(
                left, hot_g, (((1,), (1,)), ((), ())), preferred_element_type=F32
            ).astype(BF16)
            for o in range(n_plane):
                part[o, k * width : (k + 1) * width, :] = flat[o * width : (o + 1) * width]
        for d in range(1, n_plane):
            start(p_copy(d, p_peer(d), plane))
        in_part[plane] = part[plane]

    coul_x, coul_y = rows // NX, rows // (NX * NY)

    def dy_copy(d, target, owner):
        block = coul16.at[pl.ds(x * coul_x + owner * coul_y, coul_y)]
        return remote(block, block, s_dy.at[d], r_dy.at[d], at_band(x, zh, target))

    def send_dy():
        for d in range(1, n_plane):
            p_copy(d, p_peer(d), p_peer(n_plane - d)).wait_recv()
        summed = in_part[0].astype(F32)
        for o in range(1, n_plane):
            summed = summed + in_part[o].astype(F32)
        coul16[pl.ds(x * coul_x + y * coul_y, coul_y), :] = summed.astype(BF16)
        for d in range(1, NY):
            start(dy_copy(d, y_peer(d), y))

    def dx_copy(d, target, owner):
        block = coul16.at[pl.ds(owner * coul_x, coul_x)]
        return remote(block, block, s_dx.at[d], r_dx.at[d], at_band(target, zh, y))

    def send_dx():
        for d in range(1, NY):
            dy_copy(d, y_peer(d), y_peer(NY - d)).wait_recv()
        for d in range(1, NX):
            start(dx_copy(d, x_peer(d), x))

    def wait_dense():
        for d in range(1, NX):
            dx_copy(d, x_peer(d), x_peer(NX - d)).wait_recv()
        dense[...] = coul16[...].astype(F32)

    half = width // GROUPS
    block_f, block_b = width * half, width * half

    def f_copy(g, s, d, target, slot):
        return remote(
            send_f.at[s, g, target], recv_f.at[s, g, slot],
            s_f.at[g, s, d], r_f.at[g, s, d], {"plane": target},
        )

    def forward(g, s):
        for d in range(1, NX):
            gx_copy(g, s, d, x_peer(d), x_peer(NX - d)).wait_recv()
        cas = cas_ref[...]
        group = 4

        def step(i, _):
            at = pl.ds(pl.multiple_of(g * rows_g + i * (group * n), group * n), group * n)
            pair = (orb[at, :] * shared[s, at, :].astype(F32)).astype(BF16)
            along = dot(pair, cas).astype(BF16)
            for k in range(group):
                plane_k = dot(cas, along[k * n : (k + 1) * n])
                grid_a[pl.ds(i * group + k, n, stride=half), :] = plane_k
            return 0

        lax.fori_loop(0, half // group, step, 0)
        for d in range(1, n_plane):
            t = p_peer(d)
            at = pl.ds(pl.multiple_of(t * block_f, block_f), block_f)
            send_f[s, g, t] = grid_a[at, :].astype(BF16)
            start(f_copy(g, s, d, t, plane))
        at = pl.ds(pl.multiple_of(plane * block_f, block_f), block_f)
        recv_f[s, g, plane] = grid_a[at, :].astype(BF16)

    def b_copy(g, s, d, target, slot):
        return remote(
            send_b.at[s, g, target], recv_b.at[s, g, slot],
            s_b.at[g, s, d], r_b.at[g, s, d], {"plane": target},
        )

    def middle(s):
        for g in range(GROUPS):
            for d in range(1, n_plane):
                f_copy(g, s, d, p_peer(d), p_peer(n_plane - d)).wait_recv()
        cas, twin = cas_ref[...], twin_ref[...]
        unroll = 2

        def step(i, _):
            for k in range(unroll):
                j = i * unroll + k
                at = pl.ds(pl.multiple_of(j * 2 * half, 2 * half), 2 * half)
                sticks = recv_f[s, :, :, at, :].reshape(2 * n, n)
                spectrum = dot(twin, sticks)
                for h in range(2):
                    at = pl.ds(2 * j + h, n, stride=width)
                    scaled = (spectrum[h * n : (h + 1) * n] * dense[at, :]).astype(BF16)
                    grid_b[at, :] = dot(cas, scaled) * (1.0 / n)
            return 0

        lax.fori_loop(0, width // (2 * unroll), step, 0)
        for g in range(GROUPS):
            for d in range(n_plane):
                t = p_peer(d)
                start_row = t * (GROUPS * block_b) + g * block_b
                at = pl.ds(pl.multiple_of(start_row, block_b), block_b)
                if d:
                    send_b[s, g, t] = grid_b[at, :].astype(BF16)
                    start(b_copy(g, s, d, t, plane))
                else:
                    recv_b[s, g, plane] = grid_b[at, :].astype(BF16)

    def inverse(g, s):
        for d in range(1, n_plane):
            b_copy(g, s, d, p_peer(d), p_peer(n_plane - d)).wait_recv()
        cas = cas_ref[...]
        group = 4

        def step(i, _):
            for k in range(group):
                xi = i * group + k
                at = pl.ds(pl.multiple_of(xi * width, width), width)
                field = recv_b[s, g, :, at, :].reshape(n, n)
                inverse_y = (dot(cas, field) * (1.0 / n)).astype(BF16)
                at = pl.ds(pl.multiple_of(g * rows_g + xi * n, n), n)
                term = dot(inverse_y, cas) * (1.0 / n) * shared[s, at, :].astype(F32)
                if s == 0:
                    total[at, :] = term
                else:
                    out_ref[at, :] = (total[at, :] + term).astype(BF16)
            return 0

        lax.fori_loop(0, half // group, step, 0)

    send_x(0)
    send_x(1)
    send_part()
    wait_x(0)
    send_y(0, 0)
    send_z(0, 0)
    wait_x(1)
    send_y(1, 0)
    send_y(0, 1)
    send_y(1, 1)
    send_gy(0, 0)
    send_z(1, 0)
    send_gx(0, 0)
    send_gy(1, 0)
    send_z(0, 1)
    send_gx(1, 0)
    send_gy(0, 1)
    send_z(1, 1)
    loads[3].wait()
    loads[4].wait()
    send_dy()
    forward(0, 0)
    send_gx(0, 1)
    send_gy(1, 1)
    forward(1, 0)
    send_gx(1, 1)
    send_dx()
    forward(0, 1)
    forward(1, 1)
    wait_dense()
    middle(0)
    middle(1)
    inverse(0, 0)
    inverse(1, 0)
    inverse(0, 1)
    inverse(1, 1)
    for copy in copies:
        copy.wait_send()


def on_device(orbitals, coulomb, stick_lists, roots):
    _, width, n, _ = orbitals.shape
    n_plane = n // width
    rows = width * n
    rows_g = rows // GROUPS
    chunk_x, chunk_y = rows_g // NX, rows_g // (NX * NY)
    coul_block = n // (NX * NY) * width
    block = width * width // GROUPS
    hbm = pl.BlockSpec(memory_space=pl.ANY)
    vmem = pl.BlockSpec(memory_space=pltpu.VMEM)
    dma = pltpu.SemaphoreType.DMA

    def pair_of_sems(*shape):
        return [dma(shape), dma(shape)]

    gs = (GROUPS, STEPS)
    spectra = pltpu.VMEM((STEPS, GROUPS, n_plane, block, n), BF16)
    out = pl.pallas_call(
        functools.partial(kernel, n, n_plane),
        out_shape=jax.ShapeDtypeStruct((rows, n), BF16),
        in_specs=[pl.BlockSpec(memory_space=pltpu.SMEM)] + [hbm] * 5,
        out_specs=vmem,
        scratch_shapes=[
            pltpu.VMEM((rows, n), F32),
            pltpu.VMEM((n, n), BF16),
            pltpu.VMEM((2 * n, 2 * n), BF16),
            pltpu.VMEM((16, coulomb.shape[1]), BF16),
            pltpu.VMEM(stick_lists.shape, jnp.int32),
            pltpu.VMEM((rows, n), BF16),
            pltpu.VMEM((GROUPS, NX, chunk_x, n), BF16),
            pltpu.VMEM(gs + (chunk_x, n), BF16),
            pltpu.VMEM(gs + (NY, chunk_y, n), BF16),
            pltpu.VMEM(gs + (chunk_y, n), BF16),
            pltpu.VMEM(gs + (chunk_y, n), BF16),
            pltpu.VMEM((STEPS, rows, n), BF16),
            pltpu.VMEM((n_plane, coul_block, n), BF16),
            pltpu.VMEM((n_plane, coul_block, n), BF16),
            pltpu.VMEM((rows, n), BF16),
            pltpu.VMEM((rows, n), F32),
            pltpu.VMEM((rows_g, n), F32),
            pltpu.VMEM((rows, n), F32),
            spectra, spectra, spectra, spectra,
            pltpu.VMEM((rows, n), F32),
            dma((5,)),
            *pair_of_sems(GROUPS, NX),
            *pair_of_sems(*gs, NY),
            *pair_of_sems(*gs),
            *pair_of_sems(*gs, NY),
            *pair_of_sems(*gs, NX),
            *pair_of_sems(n_plane),
            *pair_of_sems(NY),
            *pair_of_sems(NX),
            *pair_of_sems(*gs, n_plane),
            *pair_of_sems(*gs, n_plane),
        ],
        compiler_params=pltpu.CompilerParams(
            collective_id=0, has_side_effects=True, vmem_limit_bytes=59 * 1024 * 1024
        ),
        name="exchange",
    )(
        roots, orbitals.reshape(rows, n),
        jnp.asarray(cas_table(n)).astype(BF16), jnp.asarray(pair_table(n, width)).astype(BF16),
        coulomb, stick_lists,
    )
    return out.reshape(1, width, n, n)


def solution(mesh):
    in_specs = (P("band", "plane", None, None), P(None, "plane"), P(), P())
    out_specs = P("band", "plane", None, None)
    return jax.shard_map(
        on_device, mesh=mesh, in_specs=in_specs, out_specs=out_specs, check_vma=False
    )
```

```python
import functools
import math

import jax
import jax.numpy as jnp
import numpy as np
from jax import lax
from jax.experimental import pallas as pl
from jax.experimental.pallas import tpu as pltpu
from jax.sharding import PartitionSpec as P

NX, NZ, NY = 4, 2, 8
GROUPS = 2
STEPS = 2
PIECES = 3
MESH = pl.DeviceIdType.MESH
F32, BF16 = jnp.float32, jnp.bfloat16


def cas_table(n):
    k = np.arange(n)
    angles = 2.0 * math.pi / n * ((k[:, None] * k[None, :]) % n)
    return np.asarray(np.cos(angles) + np.sin(angles), np.float32)


def pair_table(n, width):
    cas = cas_table(n)
    half = width // GROUPS
    table = np.zeros((2, n, GROUPS, n // width, 2, half), np.float32)
    by_x = cas.reshape(n, n // width, GROUPS, half).transpose(0, 2, 1, 3)
    for h in range(2):
        table[h, :, :, :, h, :] = by_x
    return table.reshape(2 * n, 2 * n)


def dot(a, b):
    return jnp.dot(a, b, preferred_element_type=F32)


def pick(index, values):
    out = values[0]
    for k in range(1, len(values)):
        out = jnp.where(index == k, values[k], out)
    return out


def remote(src, dst, send_sem, recv_sem, device):
    return pltpu.make_async_remote_copy(
        src_ref=src, dst_ref=dst, send_sem=send_sem, recv_sem=recv_sem,
        device_id=device, device_id_type=MESH,
    )


def kernel(
    n, n_plane,
    roots_ref, orb_hbm, cas_hbm, twin_hbm, coulomb_hbm, ids_hbm, out_ref,
    orb, cas_ref, twin_ref, coulomb, ids_ref,
    orb16, in_x, sel, in_y, cand, in_z, shared,
    flat_sum, part, in_part, coul16, dense, grid_a, grid_b, send_f, recv_f, send_b, recv_b, total,
    s_in, s_x, r_x, s_y, r_y, s_z, r_z, s_gy, r_gy, s_gx, r_gx,
    s_p, r_p, s_dy, r_dy, s_dx, r_dx, s_f, r_f, s_b, r_b,
):
    width = n // n_plane
    rows = width * n
    rows_g = rows // GROUPS
    chunk_x, chunk_y = rows_g // NX, rows_g // (NX * NY)
    band, plane = lax.axis_index("band"), lax.axis_index("plane")
    y = lax.rem(band, NY)
    zh = lax.rem(band // NY, NZ)
    x = band // (NY * NZ)

    def at_band(bx, bz, by):
        return {"band": (bx * NZ + bz) * NY + by}

    def x_peer(d):
        return lax.rem(x + d, NX)

    def y_peer(d):
        return lax.rem(y + d, NY)

    def p_peer(d):
        return lax.rem(plane + d, n_plane)

    barrier = pltpu.get_barrier_semaphore()
    peers = [at_band(x_peer(d), zh, y) for d in range(1, NX)]
    peers += [at_band(x, zh, y_peer(d)) for d in range(1, NY)]
    peers += [at_band(x, lax.rem(zh + d, NZ), y) for d in range(1, NZ)]
    peers += [{"plane": p_peer(d)} for d in range(1, n_plane)]
    for peer in peers:
        pl.semaphore_signal(barrier, inc=1, device_id=peer, device_id_type=MESH)

    coul_rows = n // (NX * NY)
    first_row = (x * NY + y) * coul_rows
    coul_tile = pl.multiple_of(first_row // 16 * 16, 16)
    loads = [
        pltpu.make_async_copy(orb_hbm, orb, s_in.at[0]),
        pltpu.make_async_copy(coulomb_hbm.at[pl.ds(coul_tile, 16)], coulomb, s_in.at[1]),
        pltpu.make_async_copy(ids_hbm, ids_ref, s_in.at[2]),
        pltpu.make_async_copy(cas_hbm, cas_ref, s_in.at[3]),
        pltpu.make_async_copy(twin_hbm, twin_ref, s_in.at[4]),
    ]
    for load in loads:
        load.start()
    loads[0].wait()
    orb16[...] = orb[...].astype(BF16)
    pl.semaphore_wait(barrier, len(peers))

    def start(copy):
        copy.start()

    def arrived(region, sem):
        remote(region, region, sem, sem, {"plane": p_peer(1)}).wait_recv()

    def sent(region, sem):
        remote(region, region, sem, sem, {"plane": p_peer(1)}).wait_send()

    def x_copy(g, target, slot):
        return remote(
            orb16.at[pl.ds(g * rows_g + target * chunk_x, chunk_x)], in_x.at[g, slot],
            s_x.at[g], r_x.at[g], at_band(target, zh, y),
        )

    def send_x(g):
        for d in range(1, NX):
            start(x_copy(g, x_peer(d), x))
        in_x[g, x] = orb16[pl.ds(g * rows_g + x * chunk_x, chunk_x), :]

    def wait_x(g):
        arrived(in_x.at[g, pl.ds(0, NX - 1)], r_x.at[g])

    root = [roots_ref[s] for s in range(STEPS)]
    root_y = [lax.rem(r, NY) for r in root]
    root_z = [lax.rem(r // NY, NZ) for r in root]
    root_x = [r // (NY * NZ) for r in root]

    def y_copy(g, s, target, slot):
        return remote(
            sel.at[g, s, pl.ds(target * chunk_y, chunk_y)], in_y.at[g, s, slot],
            s_y.at[g, s], r_y.at[g, s], at_band(x, zh, target),
        )

    def send_y(g, s):
        sel[g, s] = pick(root_x[s], [in_x[g, k] for k in range(NX)])
        for d in range(1, NY):
            start(y_copy(g, s, y_peer(d), y))
        in_y[g, s, y] = sel[g, s, pl.ds(y * chunk_y, chunk_y), :]

    def z_copy(g, s):
        return remote(
            cand.at[g, s], in_z.at[g, s], s_z.at[g, s], r_z.at[g, s],
            at_band(x, lax.rem(zh + 1, NZ), y),
        )

    def send_z(g, s):
        arrived(in_y.at[g, s, pl.ds(0, NY - 1)], r_y.at[g, s])
        cand[g, s] = pick(root_y[s], [in_y[g, s, k] for k in range(NY)])
        start(z_copy(g, s))

    def gy_copy(g, s, target, owner):
        block = shared.at[s, pl.ds(g * rows_g + x * chunk_x + owner * chunk_y, chunk_y)]
        return remote(block, block, s_gy.at[g, s], r_gy.at[g, s], at_band(x, zh, target))

    def send_gy(g, s):
        z_copy(g, s).wait_recv()
        at = pl.ds(g * rows_g + x * chunk_x + y * chunk_y, chunk_y)
        shared[s, at, :] = jnp.where(root_z[s] == zh, cand[g, s], in_z[g, s])
        for d in range(1, NY):
            start(gy_copy(g, s, y_peer(d), y))

    def gx_copy(g, s, target, owner):
        block = shared.at[s, pl.ds(g * rows_g + owner * chunk_x, chunk_x)]
        return remote(block, block, s_gx.at[g, s], r_gx.at[g, s], at_band(target, zh, y))

    def send_gx(g, s):
        first = g * rows_g + x * chunk_x
        arrived(shared.at[s, pl.ds(first, (NY - 1) * chunk_y)], r_gy.at[g, s])
        for d in range(1, NX):
            start(gx_copy(g, s, x_peer(d), x))

    def p_copy(target, slot):
        return remote(part.at[target], in_part.at[slot], s_p, r_p, {"plane": target})

    slots = ids_ref.shape[1]
    piece = -(-slots // (128 * PIECES)) * 128

    def add_part(i):
        if i == 0:
            loads[1].wait()
            loads[2].wait()
        at = slice(i * piece, min((i + 1) * piece, slots))
        ids = ids_ref[pl.ds(plane, 1), at]
        valid = ids >= 0
        id_h = jnp.where(valid, ids // n, -1)
        id_g = jnp.where(valid, lax.rem(ids, n), -1)
        iota = lax.broadcasted_iota(jnp.int32, (n, ids.shape[1]), 0)
        hot_h = iota == id_h
        hot_g = jnp.where(iota == id_g, 1.0, 0.0).astype(BF16)
        tile = coulomb[:, at].astype(F32)
        own = tile[:coul_rows]
        for k in range(1, 16 // coul_rows):
            inside = first_row - coul_tile == k * coul_rows
            own = jnp.where(inside, tile[k * coul_rows : (k + 1) * coul_rows], own)
        left = jnp.concatenate(
            [jnp.where(hot_h, own[k : k + 1], 0.0).astype(BF16) for k in range(coul_rows)], 0
        )
        flat = lax.dot_general(
            left, hot_g, (((1,), (1,)), ((), ())), preferred_element_type=F32
        )
        flat_sum[...] = flat if i == 0 else flat_sum[...] + flat

    def send_part():
        for k in range(coul_rows):
            for o in range(n_plane):
                at = slice(k * n + o * width, k * n + (o + 1) * width)
                part[o, k * width : (k + 1) * width, :] = flat_sum[at, :].astype(BF16)
        for d in range(1, n_plane):
            start(p_copy(p_peer(d), plane))
        in_part[plane] = part[plane]

    coul_x, coul_y = rows // NX, rows // (NX * NY)

    def dy_copy(target, owner):
        block = coul16.at[pl.ds(x * coul_x + owner * coul_y, coul_y)]
        return remote(block, block, s_dy, r_dy, at_band(x, zh, target))

    def send_dy():
        arrived(in_part.at[pl.ds(0, n_plane - 1)], r_p)
        summed = in_part[0].astype(F32)
        for o in range(1, n_plane):
            summed = summed + in_part[o].astype(F32)
        coul16[pl.ds(x * coul_x + y * coul_y, coul_y), :] = summed.astype(BF16)
        for d in range(1, NY):
            start(dy_copy(y_peer(d), y))

    def dx_copy(target, owner):
        block = coul16.at[pl.ds(owner * coul_x, coul_x)]
        return remote(block, block, s_dx, r_dx, at_band(target, zh, y))

    def send_dx():
        arrived(coul16.at[pl.ds(x * coul_x, (NY - 1) * coul_y)], r_dy)
        for d in range(1, NX):
            start(dx_copy(x_peer(d), x))

    def wait_dense():
        arrived(coul16.at[pl.ds(0, (NX - 1) * coul_x)], r_dx)
        dense[...] = coul16[...].astype(F32)

    half = width // GROUPS
    block_f, block_b = width * half, width * half

    def f_copy(g, s, target, slot):
        return remote(
            send_f.at[s, g, target], recv_f.at[s, g, slot],
            s_f.at[g, s], r_f.at[g, s], {"plane": target},
        )

    def forward(g, s):
        arrived(shared.at[s, pl.ds(g * rows_g, (NX - 1) * chunk_x)], r_gx.at[g, s])
        cas = cas_ref[...]
        group = 4

        def step(i, _):
            at = pl.ds(pl.multiple_of(g * rows_g + i * (group * n), group * n), group * n)
            pair = (orb[at, :] * shared[s, at, :].astype(F32)).astype(BF16)
            along = dot(pair, cas).astype(BF16)
            for k in range(group):
                plane_k = dot(cas, along[k * n : (k + 1) * n])
                grid_a[pl.ds(i * group + k, n, stride=half), :] = plane_k
            return 0

        lax.fori_loop(0, half // group, step, 0)
        for d in range(1, n_plane):
            t = p_peer(d)
            at = pl.ds(pl.multiple_of(t * block_f, block_f), block_f)
            send_f[s, g, t] = grid_a[at, :].astype(BF16)
            start(f_copy(g, s, t, plane))
        at = pl.ds(pl.multiple_of(plane * block_f, block_f), block_f)
        recv_f[s, g, plane] = grid_a[at, :].astype(BF16)

    def b_copy(g, s, target, slot):
        return remote(
            send_b.at[s, g, target], recv_b.at[s, g, slot],
            s_b.at[g, s], r_b.at[g, s], {"plane": target},
        )

    def middle(s):
        for g in range(GROUPS):
            arrived(recv_f.at[s, g, pl.ds(0, n_plane - 1)], r_f.at[g, s])
        cas, twin = cas_ref[...], twin_ref[...]
        unroll = 2

        def step(i, _):
            for k in range(unroll):
                j = i * unroll + k
                at = pl.ds(pl.multiple_of(j * 2 * half, 2 * half), 2 * half)
                sticks = recv_f[s, :, :, at, :].reshape(2 * n, n)
                spectrum = dot(twin, sticks)
                for h in range(2):
                    at = pl.ds(2 * j + h, n, stride=width)
                    scaled = (spectrum[h * n : (h + 1) * n] * dense[at, :]).astype(BF16)
                    grid_b[at, :] = dot(cas, scaled) * (1.0 / n)
            return 0

        lax.fori_loop(0, width // (2 * unroll), step, 0)
        for g in range(GROUPS):
            for d in range(n_plane):
                t = p_peer(d)
                start_row = t * (GROUPS * block_b) + g * block_b
                at = pl.ds(pl.multiple_of(start_row, block_b), block_b)
                if d:
                    send_b[s, g, t] = grid_b[at, :].astype(BF16)
                    start(b_copy(g, s, t, plane))
                else:
                    recv_b[s, g, plane] = grid_b[at, :].astype(BF16)

    def inverse(g, s):
        arrived(recv_b.at[s, g, pl.ds(0, n_plane - 1)], r_b.at[g, s])
        cas = cas_ref[...]
        group = 4

        def step(i, _):
            for k in range(group):
                xi = i * group + k
                at = pl.ds(pl.multiple_of(xi * width, width), width)
                field = recv_b[s, g, :, at, :].reshape(n, n)
                inverse_y = (dot(cas, field) * (1.0 / n)).astype(BF16)
                at = pl.ds(pl.multiple_of(g * rows_g + xi * n, n), n)
                term = dot(inverse_y, cas) * (1.0 / n) * shared[s, at, :].astype(F32)
                if s == 0:
                    total[at, :] = term
                else:
                    out_ref[at, :] = (total[at, :] + term).astype(BF16)
            return 0

        lax.fori_loop(0, half // group, step, 0)

    send_x(0)
    send_x(1)
    add_part(0)
    wait_x(0)
    send_y(0, 0)
    add_part(1)
    send_z(0, 0)
    wait_x(1)
    send_y(1, 0)
    send_gy(0, 0)
    send_z(1, 0)
    add_part(2)
    send_gx(0, 0)
    send_gy(1, 0)
    send_y(0, 1)
    send_part()
    send_gx(1, 0)
    send_y(1, 1)
    send_z(0, 1)
    loads[3].wait()
    forward(0, 0)
    send_gy(0, 1)
    send_z(1, 1)
    forward(1, 0)
    send_gx(0, 1)
    send_gy(1, 1)
    send_dy()
    send_gx(1, 1)
    forward(0, 1)
    send_dx()
    forward(1, 1)
    for g in range(GROUPS):
        sent(in_x.at[g, pl.ds(0, NX - 1)], s_x.at[g])
        for s in range(STEPS):
            sent(in_y.at[g, s, pl.ds(0, NY - 1)], s_y.at[g, s])
            sent(in_z.at[g, s], s_z.at[g, s])
            sent(shared.at[s, pl.ds(0, (NY - 1) * chunk_y)], s_gy.at[g, s])
            sent(shared.at[s, pl.ds(0, (NX - 1) * chunk_x)], s_gx.at[g, s])
    sent(in_part.at[pl.ds(0, n_plane - 1)], s_p)
    loads[4].wait()
    wait_dense()
    middle(0)
    sent(coul16.at[pl.ds(0, (NY - 1) * coul_y)], s_dy)
    sent(coul16.at[pl.ds(0, (NX - 1) * coul_x)], s_dx)
    middle(1)
    for g in range(GROUPS):
        for s in range(STEPS):
            sent(recv_f.at[s, g, pl.ds(0, n_plane - 1)], s_f.at[g, s])
    inverse(0, 0)
    inverse(1, 0)
    inverse(0, 1)
    inverse(1, 1)
    for g in range(GROUPS):
        for s in range(STEPS):
            sent(recv_b.at[s, g, pl.ds(0, n_plane - 1)], s_b.at[g, s])


def on_device(orbitals, coulomb, stick_lists, roots):
    _, width, n, _ = orbitals.shape
    n_plane = n // width
    rows = width * n
    rows_g = rows // GROUPS
    chunk_x, chunk_y = rows_g // NX, rows_g // (NX * NY)
    coul_block = n // (NX * NY) * width
    block = width * width // GROUPS
    hbm = pl.BlockSpec(memory_space=pl.ANY)
    vmem = pl.BlockSpec(memory_space=pltpu.VMEM)
    dma = pltpu.SemaphoreType.DMA

    def pair_of_sems(*shape):
        return [dma(shape), dma(shape)]

    gs = (GROUPS, STEPS)
    spectra = pltpu.VMEM((STEPS, GROUPS, n_plane, block, n), BF16)
    out = pl.pallas_call(
        functools.partial(kernel, n, n_plane),
        out_shape=jax.ShapeDtypeStruct((rows, n), BF16),
        in_specs=[pl.BlockSpec(memory_space=pltpu.SMEM)] + [hbm] * 5,
        out_specs=vmem,
        scratch_shapes=[
            pltpu.VMEM((rows, n), F32),
            pltpu.VMEM((n, n), BF16),
            pltpu.VMEM((2 * n, 2 * n), BF16),
            pltpu.VMEM((16, coulomb.shape[1]), BF16),
            pltpu.VMEM(stick_lists.shape, jnp.int32),
            pltpu.VMEM((rows, n), BF16),
            pltpu.VMEM((GROUPS, NX, chunk_x, n), BF16),
            pltpu.VMEM(gs + (chunk_x, n), BF16),
            pltpu.VMEM(gs + (NY, chunk_y, n), BF16),
            pltpu.VMEM(gs + (chunk_y, n), BF16),
            pltpu.VMEM(gs + (chunk_y, n), BF16),
            pltpu.VMEM((STEPS, rows, n), BF16),
            pltpu.VMEM((n // (NX * NY) * n, n), F32),
            pltpu.VMEM((n_plane, coul_block, n), BF16),
            pltpu.VMEM((n_plane, coul_block, n), BF16),
            pltpu.VMEM((rows, n), BF16),
            pltpu.VMEM((rows, n), F32),
            pltpu.VMEM((rows_g, n), F32),
            pltpu.VMEM((rows, n), F32),
            spectra, spectra, spectra, spectra,
            pltpu.VMEM((rows, n), F32),
            dma((5,)),
            *pair_of_sems(GROUPS),
            *pair_of_sems(*gs),
            *pair_of_sems(*gs),
            *pair_of_sems(*gs),
            *pair_of_sems(*gs),
            dma, dma, dma, dma, dma, dma,
            *pair_of_sems(*gs),
            *pair_of_sems(*gs),
        ],
        compiler_params=pltpu.CompilerParams(
            collective_id=0, has_side_effects=True, vmem_limit_bytes=57 * 1024 * 1024
        ),
        name="exchange",
    )(
        roots, orbitals.reshape(rows, n),
        jnp.asarray(cas_table(n)).astype(BF16), jnp.asarray(pair_table(n, width)).astype(BF16),
        coulomb, stick_lists,
    )
    return out.reshape(1, width, n, n)


def solution(mesh):
    in_specs = (P("band", "plane", None, None), P(None, "plane"), P(), P())
    out_specs = P("band", "plane", None, None)
    return jax.shard_map(
        on_device, mesh=mesh, in_specs=in_specs, out_specs=out_specs, check_vma=False
    )
```

```python
import functools
import math

import jax
import jax.numpy as jnp
import numpy as np
from jax import lax
from jax.experimental import pallas as pl
from jax.experimental.pallas import tpu as pltpu
from jax.sharding import PartitionSpec as P

NX, NZ, NY = 4, 2, 8
STICKS = 12288
GROUPS = 2
STEPS = 2
PIECES = 3
MESH = pl.DeviceIdType.MESH
F32, BF16 = jnp.float32, jnp.bfloat16


def cas_table(n):
    k = np.arange(n)
    angles = 2.0 * math.pi / n * ((k[:, None] * k[None, :]) % n)
    return np.asarray(np.cos(angles) + np.sin(angles), np.float32)


def pair_table(n, width):
    cas = cas_table(n)
    half = width // GROUPS
    table = np.zeros((2, n, GROUPS, n // width, 2, half), np.float32)
    by_x = cas.reshape(n, n // width, GROUPS, half).transpose(0, 2, 1, 3)
    for h in range(2):
        table[h, :, :, :, h, :] = by_x
    return table.reshape(2 * n, 2 * n)


def packing(n, n_plane):
    signed = np.minimum(np.arange(n), n - np.arange(n))
    squares = signed[:, None] ** 2 + signed[None, :] ** 2
    kept = (squares <= np.sort(squares.reshape(-1))[STICKS - 1]).sum(1)
    best = None
    for t in range(1, n // 2 + 1):
        for extra in ([], [n - t + 1]):
            second = [h for h in range(n) if kept[h] and (signed[h] >= t or h in extra)]
            firsts = [h for h in range(n) if kept[h] and h not in second]
            free, mate = sorted(firsts, key=lambda h: -kept[h]), {}
            for h in sorted(second, key=lambda h: -kept[h]):
                host = next((f for f in free if kept[f] + kept[h] <= n), None)
                if host is None:
                    break
                free.remove(host)
                mate[host] = h
            else:
                if best is None or len(firsts) < len(best[0]):
                    best = firsts, mate, t, extra
    firsts, mate, t, extra = best
    per_owner = -(-len(firsts) // (2 * n_plane)) * 2
    table = -np.ones((per_owner * n_plane, 3), np.int64)
    for row, h in enumerate(firsts):
        table[row] = h, mate.get(h, -1), kept[h]
    return table, per_owner, t, (extra or [-1])[0]


def tables(n, n_plane):
    width = n // n_plane
    cas = cas_table(n)
    rows, per_owner, _, _ = packing(n, n_plane)
    order = sorted(range(n), key=lambda g: (min(g, n - g), g > n // 2))
    both = np.concatenate([cas[:, order], cas[:, order[::-1]]], 1)
    first, second = np.zeros((n, n), np.float32), np.zeros((n, n), np.float32)
    for row, (h, other, _) in enumerate(rows):
        if h >= 0:
            first[row] = cas[h]
        if other >= 0:
            second[row] = cas[other]
    wide = np.concatenate([both, pair_table(n, width), np.concatenate([first.T, second.T], 1)], 0)
    slim = np.concatenate([first, second, both.T, cas], 0)
    labels = np.full((n, 128), -7, np.int32)
    for row, (h, other, length) in enumerate(rows):
        place = row // per_owner * width + row % per_owner
        labels[place, 0] = h if h >= 0 else -7
        labels[place, 1] = other if other >= 0 else -7
    labels[:, 2] = n
    labels[: len(rows), 2] = np.where(rows[:, 2] < 0, n, rows[:, 2])
    return jnp.asarray(wide).astype(BF16), jnp.asarray(slim).astype(BF16), jnp.asarray(labels)


def dot(a, b):
    return jnp.dot(a, b, preferred_element_type=F32)


def pick(index, values):
    out = values[0]
    for k in range(1, len(values)):
        out = jnp.where(index == k, values[k], out)
    return out


def remote(src, dst, send_sem, recv_sem, device):
    return pltpu.make_async_remote_copy(
        src_ref=src, dst_ref=dst, send_sem=send_sem, recv_sem=recv_sem,
        device_id=device, device_id_type=MESH,
    )


def kernel(
    n, n_plane,
    roots_ref, orb_hbm, wide_hbm, slim_hbm, labels_hbm, coulomb_hbm, ids_hbm, out_ref,
    orb, wide, slim, labels, coulomb, ids_ref,
    orb16, in_x, sel, in_y, cand, in_z, shared,
    flat_sum, part, in_part, coul16, dense, grid_a, grid_b, send_f, recv_f, send_b, recv_b, total,
    s_in, s_x, r_x, s_y, r_y, s_z, r_z, s_gy, r_gy, s_gx, r_gx,
    s_p, r_p, s_dy, r_dy, s_dx, r_dx, s_f, r_f, s_b, r_b,
):
    width = n // n_plane
    rows = width * n
    rows_g = rows // GROUPS
    _, per_owner, edge, edge_row = packing(n, n_plane)
    n_packed = per_owner * n_plane
    chunk_x, chunk_y = rows_g // NX, rows_g // (NX * NY)
    band, plane = lax.axis_index("band"), lax.axis_index("plane")
    y = lax.rem(band, NY)
    zh = lax.rem(band // NY, NZ)
    x = band // (NY * NZ)

    def at_band(bx, bz, by):
        return {"band": (bx * NZ + bz) * NY + by}

    def x_peer(d):
        return lax.rem(x + d, NX)

    def y_peer(d):
        return lax.rem(y + d, NY)

    def p_peer(d):
        return lax.rem(plane + d, n_plane)

    barrier = pltpu.get_barrier_semaphore()
    peers = [at_band(x_peer(d), zh, y) for d in range(1, NX)]
    peers += [at_band(x, zh, y_peer(d)) for d in range(1, NY)]
    peers += [at_band(x, lax.rem(zh + d, NZ), y) for d in range(1, NZ)]
    peers += [{"plane": p_peer(d)} for d in range(1, n_plane)]
    for peer in peers:
        pl.semaphore_signal(barrier, inc=1, device_id=peer, device_id_type=MESH)

    coul_rows = n // (NX * NY)
    first_row = (x * NY + y) * coul_rows
    coul_tile = pl.multiple_of(first_row // 16 * 16, 16)
    loads = [
        pltpu.make_async_copy(orb_hbm, orb, s_in.at[0]),
        pltpu.make_async_copy(coulomb_hbm.at[pl.ds(coul_tile, 16)], coulomb, s_in.at[1]),
        pltpu.make_async_copy(ids_hbm, ids_ref, s_in.at[2]),
        pltpu.make_async_copy(labels_hbm, labels, s_in.at[3]),
        pltpu.make_async_copy(slim_hbm, slim, s_in.at[4]),
        pltpu.make_async_copy(wide_hbm, wide, s_in.at[5]),
    ]
    for load in loads:
        load.start()
    loads[0].wait()
    orb16[...] = orb[...].astype(BF16)
    pl.semaphore_wait(barrier, len(peers))

    def start(copy):
        copy.start()

    def arrived(region, sem):
        remote(region, region, sem, sem, {"plane": p_peer(1)}).wait_recv()

    def sent(region, sem):
        remote(region, region, sem, sem, {"plane": p_peer(1)}).wait_send()

    def x_copy(g, target, slot):
        return remote(
            orb16.at[pl.ds(g * rows_g + target * chunk_x, chunk_x)], in_x.at[g, slot],
            s_x.at[g], r_x.at[g], at_band(target, zh, y),
        )

    def send_x(g):
        for d in range(1, NX):
            start(x_copy(g, x_peer(d), x))
        in_x[g, x] = orb16[pl.ds(g * rows_g + x * chunk_x, chunk_x), :]

    def wait_x(g):
        arrived(in_x.at[g, pl.ds(0, NX - 1)], r_x.at[g])

    root = [roots_ref[s] for s in range(STEPS)]
    root_y = [lax.rem(r, NY) for r in root]
    root_z = [lax.rem(r // NY, NZ) for r in root]
    root_x = [r // (NY * NZ) for r in root]

    def y_copy(g, s, target, slot):
        return remote(
            sel.at[g, s, pl.ds(target * chunk_y, chunk_y)], in_y.at[g, s, slot],
            s_y.at[g, s], r_y.at[g, s], at_band(x, zh, target),
        )

    def send_y(g, s):
        sel[g, s] = pick(root_x[s], [in_x[g, k] for k in range(NX)])
        for d in range(1, NY):
            start(y_copy(g, s, y_peer(d), y))
        in_y[g, s, y] = sel[g, s, pl.ds(y * chunk_y, chunk_y), :]

    def z_copy(g, s):
        return remote(
            cand.at[g, s], in_z.at[g, s], s_z.at[g, s], r_z.at[g, s],
            at_band(x, lax.rem(zh + 1, NZ), y),
        )

    def send_z(g, s):
        arrived(in_y.at[g, s, pl.ds(0, NY - 1)], r_y.at[g, s])
        cand[g, s] = pick(root_y[s], [in_y[g, s, k] for k in range(NY)])
        start(z_copy(g, s))

    def gy_copy(g, s, target, owner):
        block = shared.at[s, pl.ds(g * rows_g + x * chunk_x + owner * chunk_y, chunk_y)]
        return remote(block, block, s_gy.at[g, s], r_gy.at[g, s], at_band(x, zh, target))

    def send_gy(g, s):
        z_copy(g, s).wait_recv()
        at = pl.ds(g * rows_g + x * chunk_x + y * chunk_y, chunk_y)
        shared[s, at, :] = jnp.where(root_z[s] == zh, cand[g, s], in_z[g, s])
        for d in range(1, NY):
            start(gy_copy(g, s, y_peer(d), y))

    def gx_copy(g, s, target, owner):
        block = shared.at[s, pl.ds(g * rows_g + owner * chunk_x, chunk_x)]
        return remote(block, block, s_gx.at[g, s], r_gx.at[g, s], at_band(target, zh, y))

    def send_gx(g, s):
        first = g * rows_g + x * chunk_x
        arrived(shared.at[s, pl.ds(first, (NY - 1) * chunk_y)], r_gy.at[g, s])
        for d in range(1, NX):
            start(gx_copy(g, s, x_peer(d), x))

    def p_copy(target, slot):
        return remote(part.at[target], in_part.at[slot], s_p, r_p, {"plane": target})

    slots = ids_ref.shape[1]
    piece = -(-slots // (128 * PIECES)) * 128

    def add_part(i):
        if i == 0:
            loads[1].wait()
            loads[2].wait()
            loads[3].wait()
        at = slice(i * piece, min((i + 1) * piece, slots))
        ids = ids_ref[pl.ds(plane, 1), at]
        valid = ids >= 0
        id_h = jnp.where(valid, ids // n, -1)
        id_g = jnp.where(valid, lax.rem(ids, n), 0)
        lane = jnp.where(id_g == 0, 0, jnp.where(id_g <= n // 2, 2 * id_g - 1, 2 * (n - id_g)))
        reverse = (jnp.minimum(id_h, n - id_h) >= edge) | (id_h == edge_row)
        lane = jnp.where(reverse, n - 1 - lane, lane)
        iota = lax.broadcasted_iota(jnp.int32, (n, ids.shape[1]), 0)
        hot_h = (labels[:, 0:1] == id_h) | (labels[:, 1:2] == id_h)
        hot_g = jnp.where(iota == lane, 1.0, 0.0).astype(BF16)
        tile = coulomb[:, at].astype(F32)
        own = tile[:coul_rows]
        for k in range(1, 16 // coul_rows):
            inside = first_row - coul_tile == k * coul_rows
            own = jnp.where(inside, tile[k * coul_rows : (k + 1) * coul_rows], own)
        left = jnp.concatenate(
            [jnp.where(hot_h, own[k : k + 1], 0.0).astype(BF16) for k in range(coul_rows)], 0
        )
        flat = lax.dot_general(
            left, hot_g, (((1,), (1,)), ((), ())), preferred_element_type=F32
        )
        flat_sum[...] = flat if i == 0 else flat_sum[...] + flat

    def send_part():
        for k in range(coul_rows):
            for o in range(n_plane):
                at = slice(k * n + o * width, k * n + (o + 1) * width)
                part[o, k * width : (k + 1) * width, :] = flat_sum[at, :].astype(BF16)
        for d in range(1, n_plane):
            start(p_copy(p_peer(d), plane))
        in_part[plane] = part[plane]

    coul_x, coul_y = rows // NX, rows // (NX * NY)

    def dy_copy(target, owner):
        block = coul16.at[pl.ds(x * coul_x + owner * coul_y, coul_y)]
        return remote(block, block, s_dy, r_dy, at_band(x, zh, target))

    def send_dy():
        arrived(in_part.at[pl.ds(0, n_plane - 1)], r_p)
        summed = in_part[0].astype(F32)
        for o in range(1, n_plane):
            summed = summed + in_part[o].astype(F32)
        coul16[pl.ds(x * coul_x + y * coul_y, coul_y), :] = summed.astype(BF16)
        for d in range(1, NY):
            start(dy_copy(y_peer(d), y))

    def dx_copy(target, owner):
        block = coul16.at[pl.ds(owner * coul_x, coul_x)]
        return remote(block, block, s_dx, r_dx, at_band(target, zh, y))

    def send_dx():
        arrived(coul16.at[pl.ds(x * coul_x, (NY - 1) * coul_y)], r_dy)
        for d in range(1, NX):
            start(dx_copy(x_peer(d), x))

    def wait_dense():
        arrived(coul16.at[pl.ds(0, (NX - 1) * coul_x)], r_dx)
        dense[...] = coul16[...].astype(F32)

    half = width // GROUPS
    block = per_owner * half

    def f_copy(g, s, target, slot):
        return remote(
            send_f.at[s, g, target], recv_f.at[s, g, slot],
            s_f.at[g, s], r_f.at[g, s], {"plane": target},
        )

    def forward(g, s):
        arrived(shared.at[s, pl.ds(g * rows_g, (NX - 1) * chunk_x)], r_gx.at[g, s])
        both = wide[:n, :]
        first, second = slim[:n_packed, :], slim[n : n + n_packed, :]
        in_first = lax.broadcasted_iota(jnp.int32, (n_packed, n), 1) < labels[:n_packed, 2:3]
        group = 4

        def step(i, _):
            at = pl.ds(pl.multiple_of(g * rows_g + i * (group * n), group * n), group * n)
            pair = (orb[at, :] * shared[s, at, :].astype(F32)).astype(BF16)
            along = dot(pair, both).astype(BF16)
            for k in range(group):
                plane_k = along[k * n : (k + 1) * n]
                packed = jnp.where(in_first, dot(first, plane_k[:, :n]), dot(second, plane_k[:, n:]))
                grid_a[pl.ds(i * group + k, n_packed, stride=half), :] = packed
            return 0

        lax.fori_loop(0, half // group, step, 0)
        for d in range(1, n_plane):
            t = p_peer(d)
            send_f[s, g, t] = grid_a[pl.ds(pl.multiple_of(t * block, block), block), :].astype(BF16)
            start(f_copy(g, s, t, plane))
        at = pl.ds(pl.multiple_of(plane * block, block), block)
        recv_f[s, g, plane] = grid_a[at, :].astype(BF16)

    def b_copy(g, s, target, slot):
        return remote(
            send_b.at[s, g, target], recv_b.at[s, g, slot],
            s_b.at[g, s], r_b.at[g, s], {"plane": target},
        )

    def middle(s):
        for g in range(GROUPS):
            arrived(recv_f.at[s, g, pl.ds(0, n_plane - 1)], r_f.at[g, s])
        twin, cas = wide[n : 3 * n, :], slim[4 * n : 5 * n, :]
        for j in range(per_owner // 2):
            at = slice(j * 2 * half, (j + 1) * 2 * half)
            spectrum = dot(twin, recv_f[s, :, :, at, :].reshape(2 * n, n))
            back = []
            for h in range(2):
                coul = dense[pl.ds(2 * j + h, n, stride=width), :]
                scaled = (spectrum[h * n : (h + 1) * n] * coul).astype(BF16)
                back.append((dot(cas, scaled) * (1.0 / n)).reshape(n_plane, GROUPS, half, n))
            for g in range(GROUPS):
                for q in range(n_plane):
                    both = jnp.concatenate([back[0][q, g], back[1][q, g]], 0)
                    send_b[s, g, q, at, :] = both.astype(BF16)
        for g in range(GROUPS):
            for d in range(1, n_plane):
                start(b_copy(g, s, p_peer(d), plane))
            recv_b[s, g, plane] = send_b[s, g, plane]

    def inverse(g, s):
        arrived(recv_b.at[s, g, pl.ds(0, n_plane - 1)], r_b.at[g, s])
        first, second = wide[3 * n :, :n], wide[3 * n :, n:]
        both = slim[2 * n : 4 * n, :]
        in_first = lax.broadcasted_iota(jnp.int32, (n, n), 1) < labels[:, 2:3]
        grid_b[: n_packed * half, :] = recv_b[s, g].reshape(n_packed * half, n).astype(F32)
        group = 4

        def step(i, _):
            for k in range(group):
                xi = i * group + k
                packed = grid_b[pl.ds(xi, n, stride=half), :]
                from_first = dot(first, jnp.where(in_first, packed, 0.0).astype(BF16))
                from_second = dot(second, jnp.where(in_first, 0.0, packed).astype(BF16))
                inverse_y = jnp.concatenate([from_first, from_second], 1) * (1.0 / n)
                at = pl.ds(pl.multiple_of(g * rows_g + xi * n, n), n)
                potential = dot(inverse_y.astype(BF16), both) * (1.0 / n)
                term = potential * shared[s, at, :].astype(F32)
                if s == 0:
                    total[at, :] = term
                else:
                    out_ref[at, :] = (total[at, :] + term).astype(BF16)
            return 0

        lax.fori_loop(0, half // group, step, 0)

    send_x(0)
    send_x(1)
    add_part(0)
    wait_x(0)
    send_y(0, 0)
    add_part(1)
    send_z(0, 0)
    wait_x(1)
    send_y(1, 0)
    send_gy(0, 0)
    send_z(1, 0)
    for i in range(2, PIECES):
        add_part(i)
    send_gx(0, 0)
    send_gy(1, 0)
    send_y(0, 1)
    send_part()
    send_gx(1, 0)
    send_y(1, 1)
    send_z(0, 1)
    loads[4].wait()
    loads[5].wait()
    forward(0, 0)
    send_gy(0, 1)
    send_z(1, 1)
    forward(1, 0)
    send_gx(0, 1)
    send_gy(1, 1)
    send_dy()
    send_gx(1, 1)
    forward(0, 1)
    send_dx()
    forward(1, 1)
    for g in range(GROUPS):
        sent(in_x.at[g, pl.ds(0, NX - 1)], s_x.at[g])
        for s in range(STEPS):
            sent(in_y.at[g, s, pl.ds(0, NY - 1)], s_y.at[g, s])
            sent(in_z.at[g, s], s_z.at[g, s])
            sent(shared.at[s, pl.ds(0, (NY - 1) * chunk_y)], s_gy.at[g, s])
            sent(shared.at[s, pl.ds(0, (NX - 1) * chunk_x)], s_gx.at[g, s])
    sent(in_part.at[pl.ds(0, n_plane - 1)], s_p)
    grid_b[n_packed * half :, :] = jnp.zeros(((n - n_packed) * half, n), F32)
    wait_dense()
    middle(0)
    sent(coul16.at[pl.ds(0, (NY - 1) * coul_y)], s_dy)
    sent(coul16.at[pl.ds(0, (NX - 1) * coul_x)], s_dx)
    middle(1)
    for g in range(GROUPS):
        for s in range(STEPS):
            sent(recv_f.at[s, g, pl.ds(0, n_plane - 1)], s_f.at[g, s])
    inverse(0, 0)
    inverse(1, 0)
    inverse(0, 1)
    inverse(1, 1)
    for g in range(GROUPS):
        for s in range(STEPS):
            sent(recv_b.at[s, g, pl.ds(0, n_plane - 1)], s_b.at[g, s])


def on_device(orbitals, coulomb, stick_lists, roots):
    _, width, n, _ = orbitals.shape
    n_plane = n // width
    rows = width * n
    rows_g = rows // GROUPS
    chunk_x, chunk_y = rows_g // NX, rows_g // (NX * NY)
    coul_block = n // (NX * NY) * width
    per_owner = packing(n, n_plane)[1]
    wide, slim, labels = tables(n, n_plane)
    hbm = pl.BlockSpec(memory_space=pl.ANY)
    vmem = pl.BlockSpec(memory_space=pltpu.VMEM)
    dma = pltpu.SemaphoreType.DMA

    def pair_of_sems(*shape):
        return [dma(shape), dma(shape)]

    gs = (GROUPS, STEPS)
    spectra = pltpu.VMEM((STEPS, GROUPS, n_plane, per_owner * width // GROUPS, n), BF16)
    out = pl.pallas_call(
        functools.partial(kernel, n, n_plane),
        out_shape=jax.ShapeDtypeStruct((rows, n), BF16),
        in_specs=[pl.BlockSpec(memory_space=pltpu.SMEM)] + [hbm] * 6,
        out_specs=vmem,
        scratch_shapes=[
            pltpu.VMEM((rows, n), F32),
            pltpu.VMEM(wide.shape, BF16),
            pltpu.VMEM(slim.shape, BF16),
            pltpu.VMEM(labels.shape, jnp.int32),
            pltpu.VMEM((16, coulomb.shape[1]), BF16),
            pltpu.VMEM(stick_lists.shape, jnp.int32),
            pltpu.VMEM((rows, n), BF16),
            pltpu.VMEM((GROUPS, NX, chunk_x, n), BF16),
            pltpu.VMEM(gs + (chunk_x, n), BF16),
            pltpu.VMEM(gs + (NY, chunk_y, n), BF16),
            pltpu.VMEM(gs + (chunk_y, n), BF16),
            pltpu.VMEM(gs + (chunk_y, n), BF16),
            pltpu.VMEM((STEPS, rows, n), BF16),
            pltpu.VMEM((n // (NX * NY) * n, n), F32),
            pltpu.VMEM((n_plane, coul_block, n), BF16),
            pltpu.VMEM((n_plane, coul_block, n), BF16),
            pltpu.VMEM((rows, n), BF16),
            pltpu.VMEM((rows, n), F32),
            pltpu.VMEM((rows_g, n), F32),
            pltpu.VMEM((rows_g, n), F32),
            spectra, spectra, spectra, spectra,
            pltpu.VMEM((rows, n), F32),
            dma((6,)),
            *pair_of_sems(GROUPS),
            *pair_of_sems(*gs),
            *pair_of_sems(*gs),
            *pair_of_sems(*gs),
            *pair_of_sems(*gs),
            dma, dma, dma, dma, dma, dma,
            *pair_of_sems(*gs),
            *pair_of_sems(*gs),
        ],
        compiler_params=pltpu.CompilerParams(
            collective_id=0, has_side_effects=True, vmem_limit_bytes=57 * 1024 * 1024
        ),
        name="exchange",
    )(
        roots, orbitals.reshape(rows, n),
        wide, slim, labels, coulomb, stick_lists,
    )
    return out.reshape(1, width, n, n)


def solution(mesh):
    in_specs = (P("band", "plane", None, None), P(None, "plane"), P(), P())
    out_specs = P("band", "plane", None, None)
    return jax.shard_map(
        on_device, mesh=mesh, in_specs=in_specs, out_specs=out_specs, check_vma=False
    )
```

```python
import functools
import math

import jax
import jax.numpy as jnp
import numpy as np
from jax import lax
from jax.experimental import pallas as pl
from jax.experimental.pallas import tpu as pltpu
from jax.sharding import PartitionSpec as P

NX, NZ, NY = 4, 2, 8
STICKS = 12288
GROUPS = 2
STEPS = 2
PIECES = 3
MESH = pl.DeviceIdType.MESH
F32, BF16 = jnp.float32, jnp.bfloat16


def cas_table(n):
    k = np.arange(n)
    angles = 2.0 * math.pi / n * ((k[:, None] * k[None, :]) % n)
    return np.asarray(np.cos(angles) + np.sin(angles), np.float32)


def pair_table(n, width):
    cas = cas_table(n)
    half = width // GROUPS
    table = np.zeros((2, n, GROUPS, n // width, 2, half), np.float32)
    by_x = cas.reshape(n, n // width, GROUPS, half).transpose(0, 2, 1, 3)
    for h in range(2):
        table[h, :, :, :, h, :] = by_x
    return table.reshape(2 * n, 2 * n)


def packing(n, n_plane):
    signed = np.minimum(np.arange(n), n - np.arange(n))
    squares = signed[:, None] ** 2 + signed[None, :] ** 2
    kept = (squares <= np.sort(squares.reshape(-1))[STICKS - 1]).sum(1)
    best = None
    for t in range(1, n // 2 + 1):
        for extra in ([], [n - t + 1]):
            second = [h for h in range(n) if kept[h] and (signed[h] >= t or h in extra)]
            firsts = [h for h in range(n) if kept[h] and h not in second]
            free, mate = sorted(firsts, key=lambda h: -kept[h]), {}
            for h in sorted(second, key=lambda h: -kept[h]):
                host = next((f for f in free if kept[f] + kept[h] <= n), None)
                if host is None:
                    break
                free.remove(host)
                mate[host] = h
            else:
                if best is None or len(firsts) < len(best[0]):
                    best = firsts, mate, t, extra
    firsts, mate, t, extra = best
    per_owner = -(-len(firsts) // (2 * n_plane)) * 2
    table = -np.ones((per_owner * n_plane, 3), np.int64)
    for row, h in enumerate(firsts):
        table[row] = h, mate.get(h, -1), kept[h]
    return table, per_owner, t, (extra or [-1])[0]


def tables(n, n_plane):
    width = n // n_plane
    cas = cas_table(n)
    rows, per_owner, _, _ = packing(n, n_plane)
    order = sorted(range(n), key=lambda g: (min(g, n - g), g > n // 2))
    both = np.concatenate([cas[:, order], cas[:, order[::-1]]], 1)
    first, second = np.zeros((n, n), np.float32), np.zeros((n, n), np.float32)
    for row, (h, other, _) in enumerate(rows):
        if h >= 0:
            first[row] = cas[h]
        if other >= 0:
            second[row] = cas[other]
    wide = np.concatenate([both, pair_table(n, width), np.concatenate([first.T, second.T], 1)], 0)
    slim = np.concatenate([first, second, both.T, cas], 0)
    labels = np.full((n, 128), -7, np.int32)
    for row, (h, other, length) in enumerate(rows):
        place = row // per_owner * width + row % per_owner
        labels[place, 0] = h if h >= 0 else -7
        labels[place, 1] = other if other >= 0 else -7
    labels[:, 2] = n
    labels[: len(rows), 2] = np.where(rows[:, 2] < 0, n, rows[:, 2])
    return jnp.asarray(wide).astype(BF16), jnp.asarray(slim).astype(BF16), jnp.asarray(labels)


def dot(a, b):
    return jnp.dot(a, b, preferred_element_type=F32)


def pick(index, values):
    out = values[0]
    for k in range(1, len(values)):
        out = jnp.where(index == k, values[k], out)
    return out


def remote(src, dst, send_sem, recv_sem, device):
    return pltpu.make_async_remote_copy(
        src_ref=src, dst_ref=dst, send_sem=send_sem, recv_sem=recv_sem,
        device_id=device, device_id_type=MESH,
    )


def kernel(
    n, n_plane,
    roots_ref, orb_hbm, wide_hbm, slim_hbm, labels_hbm, coulomb_hbm, ids_hbm, out_ref,
    orb, wide, slim, labels, coulomb, ids_ref,
    orb16, in_x, sel, in_y, cand, in_z, shared,
    flat_sum, part, in_part, coul16, dense, grid_a, grid_b, send_f, recv_f, send_b, recv_b, total,
    s_in, s_x, r_x, s_y, r_y, s_z, r_z, s_gy, r_gy, s_gx, r_gx,
    s_p, r_p, s_dy, r_dy, s_dx, r_dx, s_f, r_f, s_b, r_b,
):
    width = n // n_plane
    rows = width * n
    rows_g = rows // GROUPS
    _, per_owner, edge, edge_row = packing(n, n_plane)
    n_packed = per_owner * n_plane
    chunk_x, chunk_y = rows_g // NX, rows_g // (NX * NY)
    band, plane = lax.axis_index("band"), lax.axis_index("plane")
    y = lax.rem(band, NY)
    zh = lax.rem(band // NY, NZ)
    x = band // (NY * NZ)

    def at_band(bx, bz, by):
        return {"band": (bx * NZ + bz) * NY + by}

    def x_peer(d):
        return lax.rem(x + d, NX)

    def y_peer(d):
        return lax.rem(y + d, NY)

    def p_peer(d):
        return lax.rem(plane + d, n_plane)

    barrier = pltpu.get_barrier_semaphore()
    peers = [at_band(x_peer(d), zh, y) for d in range(1, NX)]
    peers += [at_band(x, zh, y_peer(d)) for d in range(1, NY)]
    peers += [at_band(x, lax.rem(zh + d, NZ), y) for d in range(1, NZ)]
    peers += [{"plane": p_peer(d)} for d in range(1, n_plane)]
    for peer in peers:
        pl.semaphore_signal(barrier, inc=1, device_id=peer, device_id_type=MESH)

    coul_rows = n // (NX * NY)
    first_row = (x * NY + y) * coul_rows
    coul_tile = pl.multiple_of(first_row // 16 * 16, 16)
    loads = [
        pltpu.make_async_copy(orb_hbm, orb, s_in.at[0]),
        pltpu.make_async_copy(coulomb_hbm.at[pl.ds(coul_tile, 16)], coulomb, s_in.at[1]),
        pltpu.make_async_copy(ids_hbm, ids_ref, s_in.at[2]),
        pltpu.make_async_copy(labels_hbm, labels, s_in.at[3]),
        pltpu.make_async_copy(slim_hbm, slim, s_in.at[4]),
        pltpu.make_async_copy(wide_hbm, wide, s_in.at[5]),
    ]
    for load in loads:
        load.start()
    loads[0].wait()
    orb16[...] = orb[...].astype(BF16)
    pl.semaphore_wait(barrier, len(peers))

    def start(copy):
        copy.start()

    def arrived(region, sem):
        remote(region, region, sem, sem, {"plane": p_peer(1)}).wait_recv()

    def sent(region, sem):
        remote(region, region, sem, sem, {"plane": p_peer(1)}).wait_send()

    def x_copy(g, target, slot):
        return remote(
            orb16.at[pl.ds(g * rows_g + target * chunk_x, chunk_x)], in_x.at[g, slot],
            s_x.at[g], r_x.at[g], at_band(target, zh, y),
        )

    def send_x(g):
        for d in range(1, NX):
            start(x_copy(g, x_peer(d), x))
        in_x[g, x] = orb16[pl.ds(g * rows_g + x * chunk_x, chunk_x), :]

    def wait_x(g):
        arrived(in_x.at[g, pl.ds(0, NX - 1)], r_x.at[g])

    root = [roots_ref[s] for s in range(STEPS)]
    root_y = [lax.rem(r, NY) for r in root]
    root_z = [lax.rem(r // NY, NZ) for r in root]
    root_x = [r // (NY * NZ) for r in root]

    def y_copy(g, s, target, slot):
        return remote(
            sel.at[g, s, pl.ds(target * chunk_y, chunk_y)], in_y.at[g, s, slot],
            s_y.at[g, s], r_y.at[g, s], at_band(x, zh, target),
        )

    def send_y(g, s):
        sel[g, s] = pick(root_x[s], [in_x[g, k] for k in range(NX)])
        for d in range(1, NY):
            start(y_copy(g, s, y_peer(d), y))
        in_y[g, s, y] = sel[g, s, pl.ds(y * chunk_y, chunk_y), :]

    def z_copy(g, s):
        return remote(
            cand.at[g, s], in_z.at[g, s], s_z.at[g, s], r_z.at[g, s],
            at_band(x, lax.rem(zh + 1, NZ), y),
        )

    def send_z(g, s):
        arrived(in_y.at[g, s, pl.ds(0, NY - 1)], r_y.at[g, s])
        cand[g, s] = pick(root_y[s], [in_y[g, s, k] for k in range(NY)])
        start(z_copy(g, s))

    def gy_copy(g, s, target, owner):
        block = shared.at[s, pl.ds(g * rows_g + x * chunk_x + owner * chunk_y, chunk_y)]
        return remote(block, block, s_gy.at[g, s], r_gy.at[g, s], at_band(x, zh, target))

    def send_gy(g, s):
        z_copy(g, s).wait_recv()
        at = pl.ds(g * rows_g + x * chunk_x + y * chunk_y, chunk_y)
        shared[s, at, :] = jnp.where(root_z[s] == zh, cand[g, s], in_z[g, s])
        for d in range(1, NY):
            start(gy_copy(g, s, y_peer(d), y))

    left, right, far = x_peer(NX - 1), x_peer(1), x_peer(2)

    def relay_start(rows_of, sems):
        own = rows_of(x, 0, 2)
        start(remote(own, own, sems(0, 0), sems(1, 0), at_band(right, zh, y)))
        start(remote(own, own, sems(0, 1), sems(1, 1), at_band(left, zh, y)))

    def relay_on(rows_of, sems):
        arrived(rows_of(left, 0, 2), sems(1, 0))
        passed = rows_of(left, 0, 1)
        start(remote(passed, passed, sems(0, 2), sems(1, 2), at_band(right, zh, y)))
        arrived(rows_of(right, 0, 2), sems(1, 1))
        passed = rows_of(right, 1, 1)
        start(remote(passed, passed, sems(0, 3), sems(1, 3), at_band(left, zh, y)))

    def relay_end(rows_of, sems):
        arrived(rows_of(far, 0, 1), sems(1, 2))
        arrived(rows_of(far, 1, 1), sems(1, 3))

    def relay_sent(rows_of, sems):
        sent(rows_of(x, 0, 2), sems(0, 0))
        sent(rows_of(x, 0, 2), sems(0, 1))
        sent(rows_of(x, 0, 1), sems(0, 2))
        sent(rows_of(x, 0, 1), sems(0, 3))

    def gx(g, s):
        def rows_of(owner, first, count):
            part_rows = chunk_x // 2
            at = pl.ds(g * rows_g + owner * chunk_x + first * part_rows, count * part_rows)
            return shared.at[s, at]

        return rows_of, lambda side, k: (s_gx, r_gx)[side].at[g, s, k]

    def send_gx(g, s):
        first = g * rows_g + x * chunk_x
        arrived(shared.at[s, pl.ds(first, (NY - 1) * chunk_y)], r_gy.at[g, s])
        relay_start(*gx(g, s))

    def p_copy(target, slot):
        return remote(part.at[target], in_part.at[slot], s_p, r_p, {"plane": target})

    slots = ids_ref.shape[1]
    piece = -(-slots // (128 * PIECES)) * 128

    def add_part(i):
        if i == 0:
            loads[1].wait()
            loads[2].wait()
            loads[3].wait()
        at = slice(i * piece, min((i + 1) * piece, slots))
        ids = ids_ref[pl.ds(plane, 1), at]
        valid = ids >= 0
        id_h = jnp.where(valid, ids // n, -1)
        id_g = jnp.where(valid, lax.rem(ids, n), 0)
        lane = jnp.where(id_g == 0, 0, jnp.where(id_g <= n // 2, 2 * id_g - 1, 2 * (n - id_g)))
        reverse = (jnp.minimum(id_h, n - id_h) >= edge) | (id_h == edge_row)
        lane = jnp.where(reverse, n - 1 - lane, lane)
        iota = lax.broadcasted_iota(jnp.int32, (n, ids.shape[1]), 0)
        hot_h = (labels[:, 0:1] == id_h) | (labels[:, 1:2] == id_h)
        hot_g = jnp.where(iota == lane, 1.0, 0.0).astype(BF16)
        tile = coulomb[:, at].astype(F32)
        own = tile[:coul_rows]
        for k in range(1, 16 // coul_rows):
            inside = first_row - coul_tile == k * coul_rows
            own = jnp.where(inside, tile[k * coul_rows : (k + 1) * coul_rows], own)
        left = jnp.concatenate(
            [jnp.where(hot_h, own[k : k + 1], 0.0).astype(BF16) for k in range(coul_rows)], 0
        )
        flat = lax.dot_general(
            left, hot_g, (((1,), (1,)), ((), ())), preferred_element_type=F32
        )
        flat_sum[...] = flat if i == 0 else flat_sum[...] + flat

    def send_part():
        for k in range(coul_rows):
            for o in range(n_plane):
                at = slice(k * n + o * width, k * n + (o + 1) * width)
                part[o, k * width : (k + 1) * width, :] = flat_sum[at, :].astype(BF16)
        for d in range(1, n_plane):
            start(p_copy(p_peer(d), plane))
        in_part[plane] = part[plane]

    coul_x, coul_y = rows // NX, rows // (NX * NY)

    def dy_copy(target, owner):
        block = coul16.at[pl.ds(x * coul_x + owner * coul_y, coul_y)]
        return remote(block, block, s_dy, r_dy, at_band(x, zh, target))

    def send_dy():
        arrived(in_part.at[pl.ds(0, n_plane - 1)], r_p)
        summed = in_part[0].astype(F32)
        for o in range(1, n_plane):
            summed = summed + in_part[o].astype(F32)
        coul16[pl.ds(x * coul_x + y * coul_y, coul_y), :] = summed.astype(BF16)
        for d in range(1, NY):
            start(dy_copy(y_peer(d), y))

    def dx():
        def rows_of(owner, first, count):
            part_rows = coul_x // 2
            return coul16.at[pl.ds(owner * coul_x + first * part_rows, count * part_rows)]

        return rows_of, lambda side, k: (s_dx, r_dx)[side].at[k]

    def send_dx():
        arrived(coul16.at[pl.ds(x * coul_x, (NY - 1) * coul_y)], r_dy)
        relay_start(*dx())

    def wait_dense():
        relay_end(*dx())
        dense[...] = coul16[...].astype(F32)

    half = width // GROUPS
    block = per_owner * half

    def f_copy(g, s, target, slot):
        return remote(
            send_f.at[s, g, target], recv_f.at[s, g, slot],
            s_f.at[g, s], r_f.at[g, s], {"plane": target},
        )

    def forward(g, s):
        relay_end(*gx(g, s))
        both = wide[:n, :]
        first, second = slim[:n_packed, :], slim[n : n + n_packed, :]
        in_first = lax.broadcasted_iota(jnp.int32, (n_packed, n), 1) < labels[:n_packed, 2:3]
        group = 4

        def step(i, _):
            at = pl.ds(pl.multiple_of(g * rows_g + i * (group * n), group * n), group * n)
            pair = (orb[at, :] * shared[s, at, :].astype(F32)).astype(BF16)
            along = dot(pair, both).astype(BF16)
            for k in range(group):
                plane_k = along[k * n : (k + 1) * n]
                packed = jnp.where(in_first, dot(first, plane_k[:, :n]), dot(second, plane_k[:, n:]))
                grid_a[pl.ds(i * group + k, n_packed, stride=half), :] = packed
            return 0

        lax.fori_loop(0, half // group, step, 0)
        for d in range(1, n_plane):
            t = p_peer(d)
            send_f[s, g, t] = grid_a[pl.ds(pl.multiple_of(t * block, block), block), :].astype(BF16)
            start(f_copy(g, s, t, plane))
        at = pl.ds(pl.multiple_of(plane * block, block), block)
        recv_f[s, g, plane] = grid_a[at, :].astype(BF16)

    def b_copy(g, s, target, slot):
        return remote(
            send_b.at[s, g, target], recv_b.at[s, g, slot],
            s_b.at[g, s], r_b.at[g, s], {"plane": target},
        )

    def middle(s):
        for g in range(GROUPS):
            arrived(recv_f.at[s, g, pl.ds(0, n_plane - 1)], r_f.at[g, s])
        twin, cas = wide[n : 3 * n, :], slim[4 * n : 5 * n, :]
        for j in range(per_owner // 2):
            at = slice(j * 2 * half, (j + 1) * 2 * half)
            spectrum = dot(twin, recv_f[s, :, :, at, :].reshape(2 * n, n))
            back = []
            for h in range(2):
                coul = dense[pl.ds(2 * j + h, n, stride=width), :]
                scaled = (spectrum[h * n : (h + 1) * n] * coul).astype(BF16)
                back.append((dot(cas, scaled) * (1.0 / n)).reshape(n_plane, GROUPS, half, n))
            for g in range(GROUPS):
                for q in range(n_plane):
                    both = jnp.concatenate([back[0][q, g], back[1][q, g]], 0)
                    send_b[s, g, q, at, :] = both.astype(BF16)
        for g in range(GROUPS):
            for d in range(1, n_plane):
                start(b_copy(g, s, p_peer(d), plane))
            recv_b[s, g, plane] = send_b[s, g, plane]

    def inverse(g, s):
        arrived(recv_b.at[s, g, pl.ds(0, n_plane - 1)], r_b.at[g, s])
        first, second = wide[3 * n :, :n], wide[3 * n :, n:]
        both = slim[2 * n : 4 * n, :]
        in_first = lax.broadcasted_iota(jnp.int32, (n, n), 1) < labels[:, 2:3]
        grid_b[: n_packed * half, :] = recv_b[s, g].reshape(n_packed * half, n).astype(F32)
        group = 4

        def step(i, _):
            for k in range(group):
                xi = i * group + k
                packed = grid_b[pl.ds(xi, n, stride=half), :]
                from_first = dot(first, jnp.where(in_first, packed, 0.0).astype(BF16))
                from_second = dot(second, jnp.where(in_first, 0.0, packed).astype(BF16))
                inverse_y = jnp.concatenate([from_first, from_second], 1) * (1.0 / n)
                at = pl.ds(pl.multiple_of(g * rows_g + xi * n, n), n)
                potential = dot(inverse_y.astype(BF16), both) * (1.0 / n)
                term = potential * shared[s, at, :].astype(F32)
                if s == 0:
                    total[at, :] = term
                else:
                    out_ref[at, :] = (total[at, :] + term).astype(BF16)
            return 0

        lax.fori_loop(0, half // group, step, 0)

    send_x(0)
    send_x(1)
    add_part(0)
    wait_x(0)
    send_y(0, 0)
    add_part(1)
    send_z(0, 0)
    wait_x(1)
    send_y(1, 0)
    send_gy(0, 0)
    send_z(1, 0)
    for i in range(2, PIECES):
        add_part(i)
    send_part()
    send_gx(0, 0)
    send_gy(1, 0)
    send_y(0, 1)
    relay_on(*gx(0, 0))
    send_gx(1, 0)
    send_y(1, 1)
    send_z(0, 1)
    send_dy()
    loads[4].wait()
    loads[5].wait()
    forward(0, 0)
    relay_on(*gx(1, 0))
    send_gy(0, 1)
    send_z(1, 1)
    send_dx()
    forward(1, 0)
    send_gx(0, 1)
    send_gy(1, 1)
    relay_on(*dx())
    relay_on(*gx(0, 1))
    send_gx(1, 1)
    forward(0, 1)
    relay_on(*gx(1, 1))
    forward(1, 1)
    for g in range(GROUPS):
        sent(in_x.at[g, pl.ds(0, NX - 1)], s_x.at[g])
        for s in range(STEPS):
            sent(in_y.at[g, s, pl.ds(0, NY - 1)], s_y.at[g, s])
            sent(in_z.at[g, s], s_z.at[g, s])
            sent(shared.at[s, pl.ds(0, (NY - 1) * chunk_y)], s_gy.at[g, s])
            relay_sent(*gx(g, s))
    sent(in_part.at[pl.ds(0, n_plane - 1)], s_p)
    grid_b[n_packed * half :, :] = jnp.zeros(((n - n_packed) * half, n), F32)
    wait_dense()
    middle(0)
    sent(coul16.at[pl.ds(0, (NY - 1) * coul_y)], s_dy)
    relay_sent(*dx())
    middle(1)
    for g in range(GROUPS):
        for s in range(STEPS):
            sent(recv_f.at[s, g, pl.ds(0, n_plane - 1)], s_f.at[g, s])
    inverse(0, 0)
    inverse(1, 0)
    inverse(0, 1)
    inverse(1, 1)
    for g in range(GROUPS):
        for s in range(STEPS):
            sent(recv_b.at[s, g, pl.ds(0, n_plane - 1)], s_b.at[g, s])


def on_device(orbitals, coulomb, stick_lists, roots):
    _, width, n, _ = orbitals.shape
    n_plane = n // width
    rows = width * n
    rows_g = rows // GROUPS
    chunk_x, chunk_y = rows_g // NX, rows_g // (NX * NY)
    coul_block = n // (NX * NY) * width
    per_owner = packing(n, n_plane)[1]
    wide, slim, labels = tables(n, n_plane)
    hbm = pl.BlockSpec(memory_space=pl.ANY)
    vmem = pl.BlockSpec(memory_space=pltpu.VMEM)
    dma = pltpu.SemaphoreType.DMA

    def pair_of_sems(*shape):
        return [dma(shape), dma(shape)]

    gs = (GROUPS, STEPS)
    spectra = pltpu.VMEM((STEPS, GROUPS, n_plane, per_owner * width // GROUPS, n), BF16)
    out = pl.pallas_call(
        functools.partial(kernel, n, n_plane),
        out_shape=jax.ShapeDtypeStruct((rows, n), BF16),
        in_specs=[pl.BlockSpec(memory_space=pltpu.SMEM)] + [hbm] * 6,
        out_specs=vmem,
        scratch_shapes=[
            pltpu.VMEM((rows, n), F32),
            pltpu.VMEM(wide.shape, BF16),
            pltpu.VMEM(slim.shape, BF16),
            pltpu.VMEM(labels.shape, jnp.int32),
            pltpu.VMEM((16, coulomb.shape[1]), BF16),
            pltpu.VMEM(stick_lists.shape, jnp.int32),
            pltpu.VMEM((rows, n), BF16),
            pltpu.VMEM((GROUPS, NX, chunk_x, n), BF16),
            pltpu.VMEM(gs + (chunk_x, n), BF16),
            pltpu.VMEM(gs + (NY, chunk_y, n), BF16),
            pltpu.VMEM(gs + (chunk_y, n), BF16),
            pltpu.VMEM(gs + (chunk_y, n), BF16),
            pltpu.VMEM((STEPS, rows, n), BF16),
            pltpu.VMEM((n // (NX * NY) * n, n), F32),
            pltpu.VMEM((n_plane, coul_block, n), BF16),
            pltpu.VMEM((n_plane, coul_block, n), BF16),
            pltpu.VMEM((rows, n), BF16),
            pltpu.VMEM((rows, n), F32),
            pltpu.VMEM((rows_g, n), F32),
            pltpu.VMEM((rows_g, n), F32),
            spectra, spectra, spectra, spectra,
            pltpu.VMEM((rows, n), F32),
            dma((6,)),
            *pair_of_sems(GROUPS),
            *pair_of_sems(*gs),
            *pair_of_sems(*gs),
            *pair_of_sems(*gs),
            *pair_of_sems(*gs, 4),
            dma, dma, dma, dma,
            *pair_of_sems(4),
            *pair_of_sems(*gs),
            *pair_of_sems(*gs),
        ],
        compiler_params=pltpu.CompilerParams(
            collective_id=0, has_side_effects=True, vmem_limit_bytes=57 * 1024 * 1024
        ),
        name="exchange",
    )(
        roots, orbitals.reshape(rows, n),
        wide, slim, labels, coulomb, stick_lists,
    )
    return out.reshape(1, width, n, n)


def solution(mesh):
    in_specs = (P("band", "plane", None, None), P(None, "plane"), P(), P())
    out_specs = P("band", "plane", None, None)
    return jax.shard_map(
        on_device, mesh=mesh, in_specs=in_specs, out_specs=out_specs, check_vma=False
    )
```

```python
import functools
import math

import jax
import jax.numpy as jnp
import numpy as np
from jax import lax
from jax.experimental import pallas as pl
from jax.experimental.pallas import tpu as pltpu
from jax.sharding import PartitionSpec as P

NX, NZ, NY = 4, 2, 8
STICKS = 12288
GROUPS = 1
STEPS = 2
PIECES = 3
MESH = pl.DeviceIdType.MESH
F32, BF16 = jnp.float32, jnp.bfloat16


def cas_table(n):
    k = np.arange(n)
    angles = 2.0 * math.pi / n * ((k[:, None] * k[None, :]) % n)
    return np.asarray(np.cos(angles) + np.sin(angles), np.float32)


def pair_table(n, width):
    cas = cas_table(n)
    half = width // GROUPS
    table = np.zeros((2, n, GROUPS, n // width, 2, half), np.float32)
    by_x = cas.reshape(n, n // width, GROUPS, half).transpose(0, 2, 1, 3)
    for h in range(2):
        table[h, :, :, :, h, :] = by_x
    return table.reshape(2 * n, 2 * n)


def packing(n, n_plane):
    signed = np.minimum(np.arange(n), n - np.arange(n))
    squares = signed[:, None] ** 2 + signed[None, :] ** 2
    kept = (squares <= np.sort(squares.reshape(-1))[STICKS - 1]).sum(1)
    best = None
    for t in range(1, n // 2 + 1):
        for extra in ([], [n - t + 1]):
            second = [h for h in range(n) if kept[h] and (signed[h] >= t or h in extra)]
            firsts = [h for h in range(n) if kept[h] and h not in second]
            free, mate = sorted(firsts, key=lambda h: -kept[h]), {}
            for h in sorted(second, key=lambda h: -kept[h]):
                host = next((f for f in free if kept[f] + kept[h] <= n), None)
                if host is None:
                    break
                free.remove(host)
                mate[host] = h
            else:
                if best is None or len(firsts) < len(best[0]):
                    best = firsts, mate, t, extra
    firsts, mate, t, extra = best
    per_owner = -(-len(firsts) // (2 * n_plane)) * 2
    table = -np.ones((per_owner * n_plane, 3), np.int64)
    for row, h in enumerate(firsts):
        table[row] = h, mate.get(h, -1), kept[h]
    return table, per_owner, t, (extra or [-1])[0]


def tables(n, n_plane):
    width = n // n_plane
    cas = cas_table(n)
    rows, per_owner, _, _ = packing(n, n_plane)
    order = sorted(range(n), key=lambda g: (min(g, n - g), g > n // 2))
    both = np.concatenate([cas[:, order], cas[:, order[::-1]]], 1)
    first, second = np.zeros((n, n), np.float32), np.zeros((n, n), np.float32)
    for row, (h, other, _) in enumerate(rows):
        if h >= 0:
            first[row] = cas[h]
        if other >= 0:
            second[row] = cas[other]
    wide = np.concatenate([both, pair_table(n, width), np.concatenate([first.T, second.T], 1)], 0)
    slim = np.concatenate([first, second, both.T, cas], 0)
    labels = np.full((n, 128), -7, np.int32)
    for row, (h, other, length) in enumerate(rows):
        place = row // per_owner * width + row % per_owner
        labels[place, 0] = h if h >= 0 else -7
        labels[place, 1] = other if other >= 0 else -7
    labels[:, 2] = n
    labels[: len(rows), 2] = np.where(rows[:, 2] < 0, n, rows[:, 2])
    return jnp.asarray(wide).astype(BF16), jnp.asarray(slim).astype(BF16), jnp.asarray(labels)


def dot(a, b):
    return jnp.dot(a, b, preferred_element_type=F32)


def pick(index, values):
    out = values[0]
    for k in range(1, len(values)):
        out = jnp.where(index == k, values[k], out)
    return out


def remote(src, dst, send_sem, recv_sem, device):
    return pltpu.make_async_remote_copy(
        src_ref=src, dst_ref=dst, send_sem=send_sem, recv_sem=recv_sem,
        device_id=device, device_id_type=MESH,
    )


def kernel(
    n, n_plane,
    roots_ref, orb_hbm, wide_hbm, slim_hbm, labels_hbm, coulomb_hbm, ids_hbm, out_ref,
    orb, wide, slim, labels, coulomb, ids_ref,
    orb16, in_x, sel, in_y, cand, in_z, shared,
    flat_sum, part, in_part, coul16, dense, grid_a, grid_b, send_f, recv_f, send_b, recv_b, total,
    s_in, s_x, r_x, s_y, r_y, s_z, r_z, s_gy, r_gy, s_gx, r_gx,
    s_p, r_p, s_dy, r_dy, s_dx, r_dx, s_f, r_f, s_b, r_b,
):
    width = n // n_plane
    rows = width * n
    rows_g = rows // GROUPS
    _, per_owner, edge, edge_row = packing(n, n_plane)
    n_packed = per_owner * n_plane
    chunk_x, chunk_y = rows_g // NX, rows_g // (NX * NY)
    band, plane = lax.axis_index("band"), lax.axis_index("plane")
    y = lax.rem(band, NY)
    zh = lax.rem(band // NY, NZ)
    x = band // (NY * NZ)

    def at_band(bx, bz, by):
        return {"band": (bx * NZ + bz) * NY + by}

    def x_peer(d):
        return lax.rem(x + d, NX)

    def y_peer(d):
        return lax.rem(y + d, NY)

    def p_peer(d):
        return lax.rem(plane + d, n_plane)

    barrier = pltpu.get_barrier_semaphore()
    peers = [at_band(x_peer(d), zh, y) for d in range(1, NX)]
    peers += [at_band(x, zh, y_peer(d)) for d in range(1, NY)]
    peers += [at_band(x, lax.rem(zh + d, NZ), y) for d in range(1, NZ)]
    peers += [{"plane": p_peer(d)} for d in range(1, n_plane)]
    for peer in peers:
        pl.semaphore_signal(barrier, inc=1, device_id=peer, device_id_type=MESH)

    coul_rows = n // (NX * NY)
    first_row = (x * NY + y) * coul_rows
    coul_tile = pl.multiple_of(first_row // 16 * 16, 16)
    loads = [
        pltpu.make_async_copy(orb_hbm, orb, s_in.at[0]),
        pltpu.make_async_copy(coulomb_hbm.at[pl.ds(coul_tile, 16)], coulomb, s_in.at[1]),
        pltpu.make_async_copy(ids_hbm, ids_ref, s_in.at[2]),
        pltpu.make_async_copy(labels_hbm, labels, s_in.at[3]),
        pltpu.make_async_copy(slim_hbm, slim, s_in.at[4]),
        pltpu.make_async_copy(wide_hbm, wide, s_in.at[5]),
    ]
    for load in loads:
        load.start()
    loads[0].wait()
    orb16[...] = orb[...].astype(BF16)
    pl.semaphore_wait(barrier, len(peers))

    def start(copy):
        copy.start()

    def arrived(region, sem):
        remote(region, region, sem, sem, {"plane": p_peer(1)}).wait_recv()

    def sent(region, sem):
        remote(region, region, sem, sem, {"plane": p_peer(1)}).wait_send()

    def x_copy(g, target, slot):
        return remote(
            orb16.at[pl.ds(g * rows_g + target * chunk_x, chunk_x)], in_x.at[g, slot],
            s_x.at[g], r_x.at[g], at_band(target, zh, y),
        )

    def send_x(g):
        for d in range(1, NX):
            start(x_copy(g, x_peer(d), x))
        in_x[g, x] = orb16[pl.ds(g * rows_g + x * chunk_x, chunk_x), :]

    def wait_x(g):
        arrived(in_x.at[g, pl.ds(0, NX - 1)], r_x.at[g])

    root = [roots_ref[s] for s in range(STEPS)]
    root_y = [lax.rem(r, NY) for r in root]
    root_z = [lax.rem(r // NY, NZ) for r in root]
    root_x = [r // (NY * NZ) for r in root]

    def y_copy(g, s, target, slot):
        return remote(
            sel.at[g, s, pl.ds(target * chunk_y, chunk_y)], in_y.at[g, s, slot],
            s_y.at[g, s], r_y.at[g, s], at_band(x, zh, target),
        )

    def send_y(g, s):
        sel[g, s] = pick(root_x[s], [in_x[g, k] for k in range(NX)])
        for d in range(1, NY):
            start(y_copy(g, s, y_peer(d), y))
        in_y[g, s, y] = sel[g, s, pl.ds(y * chunk_y, chunk_y), :]

    def z_copy(g, s):
        return remote(
            cand.at[g, s], in_z.at[g, s], s_z.at[g, s], r_z.at[g, s],
            at_band(x, lax.rem(zh + 1, NZ), y),
        )

    def send_z(g, s):
        arrived(in_y.at[g, s, pl.ds(0, NY - 1)], r_y.at[g, s])
        cand[g, s] = pick(root_y[s], [in_y[g, s, k] for k in range(NY)])
        start(z_copy(g, s))

    def gy_copy(g, s, target, owner):
        block = shared.at[s, pl.ds(g * rows_g + x * chunk_x + owner * chunk_y, chunk_y)]
        return remote(block, block, s_gy.at[g, s], r_gy.at[g, s], at_band(x, zh, target))

    def send_gy(g, s):
        z_copy(g, s).wait_recv()
        at = pl.ds(g * rows_g + x * chunk_x + y * chunk_y, chunk_y)
        shared[s, at, :] = jnp.where(root_z[s] == zh, cand[g, s], in_z[g, s])
        for d in range(1, NY):
            start(gy_copy(g, s, y_peer(d), y))

    left, right, far = x_peer(NX - 1), x_peer(1), x_peer(2)

    def relay_start(rows_of, sems):
        own = rows_of(x, 0, 2)
        start(remote(own, own, sems(0, 0), sems(1, 0), at_band(right, zh, y)))
        start(remote(own, own, sems(0, 1), sems(1, 1), at_band(left, zh, y)))

    def relay_on(rows_of, sems):
        arrived(rows_of(left, 0, 2), sems(1, 0))
        passed = rows_of(left, 0, 1)
        start(remote(passed, passed, sems(0, 2), sems(1, 2), at_band(right, zh, y)))
        arrived(rows_of(right, 0, 2), sems(1, 1))
        passed = rows_of(right, 1, 1)
        start(remote(passed, passed, sems(0, 3), sems(1, 3), at_band(left, zh, y)))

    def relay_end(rows_of, sems):
        arrived(rows_of(far, 0, 1), sems(1, 2))
        arrived(rows_of(far, 1, 1), sems(1, 3))

    def relay_sent(rows_of, sems):
        sent(rows_of(x, 0, 2), sems(0, 0))
        sent(rows_of(x, 0, 2), sems(0, 1))
        sent(rows_of(x, 0, 1), sems(0, 2))
        sent(rows_of(x, 0, 1), sems(0, 3))

    def gx(g, s):
        def rows_of(owner, first, count):
            part_rows = chunk_x // 2
            at = pl.ds(g * rows_g + owner * chunk_x + first * part_rows, count * part_rows)
            return shared.at[s, at]

        return rows_of, lambda side, k: (s_gx, r_gx)[side].at[g, s, k]

    def send_gx(g, s):
        first = g * rows_g + x * chunk_x
        arrived(shared.at[s, pl.ds(first, (NY - 1) * chunk_y)], r_gy.at[g, s])
        relay_start(*gx(g, s))

    def p_copy(target, slot):
        return remote(part.at[target], in_part.at[slot], s_p, r_p, {"plane": target})

    slots = ids_ref.shape[1]
    piece = -(-slots // (128 * PIECES)) * 128

    def add_part(i):
        if i == 0:
            loads[1].wait()
            loads[2].wait()
            loads[3].wait()
        at = slice(i * piece, min((i + 1) * piece, slots))
        ids = ids_ref[pl.ds(plane, 1), at]
        valid = ids >= 0
        id_h = jnp.where(valid, ids // n, -1)
        id_g = jnp.where(valid, lax.rem(ids, n), 0)
        lane = jnp.where(id_g == 0, 0, jnp.where(id_g <= n // 2, 2 * id_g - 1, 2 * (n - id_g)))
        reverse = (jnp.minimum(id_h, n - id_h) >= edge) | (id_h == edge_row)
        lane = jnp.where(reverse, n - 1 - lane, lane)
        iota = lax.broadcasted_iota(jnp.int32, (n, ids.shape[1]), 0)
        hot_h = (labels[:, 0:1] == id_h) | (labels[:, 1:2] == id_h)
        hot_g = jnp.where(iota == lane, 1.0, 0.0).astype(BF16)
        tile = coulomb[:, at].astype(F32)
        own = tile[:coul_rows]
        for k in range(1, 16 // coul_rows):
            inside = first_row - coul_tile == k * coul_rows
            own = jnp.where(inside, tile[k * coul_rows : (k + 1) * coul_rows], own)
        left = jnp.concatenate(
            [jnp.where(hot_h, own[k : k + 1], 0.0).astype(BF16) for k in range(coul_rows)], 0
        )
        flat = lax.dot_general(
            left, hot_g, (((1,), (1,)), ((), ())), preferred_element_type=F32
        )
        flat_sum[...] = flat if i == 0 else flat_sum[...] + flat

    def send_part():
        for k in range(coul_rows):
            for o in range(n_plane):
                at = slice(k * n + o * width, k * n + (o + 1) * width)
                part[o, k * width : (k + 1) * width, :] = flat_sum[at, :].astype(BF16)
        for d in range(1, n_plane):
            start(p_copy(p_peer(d), plane))
        in_part[plane] = part[plane]

    coul_x, coul_y = rows // NX, rows // (NX * NY)

    def dy_copy(target, owner):
        block = coul16.at[pl.ds(x * coul_x + owner * coul_y, coul_y)]
        return remote(block, block, s_dy, r_dy, at_band(x, zh, target))

    def send_dy():
        arrived(in_part.at[pl.ds(0, n_plane - 1)], r_p)
        summed = in_part[0].astype(F32)
        for o in range(1, n_plane):
            summed = summed + in_part[o].astype(F32)
        coul16[pl.ds(x * coul_x + y * coul_y, coul_y), :] = summed.astype(BF16)
        for d in range(1, NY):
            start(dy_copy(y_peer(d), y))

    def dx():
        def rows_of(owner, first, count):
            part_rows = coul_x // 2
            return coul16.at[pl.ds(owner * coul_x + first * part_rows, count * part_rows)]

        return rows_of, lambda side, k: (s_dx, r_dx)[side].at[k]

    def send_dx():
        arrived(coul16.at[pl.ds(x * coul_x, (NY - 1) * coul_y)], r_dy)
        relay_start(*dx())

    def wait_dense():
        relay_end(*dx())
        dense[...] = coul16[...].astype(F32)

    half = width // GROUPS
    block = per_owner * half

    def f_copy(g, s, target, slot):
        return remote(
            send_f.at[s, g, target], recv_f.at[s, g, slot],
            s_f.at[g, s], r_f.at[g, s], {"plane": target},
        )

    def forward(g, s):
        relay_end(*gx(g, s))
        both = wide[:n, :]
        first, second = slim[:n_packed, :], slim[n : n + n_packed, :]
        in_first = lax.broadcasted_iota(jnp.int32, (n_packed, n), 1) < labels[:n_packed, 2:3]
        group = 4

        def step(i, _):
            at = pl.ds(pl.multiple_of(g * rows_g + i * (group * n), group * n), group * n)
            pair = (orb[at, :] * shared[s, at, :].astype(F32)).astype(BF16)
            along = dot(pair, both).astype(BF16)
            for k in range(group):
                plane_k = along[k * n : (k + 1) * n]
                packed = jnp.where(in_first, dot(first, plane_k[:, :n]), dot(second, plane_k[:, n:]))
                grid_a[pl.ds(i * group + k, n_packed, stride=half), :] = packed
            return 0

        lax.fori_loop(0, half // group, step, 0)
        for d in range(1, n_plane):
            t = p_peer(d)
            send_f[s, g, t] = grid_a[pl.ds(pl.multiple_of(t * block, block), block), :].astype(BF16)
            start(f_copy(g, s, t, plane))
        at = pl.ds(pl.multiple_of(plane * block, block), block)
        recv_f[s, g, plane] = grid_a[at, :].astype(BF16)

    def b_copy(g, s, target, slot):
        return remote(
            send_b.at[s, g, target], recv_b.at[s, g, slot],
            s_b.at[g, s], r_b.at[g, s], {"plane": target},
        )

    def middle(s):
        for g in range(GROUPS):
            arrived(recv_f.at[s, g, pl.ds(0, n_plane - 1)], r_f.at[g, s])
        twin, cas = wide[n : 3 * n, :], slim[4 * n : 5 * n, :]
        for j in range(per_owner // 2):
            at = slice(j * 2 * half, (j + 1) * 2 * half)
            spectrum = dot(twin, recv_f[s, :, :, at, :].reshape(2 * n, n))
            back = []
            for h in range(2):
                coul = dense[pl.ds(2 * j + h, n, stride=width), :]
                scaled = (spectrum[h * n : (h + 1) * n] * coul).astype(BF16)
                back.append((dot(cas, scaled) * (1.0 / n)).reshape(n_plane, GROUPS, half, n))
            for g in range(GROUPS):
                for q in range(n_plane):
                    both = jnp.concatenate([back[0][q, g], back[1][q, g]], 0)
                    send_b[s, g, q, at, :] = both.astype(BF16)
        for g in range(GROUPS):
            for d in range(1, n_plane):
                start(b_copy(g, s, p_peer(d), plane))
            recv_b[s, g, plane] = send_b[s, g, plane]

    def inverse(g, s):
        arrived(recv_b.at[s, g, pl.ds(0, n_plane - 1)], r_b.at[g, s])
        first, second = wide[3 * n :, :n], wide[3 * n :, n:]
        both = slim[2 * n : 4 * n, :]
        in_first = lax.broadcasted_iota(jnp.int32, (n, n), 1) < labels[:, 2:3]
        grid_b[: n_packed * half, :] = recv_b[s, g].reshape(n_packed * half, n).astype(F32)
        group = 4

        def step(i, _):
            for k in range(group):
                xi = i * group + k
                packed = grid_b[pl.ds(xi, n, stride=half), :]
                from_first = dot(first, jnp.where(in_first, packed, 0.0).astype(BF16))
                from_second = dot(second, jnp.where(in_first, 0.0, packed).astype(BF16))
                inverse_y = jnp.concatenate([from_first, from_second], 1) * (1.0 / n)
                at = pl.ds(pl.multiple_of(g * rows_g + xi * n, n), n)
                potential = dot(inverse_y.astype(BF16), both) * (1.0 / n)
                term = potential * shared[s, at, :].astype(F32)
                if s == 0:
                    total[at, :] = term
                else:
                    out_ref[at, :] = (total[at, :] + term).astype(BF16)
            return 0

        lax.fori_loop(0, half // group, step, 0)

    send_x(0)
    add_part(0)
    add_part(1)
    wait_x(0)
    send_y(0, 0)
    send_y(0, 1)
    for i in range(2, PIECES):
        add_part(i)
    send_part()
    send_z(0, 0)
    send_z(0, 1)
    send_gy(0, 0)
    send_gy(0, 1)
    send_gx(0, 0)
    send_dy()
    relay_on(*gx(0, 0))
    send_gx(0, 1)
    send_dx()
    loads[4].wait()
    loads[5].wait()
    forward(0, 0)
    relay_on(*gx(0, 1))
    relay_on(*dx())
    forward(0, 1)
    for g in range(GROUPS):
        sent(in_x.at[g, pl.ds(0, NX - 1)], s_x.at[g])
        for s in range(STEPS):
            sent(in_y.at[g, s, pl.ds(0, NY - 1)], s_y.at[g, s])
            sent(in_z.at[g, s], s_z.at[g, s])
            sent(shared.at[s, pl.ds(0, (NY - 1) * chunk_y)], s_gy.at[g, s])
            relay_sent(*gx(g, s))
    sent(in_part.at[pl.ds(0, n_plane - 1)], s_p)
    grid_b[n_packed * half :, :] = jnp.zeros(((n - n_packed) * half, n), F32)
    wait_dense()
    middle(0)
    sent(coul16.at[pl.ds(0, (NY - 1) * coul_y)], s_dy)
    relay_sent(*dx())
    middle(1)
    for g in range(GROUPS):
        for s in range(STEPS):
            sent(recv_f.at[s, g, pl.ds(0, n_plane - 1)], s_f.at[g, s])
    for s in range(STEPS):
        for g in range(GROUPS):
            inverse(g, s)
    for g in range(GROUPS):
        for s in range(STEPS):
            sent(recv_b.at[s, g, pl.ds(0, n_plane - 1)], s_b.at[g, s])


def on_device(orbitals, coulomb, stick_lists, roots):
    _, width, n, _ = orbitals.shape
    n_plane = n // width
    rows = width * n
    rows_g = rows // GROUPS
    chunk_x, chunk_y = rows_g // NX, rows_g // (NX * NY)
    coul_block = n // (NX * NY) * width
    per_owner = packing(n, n_plane)[1]
    wide, slim, labels = tables(n, n_plane)
    hbm = pl.BlockSpec(memory_space=pl.ANY)
    vmem = pl.BlockSpec(memory_space=pltpu.VMEM)
    dma = pltpu.SemaphoreType.DMA

    def pair_of_sems(*shape):
        return [dma(shape), dma(shape)]

    gs = (GROUPS, STEPS)
    spectra = pltpu.VMEM((STEPS, GROUPS, n_plane, per_owner * width // GROUPS, n), BF16)
    out = pl.pallas_call(
        functools.partial(kernel, n, n_plane),
        out_shape=jax.ShapeDtypeStruct((rows, n), BF16),
        in_specs=[pl.BlockSpec(memory_space=pltpu.SMEM)] + [hbm] * 6,
        out_specs=vmem,
        scratch_shapes=[
            pltpu.VMEM((rows, n), F32),
            pltpu.VMEM(wide.shape, BF16),
            pltpu.VMEM(slim.shape, BF16),
            pltpu.VMEM(labels.shape, jnp.int32),
            pltpu.VMEM((16, coulomb.shape[1]), BF16),
            pltpu.VMEM(stick_lists.shape, jnp.int32),
            pltpu.VMEM((rows, n), BF16),
            pltpu.VMEM((GROUPS, NX, chunk_x, n), BF16),
            pltpu.VMEM(gs + (chunk_x, n), BF16),
            pltpu.VMEM(gs + (NY, chunk_y, n), BF16),
            pltpu.VMEM(gs + (chunk_y, n), BF16),
            pltpu.VMEM(gs + (chunk_y, n), BF16),
            pltpu.VMEM((STEPS, rows, n), BF16),
            pltpu.VMEM((n // (NX * NY) * n, n), F32),
            pltpu.VMEM((n_plane, coul_block, n), BF16),
            pltpu.VMEM((n_plane, coul_block, n), BF16),
            pltpu.VMEM((rows, n), BF16),
            pltpu.VMEM((rows, n), F32),
            pltpu.VMEM((rows_g, n), F32),
            pltpu.VMEM((rows_g, n), F32),
            spectra, spectra, spectra, spectra,
            pltpu.VMEM((rows, n), F32),
            dma((6,)),
            *pair_of_sems(GROUPS),
            *pair_of_sems(*gs),
            *pair_of_sems(*gs),
            *pair_of_sems(*gs),
            *pair_of_sems(*gs, 4),
            dma, dma, dma, dma,
            *pair_of_sems(4),
            *pair_of_sems(*gs),
            *pair_of_sems(*gs),
        ],
        compiler_params=pltpu.CompilerParams(
            collective_id=0, has_side_effects=True, vmem_limit_bytes=57 * 1024 * 1024
        ),
        name="exchange",
    )(
        roots, orbitals.reshape(rows, n),
        wide, slim, labels, coulomb, stick_lists,
    )
    return out.reshape(1, width, n, n)


def solution(mesh):
    in_specs = (P("band", "plane", None, None), P(None, "plane"), P(), P())
    out_specs = P("band", "plane", None, None)
    return jax.shard_map(
        on_device, mesh=mesh, in_specs=in_specs, out_specs=out_specs, check_vma=False
    )
```

```python
import functools
import math

import jax
import jax.numpy as jnp
import numpy as np
from jax import lax
from jax.experimental import pallas as pl
from jax.experimental.pallas import tpu as pltpu
from jax.sharding import PartitionSpec as P

NX, NZ, NY = 4, 2, 8
STICKS = 12288
GROUPS = 2
STEPS = 2
PIECES = 3
MESH = pl.DeviceIdType.MESH
F32, BF16 = jnp.float32, jnp.bfloat16


def cas_table(n):
    k = np.arange(n)
    angles = 2.0 * math.pi / n * ((k[:, None] * k[None, :]) % n)
    return np.asarray(np.cos(angles) + np.sin(angles), np.float32)


def pair_table(n, width):
    cas = cas_table(n)
    half = width // GROUPS
    table = np.zeros((2, n, GROUPS, n // width, 2, half), np.float32)
    by_x = cas.reshape(n, n // width, GROUPS, half).transpose(0, 2, 1, 3)
    for h in range(2):
        table[h, :, :, :, h, :] = by_x
    return table.reshape(2 * n, 2 * n)


def packing(n, n_plane):
    signed = np.minimum(np.arange(n), n - np.arange(n))
    squares = signed[:, None] ** 2 + signed[None, :] ** 2
    kept = (squares <= np.sort(squares.reshape(-1))[STICKS - 1]).sum(1)
    best = None
    for t in range(1, n // 2 + 1):
        for extra in ([], [n - t + 1]):
            second = [h for h in range(n) if kept[h] and (signed[h] >= t or h in extra)]
            firsts = [h for h in range(n) if kept[h] and h not in second]
            free, mate = sorted(firsts, key=lambda h: -kept[h]), {}
            for h in sorted(second, key=lambda h: -kept[h]):
                host = next((f for f in free if kept[f] + kept[h] <= n), None)
                if host is None:
                    break
                free.remove(host)
                mate[host] = h
            else:
                if best is None or len(firsts) < len(best[0]):
                    best = firsts, mate, t, extra
    firsts, mate, t, extra = best
    per_owner = -(-len(firsts) // (2 * n_plane)) * 2
    table = -np.ones((per_owner * n_plane, 3), np.int64)
    for row, h in enumerate(firsts):
        table[row] = h, mate.get(h, -1), kept[h]
    return table, per_owner, t, (extra or [-1])[0]


def tables(n, n_plane):
    width = n // n_plane
    cas = cas_table(n)
    rows, per_owner, _, _ = packing(n, n_plane)
    order = sorted(range(n), key=lambda g: (min(g, n - g), g > n // 2))
    both = np.concatenate([cas[:, order], cas[:, order[::-1]]], 1)
    first, second = np.zeros((n, n), np.float32), np.zeros((n, n), np.float32)
    for row, (h, other, _) in enumerate(rows):
        if h >= 0:
            first[row] = cas[h]
        if other >= 0:
            second[row] = cas[other]
    wide = np.concatenate([both, pair_table(n, width), np.concatenate([first.T, second.T], 1)], 0)
    slim = np.concatenate([first, second, both.T, cas], 0)
    labels = np.full((n, 128), -7, np.int32)
    for row, (h, other, length) in enumerate(rows):
        place = row // per_owner * width + row % per_owner
        labels[place, 0] = h if h >= 0 else -7
        labels[place, 1] = other if other >= 0 else -7
    labels[:, 2] = n
    labels[: len(rows), 2] = np.where(rows[:, 2] < 0, n, rows[:, 2])
    return jnp.asarray(wide).astype(BF16), jnp.asarray(slim).astype(BF16), jnp.asarray(labels)


def dot(a, b):
    return jnp.dot(a, b, preferred_element_type=F32)


def pick(index, values):
    out = values[0]
    for k in range(1, len(values)):
        out = jnp.where(index == k, values[k], out)
    return out


def remote(src, dst, send_sem, recv_sem, device):
    return pltpu.make_async_remote_copy(
        src_ref=src, dst_ref=dst, send_sem=send_sem, recv_sem=recv_sem,
        device_id=device, device_id_type=MESH,
    )


def kernel(
    n, n_plane,
    roots_ref, orb_hbm, wide_hbm, slim_hbm, labels_hbm, coulomb_hbm, ids_hbm, out_ref,
    orb, wide, slim, labels, coulomb, ids_ref,
    orb16, in_x, sel, in_y, cand, in_z, shared,
    flat_sum, part, in_part, coul16, dense, grid_a, grid_b, send_f, recv_f, send_b, recv_b, total,
    s_in, s_x, r_x, s_y, r_y, s_z, r_z, s_gy, r_gy, s_gx, r_gx,
    s_p, r_p, s_dy, r_dy, s_dx, r_dx, s_f, r_f, s_b, r_b,
):
    width = n // n_plane
    rows = width * n
    rows_g = rows // GROUPS
    _, per_owner, edge, edge_row = packing(n, n_plane)
    n_packed = per_owner * n_plane
    chunk_x, chunk_y = rows_g // NX, rows_g // (NX * NY)
    band, plane = lax.axis_index("band"), lax.axis_index("plane")
    y = lax.rem(band, NY)
    zh = lax.rem(band // NY, NZ)
    x = band // (NY * NZ)

    def at_band(bx, bz, by):
        return {"band": (bx * NZ + bz) * NY + by}

    def x_peer(d):
        return lax.rem(x + d, NX)

    def y_peer(d):
        return lax.rem(y + d, NY)

    def p_peer(d):
        return lax.rem(plane + d, n_plane)

    barrier = pltpu.get_barrier_semaphore()
    peers = [at_band(x_peer(d), zh, y) for d in range(1, NX)]
    peers += [at_band(x, zh, y_peer(d)) for d in range(1, NY)]
    peers += [at_band(x, lax.rem(zh + d, NZ), y) for d in range(1, NZ)]
    peers += [{"plane": p_peer(d)} for d in range(1, n_plane)]
    for peer in peers:
        pl.semaphore_signal(barrier, inc=1, device_id=peer, device_id_type=MESH)

    coul_rows = n // (NX * NY)
    first_row = (x * NY + y) * coul_rows
    coul_tile = pl.multiple_of(first_row // 16 * 16, 16)
    loads = [
        pltpu.make_async_copy(orb_hbm, orb, s_in.at[0]),
        pltpu.make_async_copy(coulomb_hbm.at[pl.ds(coul_tile, 16)], coulomb, s_in.at[1]),
        pltpu.make_async_copy(ids_hbm, ids_ref, s_in.at[2]),
        pltpu.make_async_copy(labels_hbm, labels, s_in.at[3]),
        pltpu.make_async_copy(slim_hbm, slim, s_in.at[4]),
        pltpu.make_async_copy(wide_hbm, wide, s_in.at[5]),
    ]
    for load in loads:
        load.start()
    loads[0].wait()
    orb16[...] = orb[...].astype(BF16)
    pl.semaphore_wait(barrier, len(peers))

    def start(copy):
        copy.start()

    def arrived(region, sem):
        remote(region, region, sem, sem, {"plane": p_peer(1)}).wait_recv()

    def sent(region, sem):
        remote(region, region, sem, sem, {"plane": p_peer(1)}).wait_send()

    def x_copy(g, target, slot):
        return remote(
            orb16.at[pl.ds(g * rows_g + target * chunk_x, chunk_x)], in_x.at[g, slot],
            s_x.at[g], r_x.at[g], at_band(target, zh, y),
        )

    def send_x(g):
        for d in range(1, NX):
            start(x_copy(g, x_peer(d), x))
        in_x[g, x] = orb16[pl.ds(g * rows_g + x * chunk_x, chunk_x), :]

    def wait_x(g):
        arrived(in_x.at[g, pl.ds(0, NX - 1)], r_x.at[g])

    root = [roots_ref[s] for s in range(STEPS)]
    root_y = [lax.rem(r, NY) for r in root]
    root_z = [lax.rem(r // NY, NZ) for r in root]
    root_x = [r // (NY * NZ) for r in root]

    def y_copy(g, target, slot):
        return remote(
            sel.at[g, :, pl.ds(target * chunk_y, chunk_y)], in_y.at[g, slot],
            s_y.at[g], r_y.at[g], at_band(x, zh, target),
        )

    def send_y(g):
        for s in range(STEPS):
            sel[g, s] = pick(root_x[s], [in_x[g, k] for k in range(NX)])
        for d in range(1, NY):
            start(y_copy(g, y_peer(d), y))
        in_y[g, y] = sel[g, :, pl.ds(y * chunk_y, chunk_y), :]

    def z_copy(g):
        return remote(
            cand.at[g], in_z.at[g], s_z.at[g], r_z.at[g], at_band(x, lax.rem(zh + 1, NZ), y)
        )

    def send_z(g):
        arrived(in_y.at[g, pl.ds(0, NY - 1)], r_y.at[g])
        for s in range(STEPS):
            cand[g, s] = pick(root_y[s], [in_y[g, k, s] for k in range(NY)])
        start(z_copy(g))

    def gy_copy(g, target, owner):
        block = shared.at[:, pl.ds(g * rows_g + x * chunk_x + owner * chunk_y, chunk_y)]
        return remote(block, block, s_gy.at[g], r_gy.at[g], at_band(x, zh, target))

    def send_gy(g):
        z_copy(g).wait_recv()
        at = pl.ds(g * rows_g + x * chunk_x + y * chunk_y, chunk_y)
        for s in range(STEPS):
            shared[s, at, :] = jnp.where(root_z[s] == zh, cand[g, s], in_z[g, s])
        for d in range(1, NY):
            start(gy_copy(g, y_peer(d), y))

    def wait_gy(g):
        first = g * rows_g + x * chunk_x
        arrived(shared.at[:, pl.ds(first, (NY - 1) * chunk_y)], r_gy.at[g])

    def gx_copy(g, s, target, owner):
        block = shared.at[s, pl.ds(g * rows_g + owner * chunk_x, chunk_x)]
        return remote(block, block, s_gx.at[g, s], r_gx.at[g, s], at_band(target, zh, y))

    def send_gx(g, s):
        for d in range(1, NX):
            start(gx_copy(g, s, x_peer(d), x))

    def p_copy(target, slot):
        return remote(part.at[target], in_part.at[slot], s_p, r_p, {"plane": target})

    slots = ids_ref.shape[1]
    piece = -(-slots // (128 * PIECES)) * 128

    def add_part(i):
        if i == 0:
            loads[1].wait()
            loads[2].wait()
            loads[3].wait()
        at = slice(i * piece, min((i + 1) * piece, slots))
        ids = ids_ref[pl.ds(plane, 1), at]
        valid = ids >= 0
        id_h = jnp.where(valid, ids // n, -1)
        id_g = jnp.where(valid, lax.rem(ids, n), 0)
        lane = jnp.where(id_g == 0, 0, jnp.where(id_g <= n // 2, 2 * id_g - 1, 2 * (n - id_g)))
        reverse = (jnp.minimum(id_h, n - id_h) >= edge) | (id_h == edge_row)
        lane = jnp.where(reverse, n - 1 - lane, lane)
        iota = lax.broadcasted_iota(jnp.int32, (n, ids.shape[1]), 0)
        hot_h = (labels[:, 0:1] == id_h) | (labels[:, 1:2] == id_h)
        hot_g = jnp.where(iota == lane, 1.0, 0.0).astype(BF16)
        tile = coulomb[:, at].astype(F32)
        own = tile[:coul_rows]
        for k in range(1, 16 // coul_rows):
            inside = first_row - coul_tile == k * coul_rows
            own = jnp.where(inside, tile[k * coul_rows : (k + 1) * coul_rows], own)
        left = jnp.concatenate(
            [jnp.where(hot_h, own[k : k + 1], 0.0).astype(BF16) for k in range(coul_rows)], 0
        )
        flat = lax.dot_general(
            left, hot_g, (((1,), (1,)), ((), ())), preferred_element_type=F32
        )
        flat_sum[...] = flat if i == 0 else flat_sum[...] + flat

    def send_part():
        for k in range(coul_rows):
            for o in range(n_plane):
                at = slice(k * n + o * width, k * n + (o + 1) * width)
                part[o, k * width : (k + 1) * width, :] = flat_sum[at, :].astype(BF16)
        for d in range(1, n_plane):
            start(p_copy(p_peer(d), plane))
        in_part[plane] = part[plane]

    coul_x, coul_y = rows // NX, rows // (NX * NY)

    def dy_copy(target, owner):
        block = coul16.at[pl.ds(x * coul_x + owner * coul_y, coul_y)]
        return remote(block, block, s_dy, r_dy, at_band(x, zh, target))

    def send_dy():
        arrived(in_part.at[pl.ds(0, n_plane - 1)], r_p)
        summed = in_part[0].astype(F32)
        for o in range(1, n_plane):
            summed = summed + in_part[o].astype(F32)
        coul16[pl.ds(x * coul_x + y * coul_y, coul_y), :] = summed.astype(BF16)
        for d in range(1, NY):
            start(dy_copy(y_peer(d), y))

    def dx_copy(target, owner):
        block = coul16.at[pl.ds(owner * coul_x, coul_x)]
        return remote(block, block, s_dx, r_dx, at_band(target, zh, y))

    def send_dx():
        arrived(coul16.at[pl.ds(x * coul_x, (NY - 1) * coul_y)], r_dy)
        for d in range(1, NX):
            start(dx_copy(x_peer(d), x))

    def wait_dense():
        arrived(coul16.at[pl.ds(0, (NX - 1) * coul_x)], r_dx)
        dense[...] = coul16[...].astype(F32)

    half = width // GROUPS
    block = per_owner * half

    def f_copy(g, s, target, slot):
        return remote(
            send_f.at[s, g, target], recv_f.at[s, g, slot],
            s_f.at[g, s], r_f.at[g, s], {"plane": target},
        )

    def forward(g, s):
        arrived(shared.at[s, pl.ds(g * rows_g, (NX - 1) * chunk_x)], r_gx.at[g, s])
        both = wide[:n, :]
        first, second = slim[:n_packed, :], slim[n : n + n_packed, :]
        in_first = lax.broadcasted_iota(jnp.int32, (n_packed, n), 1) < labels[:n_packed, 2:3]
        group = 4

        def step(i, _):
            at = pl.ds(pl.multiple_of(g * rows_g + i * (group * n), group * n), group * n)
            pair = (orb[at, :] * shared[s, at, :].astype(F32)).astype(BF16)
            along = dot(pair, both).astype(BF16)
            for k in range(group):
                plane_k = along[k * n : (k + 1) * n]
                packed = jnp.where(in_first, dot(first, plane_k[:, :n]), dot(second, plane_k[:, n:]))
                grid_a[pl.ds(i * group + k, n_packed, stride=half), :] = packed
            return 0

        lax.fori_loop(0, half // group, step, 0)
        for d in range(1, n_plane):
            t = p_peer(d)
            send_f[s, g, t] = grid_a[pl.ds(pl.multiple_of(t * block, block), block), :].astype(BF16)
            start(f_copy(g, s, t, plane))
        at = pl.ds(pl.multiple_of(plane * block, block), block)
        recv_f[s, g, plane] = grid_a[at, :].astype(BF16)

    def b_copy(g, s, target, slot):
        return remote(
            send_b.at[s, g, target], recv_b.at[s, g, slot],
            s_b.at[g, s], r_b.at[g, s], {"plane": target},
        )

    def middle(s):
        for g in range(GROUPS):
            arrived(recv_f.at[s, g, pl.ds(0, n_plane - 1)], r_f.at[g, s])
        twin, cas = wide[n : 3 * n, :], slim[4 * n : 5 * n, :]
        for j in range(per_owner // 2):
            at = slice(j * 2 * half, (j + 1) * 2 * half)
            spectrum = dot(twin, recv_f[s, :, :, at, :].reshape(2 * n, n))
            back = []
            for h in range(2):
                coul = dense[pl.ds(2 * j + h, n, stride=width), :]
                scaled = (spectrum[h * n : (h + 1) * n] * coul).astype(BF16)
                back.append((dot(cas, scaled) * (1.0 / n)).reshape(n_plane, GROUPS, half, n))
            for g in range(GROUPS):
                for q in range(n_plane):
                    both = jnp.concatenate([back[0][q, g], back[1][q, g]], 0)
                    send_b[s, g, q, at, :] = both.astype(BF16)
        for g in range(GROUPS):
            for d in range(1, n_plane):
                start(b_copy(g, s, p_peer(d), plane))
            recv_b[s, g, plane] = send_b[s, g, plane]

    def inverse(g, s):
        arrived(recv_b.at[s, g, pl.ds(0, n_plane - 1)], r_b.at[g, s])
        first, second = wide[3 * n :, :n], wide[3 * n :, n:]
        both = slim[2 * n : 4 * n, :]
        in_first = lax.broadcasted_iota(jnp.int32, (n, n), 1) < labels[:, 2:3]
        grid_b[: n_packed * half, :] = recv_b[s, g].reshape(n_packed * half, n).astype(F32)
        group = 4

        def step(i, _):
            for k in range(group):
                xi = i * group + k
                packed = grid_b[pl.ds(xi, n, stride=half), :]
                from_first = dot(first, jnp.where(in_first, packed, 0.0).astype(BF16))
                from_second = dot(second, jnp.where(in_first, 0.0, packed).astype(BF16))
                inverse_y = jnp.concatenate([from_first, from_second], 1) * (1.0 / n)
                at = pl.ds(pl.multiple_of(g * rows_g + xi * n, n), n)
                potential = dot(inverse_y.astype(BF16), both) * (1.0 / n)
                term = potential * shared[s, at, :].astype(F32)
                if s == 0:
                    total[at, :] = term
                else:
                    out_ref[at, :] = (total[at, :] + term).astype(BF16)
            return 0

        lax.fori_loop(0, half // group, step, 0)

    send_x(0)
    send_x(1)
    add_part(0)
    add_part(1)
    wait_x(0)
    send_y(0)
    for i in range(2, PIECES):
        add_part(i)
    wait_x(1)
    send_y(1)
    send_part()
    send_z(0)
    send_z(1)
    send_gy(0)
    send_gy(1)
    loads[4].wait()
    loads[5].wait()
    wait_gy(0)
    send_gx(0, 0)
    send_dy()
    wait_gy(1)
    send_gx(1, 0)
    forward(0, 0)
    send_gx(0, 1)
    send_gx(1, 1)
    forward(1, 0)
    send_dx()
    forward(0, 1)
    forward(1, 1)
    for g in range(GROUPS):
        sent(in_x.at[g, pl.ds(0, NX - 1)], s_x.at[g])
        sent(in_y.at[g, pl.ds(0, NY - 1)], s_y.at[g])
        sent(in_z.at[g], s_z.at[g])
        sent(shared.at[:, pl.ds(0, (NY - 1) * chunk_y)], s_gy.at[g])
        for s in range(STEPS):
            sent(shared.at[s, pl.ds(0, (NX - 1) * chunk_x)], s_gx.at[g, s])
    sent(in_part.at[pl.ds(0, n_plane - 1)], s_p)
    grid_b[n_packed * half :, :] = jnp.zeros(((n - n_packed) * half, n), F32)
    wait_dense()
    middle(0)
    sent(coul16.at[pl.ds(0, (NY - 1) * coul_y)], s_dy)
    sent(coul16.at[pl.ds(0, (NX - 1) * coul_x)], s_dx)
    middle(1)
    for g in range(GROUPS):
        for s in range(STEPS):
            sent(recv_f.at[s, g, pl.ds(0, n_plane - 1)], s_f.at[g, s])
    inverse(0, 0)
    inverse(1, 0)
    inverse(0, 1)
    inverse(1, 1)
    for g in range(GROUPS):
        for s in range(STEPS):
            sent(recv_b.at[s, g, pl.ds(0, n_plane - 1)], s_b.at[g, s])


def on_device(orbitals, coulomb, stick_lists, roots):
    _, width, n, _ = orbitals.shape
    n_plane = n // width
    rows = width * n
    rows_g = rows // GROUPS
    chunk_x, chunk_y = rows_g // NX, rows_g // (NX * NY)
    coul_block = n // (NX * NY) * width
    per_owner = packing(n, n_plane)[1]
    wide, slim, labels = tables(n, n_plane)
    hbm = pl.BlockSpec(memory_space=pl.ANY)
    vmem = pl.BlockSpec(memory_space=pltpu.VMEM)
    dma = pltpu.SemaphoreType.DMA

    def pair_of_sems(*shape):
        return [dma(shape), dma(shape)]

    gs = (GROUPS, STEPS)
    spectra = pltpu.VMEM((STEPS, GROUPS, n_plane, per_owner * width // GROUPS, n), BF16)
    out = pl.pallas_call(
        functools.partial(kernel, n, n_plane),
        out_shape=jax.ShapeDtypeStruct((rows, n), BF16),
        in_specs=[pl.BlockSpec(memory_space=pltpu.SMEM)] + [hbm] * 6,
        out_specs=vmem,
        scratch_shapes=[
            pltpu.VMEM((rows, n), F32),
            pltpu.VMEM(wide.shape, BF16),
            pltpu.VMEM(slim.shape, BF16),
            pltpu.VMEM(labels.shape, jnp.int32),
            pltpu.VMEM((16, coulomb.shape[1]), BF16),
            pltpu.VMEM(stick_lists.shape, jnp.int32),
            pltpu.VMEM((rows, n), BF16),
            pltpu.VMEM((GROUPS, NX, chunk_x, n), BF16),
            pltpu.VMEM(gs + (chunk_x, n), BF16),
            pltpu.VMEM((GROUPS, NY, STEPS, chunk_y, n), BF16),
            pltpu.VMEM(gs + (chunk_y, n), BF16),
            pltpu.VMEM(gs + (chunk_y, n), BF16),
            pltpu.VMEM((STEPS, rows, n), BF16),
            pltpu.VMEM((n // (NX * NY) * n, n), F32),
            pltpu.VMEM((n_plane, coul_block, n), BF16),
            pltpu.VMEM((n_plane, coul_block, n), BF16),
            pltpu.VMEM((rows, n), BF16),
            pltpu.VMEM((rows, n), F32),
            pltpu.VMEM((rows_g, n), F32),
            pltpu.VMEM((rows_g, n), F32),
            spectra, spectra, spectra, spectra,
            pltpu.VMEM((rows, n), F32),
            dma((6,)),
            *pair_of_sems(GROUPS),
            *pair_of_sems(GROUPS),
            *pair_of_sems(GROUPS),
            *pair_of_sems(GROUPS),
            *pair_of_sems(*gs),
            dma, dma, dma, dma, dma, dma,
            *pair_of_sems(*gs),
            *pair_of_sems(*gs),
        ],
        compiler_params=pltpu.CompilerParams(
            collective_id=0, has_side_effects=True, vmem_limit_bytes=57 * 1024 * 1024
        ),
        name="exchange",
    )(
        roots, orbitals.reshape(rows, n),
        wide, slim, labels, coulomb, stick_lists,
    )
    return out.reshape(1, width, n, n)


def solution(mesh):
    in_specs = (P("band", "plane", None, None), P(None, "plane"), P(), P())
    out_specs = P("band", "plane", None, None)
    return jax.shard_map(
        on_device, mesh=mesh, in_specs=in_specs, out_specs=out_specs, check_vma=False
    )
```

```python
import functools
import math

import jax
import jax.numpy as jnp
import numpy as np
from jax import lax
from jax.experimental import pallas as pl
from jax.experimental.pallas import tpu as pltpu
from jax.sharding import PartitionSpec as P

NX, NZ, NY = 4, 2, 8
STICKS = 12288
GROUPS = 2
STEPS = 2
PIECES = 3
MESH = pl.DeviceIdType.MESH
F32, BF16 = jnp.float32, jnp.bfloat16


def cas_table(n):
    k = np.arange(n)
    angles = 2.0 * math.pi / n * ((k[:, None] * k[None, :]) % n)
    return np.asarray(np.cos(angles) + np.sin(angles), np.float32)


def pair_table(n, width):
    cas = cas_table(n)
    half = width // GROUPS
    table = np.zeros((2, n, GROUPS, n // width, 2, half), np.float32)
    by_x = cas.reshape(n, n // width, GROUPS, half).transpose(0, 2, 1, 3)
    for h in range(2):
        table[h, :, :, :, h, :] = by_x
    return table.reshape(2 * n, 2 * n)


def packing(n, n_plane):
    signed = np.minimum(np.arange(n), n - np.arange(n))
    squares = signed[:, None] ** 2 + signed[None, :] ** 2
    kept = (squares <= np.sort(squares.reshape(-1))[STICKS - 1]).sum(1)
    best = None
    for t in range(1, n // 2 + 1):
        for extra in ([], [n - t + 1]):
            second = [h for h in range(n) if kept[h] and (signed[h] >= t or h in extra)]
            firsts = [h for h in range(n) if kept[h] and h not in second]
            free, mate = sorted(firsts, key=lambda h: -kept[h]), {}
            for h in sorted(second, key=lambda h: -kept[h]):
                host = next((f for f in free if kept[f] + kept[h] <= n), None)
                if host is None:
                    break
                free.remove(host)
                mate[host] = h
            else:
                if best is None or len(firsts) < len(best[0]):
                    best = firsts, mate, t, extra
    firsts, mate, t, extra = best
    per_owner = -(-len(firsts) // (2 * n_plane)) * 2
    table = -np.ones((per_owner * n_plane, 3), np.int64)
    for row, h in enumerate(firsts):
        table[row] = h, mate.get(h, -1), kept[h]
    return table, per_owner, t, (extra or [-1])[0]


def tables(n, n_plane):
    width = n // n_plane
    cas = cas_table(n)
    rows, per_owner, _, _ = packing(n, n_plane)
    order = sorted(range(n), key=lambda g: (min(g, n - g), g > n // 2))
    both = np.concatenate([cas[:, order], cas[:, order[::-1]]], 1)
    first, second = np.zeros((n, n), np.float32), np.zeros((n, n), np.float32)
    for row, (h, other, _) in enumerate(rows):
        if h >= 0:
            first[row] = cas[h]
        if other >= 0:
            second[row] = cas[other]
    wide = np.concatenate([both, pair_table(n, width), np.concatenate([first.T, second.T], 1)], 0)
    slim = np.concatenate([first, second, both.T, cas], 0)
    labels = np.full((n, 128), -7, np.int32)
    for row, (h, other, length) in enumerate(rows):
        place = row // per_owner * width + row % per_owner
        labels[place, 0] = h if h >= 0 else -7
        labels[place, 1] = other if other >= 0 else -7
    labels[:, 2] = n
    labels[: len(rows), 2] = np.where(rows[:, 2] < 0, n, rows[:, 2])
    return jnp.asarray(wide).astype(BF16), jnp.asarray(slim).astype(BF16), jnp.asarray(labels)


def dot(a, b):
    return jnp.dot(a, b, preferred_element_type=F32)


def far_first(count):
    return sorted(range(1, count), key=lambda d: -min(d, count - d))


def pick(index, values):
    out = values[0]
    for k in range(1, len(values)):
        out = jnp.where(index == k, values[k], out)
    return out


def remote(src, dst, send_sem, recv_sem, device):
    return pltpu.make_async_remote_copy(
        src_ref=src, dst_ref=dst, send_sem=send_sem, recv_sem=recv_sem,
        device_id=device, device_id_type=MESH,
    )


def kernel(
    n, n_plane,
    roots_ref, orb_hbm, wide_hbm, slim_hbm, labels_hbm, coulomb_hbm, ids_hbm, out_ref,
    orb, wide, slim, labels, coulomb, ids_ref,
    orb16, in_x, sel, in_y, cand, in_z, shared,
    flat_sum, part, in_part, coul16, dense, grid_a, grid_b, send_f, recv_f, send_b, recv_b, total,
    s_in, s_x, r_x, s_y, r_y, s_z, r_z, s_gy, r_gy, s_gx, r_gx,
    s_p, r_p, s_dy, r_dy, s_dx, r_dx, s_f, r_f, s_b, r_b,
):
    width = n // n_plane
    rows = width * n
    rows_g = rows // GROUPS
    _, per_owner, edge, edge_row = packing(n, n_plane)
    n_packed = per_owner * n_plane
    chunk_x, chunk_y = rows_g // NX, rows_g // (NX * NY)
    band, plane = lax.axis_index("band"), lax.axis_index("plane")
    y = lax.rem(band, NY)
    zh = lax.rem(band // NY, NZ)
    x = band // (NY * NZ)

    def at_band(bx, bz, by):
        return {"band": (bx * NZ + bz) * NY + by}

    def x_peer(d):
        return lax.rem(x + d, NX)

    def y_peer(d):
        return lax.rem(y + d, NY)

    def p_peer(d):
        return lax.rem(plane + d, n_plane)

    bits = [lax.rem(plane // (1 << k), 2) for k in range(n_plane.bit_length() - 1)]
    owners = []
    for flip in sorted(range(1, n_plane), key=lambda f: (-(f >> 1), f)):
        t = 0
        for k, bit in enumerate(bits):
            t = t + (1 << k) * (1 - bit if flip >> k & 1 else bit)
        owners.append(t)

    barrier = pltpu.get_barrier_semaphore()
    peers = [at_band(x_peer(d), zh, y) for d in far_first(NX)]
    peers += [at_band(x, zh, y_peer(d)) for d in far_first(NY)]
    peers += [at_band(x, lax.rem(zh + d, NZ), y) for d in range(1, NZ)]
    peers += [{"plane": p_peer(d)} for d in range(1, n_plane)]
    for peer in peers:
        pl.semaphore_signal(barrier, inc=1, device_id=peer, device_id_type=MESH)

    coul_rows = n // (NX * NY)
    first_row = (x * NY + y) * coul_rows
    coul_tile = pl.multiple_of(first_row // 16 * 16, 16)
    loads = [
        pltpu.make_async_copy(orb_hbm, orb, s_in.at[0]),
        pltpu.make_async_copy(coulomb_hbm.at[pl.ds(coul_tile, 16)], coulomb, s_in.at[1]),
        pltpu.make_async_copy(ids_hbm, ids_ref, s_in.at[2]),
        pltpu.make_async_copy(labels_hbm, labels, s_in.at[3]),
        pltpu.make_async_copy(slim_hbm, slim, s_in.at[4]),
        pltpu.make_async_copy(wide_hbm, wide, s_in.at[5]),
    ]
    for load in loads:
        load.start()
    loads[0].wait()
    orb16[...] = orb[...].astype(BF16)
    pl.semaphore_wait(barrier, len(peers))

    def start(copy):
        copy.start()

    def arrived(region, sem):
        remote(region, region, sem, sem, {"plane": p_peer(1)}).wait_recv()

    def sent(region, sem):
        remote(region, region, sem, sem, {"plane": p_peer(1)}).wait_send()

    def x_copy(g, target, slot):
        return remote(
            orb16.at[pl.ds(g * rows_g + target * chunk_x, chunk_x)], in_x.at[g, slot],
            s_x.at[g], r_x.at[g], at_band(target, zh, y),
        )

    def send_x(g):
        for d in far_first(NX):
            start(x_copy(g, x_peer(d), x))
        in_x[g, x] = orb16[pl.ds(g * rows_g + x * chunk_x, chunk_x), :]

    def wait_x(g):
        arrived(in_x.at[g, pl.ds(0, NX - 1)], r_x.at[g])

    root = [roots_ref[s] for s in range(STEPS)]
    root_y = [lax.rem(r, NY) for r in root]
    root_z = [lax.rem(r // NY, NZ) for r in root]
    root_x = [r // (NY * NZ) for r in root]

    def y_copy(g, s, target, slot):
        return remote(
            sel.at[g, s, pl.ds(target * chunk_y, chunk_y)], in_y.at[g, s, slot],
            s_y.at[g, s], r_y.at[g, s], at_band(x, zh, target),
        )

    def send_y(g, s):
        sel[g, s] = pick(root_x[s], [in_x[g, k] for k in range(NX)])
        for d in far_first(NY):
            start(y_copy(g, s, y_peer(d), y))
        in_y[g, s, y] = sel[g, s, pl.ds(y * chunk_y, chunk_y), :]

    def z_copy(g, s):
        return remote(
            cand.at[g, s], in_z.at[g, s], s_z.at[g, s], r_z.at[g, s],
            at_band(x, lax.rem(zh + 1, NZ), y),
        )

    def send_z(g, s):
        arrived(in_y.at[g, s, pl.ds(0, NY - 1)], r_y.at[g, s])
        cand[g, s] = pick(root_y[s], [in_y[g, s, k] for k in range(NY)])
        start(z_copy(g, s))

    def gy_copy(g, s, target, owner):
        block = shared.at[s, pl.ds(g * rows_g + x * chunk_x + owner * chunk_y, chunk_y)]
        return remote(block, block, s_gy.at[g, s], r_gy.at[g, s], at_band(x, zh, target))

    def send_gy(g, s):
        z_copy(g, s).wait_recv()
        at = pl.ds(g * rows_g + x * chunk_x + y * chunk_y, chunk_y)
        shared[s, at, :] = jnp.where(root_z[s] == zh, cand[g, s], in_z[g, s])
        for d in far_first(NY):
            start(gy_copy(g, s, y_peer(d), y))

    def gx_copy(g, s, target, owner):
        block = shared.at[s, pl.ds(g * rows_g + owner * chunk_x, chunk_x)]
        return remote(block, block, s_gx.at[g, s], r_gx.at[g, s], at_band(target, zh, y))

    def send_gx(g, s):
        first = g * rows_g + x * chunk_x
        arrived(shared.at[s, pl.ds(first, (NY - 1) * chunk_y)], r_gy.at[g, s])
        for d in far_first(NX):
            start(gx_copy(g, s, x_peer(d), x))

    def p_copy(target, slot):
        return remote(part.at[target], in_part.at[slot], s_p, r_p, {"plane": target})

    slots = ids_ref.shape[1]
    piece = -(-slots // (128 * PIECES)) * 128

    def add_part(i):
        if i == 0:
            loads[1].wait()
            loads[2].wait()
            loads[3].wait()
        at = slice(i * piece, min((i + 1) * piece, slots))
        ids = ids_ref[pl.ds(plane, 1), at]
        valid = ids >= 0
        id_h = jnp.where(valid, ids // n, -1)
        id_g = jnp.where(valid, lax.rem(ids, n), 0)
        lane = jnp.where(id_g == 0, 0, jnp.where(id_g <= n // 2, 2 * id_g - 1, 2 * (n - id_g)))
        reverse = (jnp.minimum(id_h, n - id_h) >= edge) | (id_h == edge_row)
        lane = jnp.where(reverse, n - 1 - lane, lane)
        iota = lax.broadcasted_iota(jnp.int32, (n, ids.shape[1]), 0)
        hot_h = (labels[:, 0:1] == id_h) | (labels[:, 1:2] == id_h)
        hot_g = jnp.where(iota == lane, 1.0, 0.0).astype(BF16)
        tile = coulomb[:, at].astype(F32)
        own = tile[:coul_rows]
        for k in range(1, 16 // coul_rows):
            inside = first_row - coul_tile == k * coul_rows
            own = jnp.where(inside, tile[k * coul_rows : (k + 1) * coul_rows], own)
        left = jnp.concatenate(
            [jnp.where(hot_h, own[k : k + 1], 0.0).astype(BF16) for k in range(coul_rows)], 0
        )
        flat = lax.dot_general(
            left, hot_g, (((1,), (1,)), ((), ())), preferred_element_type=F32
        )
        flat_sum[...] = flat if i == 0 else flat_sum[...] + flat

    def send_part():
        for k in range(coul_rows):
            for o in range(n_plane):
                at = slice(k * n + o * width, k * n + (o + 1) * width)
                part[o, k * width : (k + 1) * width, :] = flat_sum[at, :].astype(BF16)
        for t in owners:
            start(p_copy(t, plane))
        in_part[plane] = part[plane]

    coul_x, coul_y = rows // NX, rows // (NX * NY)

    def dy_copy(target, owner):
        block = coul16.at[pl.ds(x * coul_x + owner * coul_y, coul_y)]
        return remote(block, block, s_dy, r_dy, at_band(x, zh, target))

    def send_dy():
        arrived(in_part.at[pl.ds(0, n_plane - 1)], r_p)
        summed = in_part[0].astype(F32)
        for o in range(1, n_plane):
            summed = summed + in_part[o].astype(F32)
        coul16[pl.ds(x * coul_x + y * coul_y, coul_y), :] = summed.astype(BF16)
        for d in far_first(NY):
            start(dy_copy(y_peer(d), y))

    def dx_copy(target, owner):
        block = coul16.at[pl.ds(owner * coul_x, coul_x)]
        return remote(block, block, s_dx, r_dx, at_band(target, zh, y))

    def send_dx():
        arrived(coul16.at[pl.ds(x * coul_x, (NY - 1) * coul_y)], r_dy)
        for d in far_first(NX):
            start(dx_copy(x_peer(d), x))

    def wait_dense():
        arrived(coul16.at[pl.ds(0, (NX - 1) * coul_x)], r_dx)
        dense[...] = coul16[...].astype(F32)

    half = width // GROUPS
    block = per_owner * half

    def f_copy(g, s, target, slot):
        return remote(
            send_f.at[s, g, target], recv_f.at[s, g, slot],
            s_f.at[g, s], r_f.at[g, s], {"plane": target},
        )

    def forward(g, s):
        arrived(shared.at[s, pl.ds(g * rows_g, (NX - 1) * chunk_x)], r_gx.at[g, s])
        both = wide[:n, :]
        first, second = slim[:n_packed, :], slim[n : n + n_packed, :]
        in_first = lax.broadcasted_iota(jnp.int32, (n_packed, n), 1) < labels[:n_packed, 2:3]
        group = 4

        def step(i, _):
            at = pl.ds(pl.multiple_of(g * rows_g + i * (group * n), group * n), group * n)
            pair = (orb[at, :] * shared[s, at, :].astype(F32)).astype(BF16)
            along = dot(pair, both).astype(BF16)
            for k in range(group):
                plane_k = along[k * n : (k + 1) * n]
                packed = jnp.where(in_first, dot(first, plane_k[:, :n]), dot(second, plane_k[:, n:]))
                grid_a[pl.ds(i * group + k, n_packed, stride=half), :] = packed
            return 0

        lax.fori_loop(0, half // group, step, 0)
        for t in owners:
            send_f[s, g, t] = grid_a[pl.ds(pl.multiple_of(t * block, block), block), :].astype(BF16)
            start(f_copy(g, s, t, plane))
        at = pl.ds(pl.multiple_of(plane * block, block), block)
        recv_f[s, g, plane] = grid_a[at, :].astype(BF16)

    def b_copy(g, s, target, slot):
        return remote(
            send_b.at[s, g, target], recv_b.at[s, g, slot],
            s_b.at[g, s], r_b.at[g, s], {"plane": target},
        )

    def middle(s):
        for g in range(GROUPS):
            arrived(recv_f.at[s, g, pl.ds(0, n_plane - 1)], r_f.at[g, s])
        twin, cas = wide[n : 3 * n, :], slim[4 * n : 5 * n, :]
        for j in range(per_owner // 2):
            at = slice(j * 2 * half, (j + 1) * 2 * half)
            spectrum = dot(twin, recv_f[s, :, :, at, :].reshape(2 * n, n))
            back = []
            for h in range(2):
                coul = dense[pl.ds(2 * j + h, n, stride=width), :]
                scaled = (spectrum[h * n : (h + 1) * n] * coul).astype(BF16)
                back.append((dot(cas, scaled) * (1.0 / n)).reshape(n_plane, GROUPS, half, n))
            for g in range(GROUPS):
                for q in range(n_plane):
                    both = jnp.concatenate([back[0][q, g], back[1][q, g]], 0)
                    send_b[s, g, q, at, :] = both.astype(BF16)
        for g in range(GROUPS):
            for t in owners:
                start(b_copy(g, s, t, plane))
            recv_b[s, g, plane] = send_b[s, g, plane]

    def inverse(g, s):
        arrived(recv_b.at[s, g, pl.ds(0, n_plane - 1)], r_b.at[g, s])
        first, second = wide[3 * n :, :n], wide[3 * n :, n:]
        both = slim[2 * n : 4 * n, :]
        in_first = lax.broadcasted_iota(jnp.int32, (n, n), 1) < labels[:, 2:3]
        grid_b[: n_packed * half, :] = recv_b[s, g].reshape(n_packed * half, n).astype(F32)
        group = 4

        def step(i, _):
            for k in range(group):
                xi = i * group + k
                packed = grid_b[pl.ds(xi, n, stride=half), :]
                from_first = dot(first, jnp.where(in_first, packed, 0.0).astype(BF16))
                from_second = dot(second, jnp.where(in_first, 0.0, packed).astype(BF16))
                inverse_y = jnp.concatenate([from_first, from_second], 1) * (1.0 / n)
                at = pl.ds(pl.multiple_of(g * rows_g + xi * n, n), n)
                potential = dot(inverse_y.astype(BF16), both) * (1.0 / n)
                term = potential * shared[s, at, :].astype(F32)
                if s == 0:
                    total[at, :] = term
                else:
                    out_ref[at, :] = (total[at, :] + term).astype(BF16)
            return 0

        lax.fori_loop(0, half // group, step, 0)

    send_x(0)
    send_x(1)
    for i in range(PIECES):
        add_part(i)
    wait_x(0)
    send_y(0, 0)
    send_y(0, 1)
    send_part()
    wait_x(1)
    send_y(1, 0)
    send_z(0, 0)
    send_y(1, 1)
    send_z(0, 1)
    send_z(1, 0)
    send_gy(0, 0)
    send_z(1, 1)
    send_gy(0, 1)
    send_gy(1, 0)
    send_gx(0, 0)
    send_gy(1, 1)
    loads[4].wait()
    loads[5].wait()
    send_gx(1, 0)
    forward(0, 0)
    send_gx(0, 1)
    send_gx(1, 1)
    send_dy()
    forward(1, 0)
    send_dx()
    forward(0, 1)
    forward(1, 1)
    for g in range(GROUPS):
        sent(in_x.at[g, pl.ds(0, NX - 1)], s_x.at[g])
        for s in range(STEPS):
            sent(in_y.at[g, s, pl.ds(0, NY - 1)], s_y.at[g, s])
            sent(in_z.at[g, s], s_z.at[g, s])
            sent(shared.at[s, pl.ds(0, (NY - 1) * chunk_y)], s_gy.at[g, s])
            sent(shared.at[s, pl.ds(0, (NX - 1) * chunk_x)], s_gx.at[g, s])
    sent(in_part.at[pl.ds(0, n_plane - 1)], s_p)
    grid_b[n_packed * half :, :] = jnp.zeros(((n - n_packed) * half, n), F32)
    wait_dense()
    middle(0)
    sent(coul16.at[pl.ds(0, (NY - 1) * coul_y)], s_dy)
    sent(coul16.at[pl.ds(0, (NX - 1) * coul_x)], s_dx)
    middle(1)
    for g in range(GROUPS):
        for s in range(STEPS):
            sent(recv_f.at[s, g, pl.ds(0, n_plane - 1)], s_f.at[g, s])
    inverse(0, 0)
    inverse(1, 0)
    inverse(0, 1)
    inverse(1, 1)
    for g in range(GROUPS):
        for s in range(STEPS):
            sent(recv_b.at[s, g, pl.ds(0, n_plane - 1)], s_b.at[g, s])


def on_device(orbitals, coulomb, stick_lists, roots):
    _, width, n, _ = orbitals.shape
    n_plane = n // width
    rows = width * n
    rows_g = rows // GROUPS
    chunk_x, chunk_y = rows_g // NX, rows_g // (NX * NY)
    coul_block = n // (NX * NY) * width
    per_owner = packing(n, n_plane)[1]
    wide, slim, labels = tables(n, n_plane)
    hbm = pl.BlockSpec(memory_space=pl.ANY)
    vmem = pl.BlockSpec(memory_space=pltpu.VMEM)
    dma = pltpu.SemaphoreType.DMA

    def pair_of_sems(*shape):
        return [dma(shape), dma(shape)]

    gs = (GROUPS, STEPS)
    spectra = pltpu.VMEM((STEPS, GROUPS, n_plane, per_owner * width // GROUPS, n), BF16)
    out = pl.pallas_call(
        functools.partial(kernel, n, n_plane),
        out_shape=jax.ShapeDtypeStruct((rows, n), BF16),
        in_specs=[pl.BlockSpec(memory_space=pltpu.SMEM)] + [hbm] * 6,
        out_specs=vmem,
        scratch_shapes=[
            pltpu.VMEM((rows, n), F32),
            pltpu.VMEM(wide.shape, BF16),
            pltpu.VMEM(slim.shape, BF16),
            pltpu.VMEM(labels.shape, jnp.int32),
            pltpu.VMEM((16, coulomb.shape[1]), BF16),
            pltpu.VMEM(stick_lists.shape, jnp.int32),
            pltpu.VMEM((rows, n), BF16),
            pltpu.VMEM((GROUPS, NX, chunk_x, n), BF16),
            pltpu.VMEM(gs + (chunk_x, n), BF16),
            pltpu.VMEM(gs + (NY, chunk_y, n), BF16),
            pltpu.VMEM(gs + (chunk_y, n), BF16),
            pltpu.VMEM(gs + (chunk_y, n), BF16),
            pltpu.VMEM((STEPS, rows, n), BF16),
            pltpu.VMEM((n // (NX * NY) * n, n), F32),
            pltpu.VMEM((n_plane, coul_block, n), BF16),
            pltpu.VMEM((n_plane, coul_block, n), BF16),
            pltpu.VMEM((rows, n), BF16),
            pltpu.VMEM((rows, n), F32),
            pltpu.VMEM((rows_g, n), F32),
            pltpu.VMEM((rows_g, n), F32),
            spectra, spectra, spectra, spectra,
            pltpu.VMEM((rows, n), F32),
            dma((6,)),
            *pair_of_sems(GROUPS),
            *pair_of_sems(*gs),
            *pair_of_sems(*gs),
            *pair_of_sems(*gs),
            *pair_of_sems(*gs),
            dma, dma, dma, dma, dma, dma,
            *pair_of_sems(*gs),
            *pair_of_sems(*gs),
        ],
        compiler_params=pltpu.CompilerParams(
            collective_id=0, has_side_effects=True, vmem_limit_bytes=57 * 1024 * 1024
        ),
        name="exchange",
    )(
        roots, orbitals.reshape(rows, n),
        wide, slim, labels, coulomb, stick_lists,
    )
    return out.reshape(1, width, n, n)


def solution(mesh):
    in_specs = (P("band", "plane", None, None), P(None, "plane"), P(), P())
    out_specs = P("band", "plane", None, None)
    return jax.shard_map(
        on_device, mesh=mesh, in_specs=in_specs, out_specs=out_specs, check_vma=False
    )
```

```python
import functools
import math

import jax
import jax.numpy as jnp
import numpy as np
from jax import lax
from jax.experimental import pallas as pl
from jax.experimental.pallas import tpu as pltpu
from jax.sharding import PartitionSpec as P

NX, NZ, NY = 4, 2, 8
STICKS = 12288
GROUPS = 2
STEPS = 2
PIECES = 3
MESH = pl.DeviceIdType.MESH
F32, BF16 = jnp.float32, jnp.bfloat16


def cas_table(n):
    k = np.arange(n)
    angles = 2.0 * math.pi / n * ((k[:, None] * k[None, :]) % n)
    return np.asarray(np.cos(angles) + np.sin(angles), np.float32)


def pair_table(n, width):
    cas = cas_table(n)
    half = width // GROUPS
    table = np.zeros((2, n, GROUPS, n // width, 2, half), np.float32)
    by_x = cas.reshape(n, n // width, GROUPS, half).transpose(0, 2, 1, 3)
    for h in range(2):
        table[h, :, :, :, h, :] = by_x
    return table.reshape(2 * n, 2 * n)


def packing(n, n_plane):
    signed = np.minimum(np.arange(n), n - np.arange(n))
    squares = signed[:, None] ** 2 + signed[None, :] ** 2
    kept = (squares <= np.sort(squares.reshape(-1))[STICKS - 1]).sum(1)
    best = None
    for t in range(1, n // 2 + 1):
        for extra in ([], [n - t + 1]):
            second = [h for h in range(n) if kept[h] and (signed[h] >= t or h in extra)]
            firsts = [h for h in range(n) if kept[h] and h not in second]
            free, mate = sorted(firsts, key=lambda h: -kept[h]), {}
            for h in sorted(second, key=lambda h: -kept[h]):
                host = next((f for f in free if kept[f] + kept[h] <= n), None)
                if host is None:
                    break
                free.remove(host)
                mate[host] = h
            else:
                if best is None or len(firsts) < len(best[0]):
                    best = firsts, mate, t, extra
    firsts, mate, t, extra = best
    per_owner = -(-len(firsts) // (2 * n_plane)) * 2
    table = -np.ones((per_owner * n_plane, 3), np.int64)
    for row, h in enumerate(firsts):
        table[row] = h, mate.get(h, -1), kept[h]
    return table, per_owner, t, (extra or [-1])[0]


def tables(n, n_plane):
    width = n // n_plane
    cas = cas_table(n)
    rows, per_owner, _, _ = packing(n, n_plane)
    order = sorted(range(n), key=lambda g: (min(g, n - g), g > n // 2))
    both = np.concatenate([cas[:, order], cas[:, order[::-1]]], 1)
    first, second = np.zeros((n, n), np.float32), np.zeros((n, n), np.float32)
    for row, (h, other, _) in enumerate(rows):
        if h >= 0:
            first[row] = cas[h]
        if other >= 0:
            second[row] = cas[other]
    wide = np.concatenate([both, pair_table(n, width), np.concatenate([first.T, second.T], 1)], 0)
    slim = np.concatenate([first, second, both.T, cas], 0)
    labels = np.full((n, 128), -7, np.int32)
    for row, (h, other, length) in enumerate(rows):
        place = row // per_owner * width + row % per_owner
        labels[place, 0] = h if h >= 0 else -7
        labels[place, 1] = other if other >= 0 else -7
    labels[:, 2] = n
    labels[: len(rows), 2] = np.where(rows[:, 2] < 0, n, rows[:, 2])
    return jnp.asarray(wide).astype(BF16), jnp.asarray(slim).astype(BF16), jnp.asarray(labels)


def dot(a, b):
    return jnp.dot(a, b, preferred_element_type=F32)


def broadcast_pieces(rows):
    return [(0, rows // 4), (rows // 4, rows // 4), (rows // 2, rows // 2)]


def far_first(count):
    return sorted(range(1, count), key=lambda d: -min(d, count - d))


def pick(index, values):
    out = values[0]
    for k in range(1, len(values)):
        out = jnp.where(index == k, values[k], out)
    return out


def remote(src, dst, send_sem, recv_sem, device):
    return pltpu.make_async_remote_copy(
        src_ref=src, dst_ref=dst, send_sem=send_sem, recv_sem=recv_sem,
        device_id=device, device_id_type=MESH,
    )


def kernel(
    n, n_plane,
    roots_ref, orb_hbm, wide_hbm, slim_hbm, labels_hbm, coulomb_hbm, ids_hbm, out_ref,
    orb, wide, slim, labels, coulomb, ids_ref,
    orb16, in_x0, in_x1, in_x2, sel0, sel1, sel2, in_y0, in_y1, in_y2,
    cand0, cand1, cand2, in_z0, in_z1, in_z2, shared,
    flat_sum, part, in_part, coul16, dense, grid_a, grid_b, send_f, recv_f, send_b, recv_b, total,
    s_in, s_x, r_x, s_y, r_y, s_z, r_z, s_gy, r_gy, s_gx, r_gx,
    s_p, r_p, s_dy, r_dy, s_dx, r_dx, s_f, r_f, s_b, r_b,
):
    width = n // n_plane
    rows = width * n
    rows_g = rows // GROUPS
    _, per_owner, edge, edge_row = packing(n, n_plane)
    n_packed = per_owner * n_plane
    in_x, sel, in_y = [in_x0, in_x1, in_x2], [sel0, sel1, sel2], [in_y0, in_y1, in_y2]
    cand, in_z = [cand0, cand1, cand2], [in_z0, in_z1, in_z2]
    pieces = broadcast_pieces(rows)
    band, plane = lax.axis_index("band"), lax.axis_index("plane")
    y = lax.rem(band, NY)
    zh = lax.rem(band // NY, NZ)
    x = band // (NY * NZ)

    def at_band(bx, bz, by):
        return {"band": (bx * NZ + bz) * NY + by}

    def x_peer(d):
        return lax.rem(x + d, NX)

    def y_peer(d):
        return lax.rem(y + d, NY)

    def p_peer(d):
        return lax.rem(plane + d, n_plane)

    bits = [lax.rem(plane // (1 << k), 2) for k in range(n_plane.bit_length() - 1)]
    owners = []
    for flip in sorted(range(1, n_plane), key=lambda f: (-(f >> 1), f)):
        t = 0
        for k, bit in enumerate(bits):
            t = t + (1 << k) * (1 - bit if flip >> k & 1 else bit)
        owners.append(t)

    barrier = pltpu.get_barrier_semaphore()
    peers = [at_band(x_peer(d), zh, y) for d in far_first(NX)]
    peers += [at_band(x, zh, y_peer(d)) for d in far_first(NY)]
    peers += [at_band(x, lax.rem(zh + d, NZ), y) for d in range(1, NZ)]
    peers += [{"plane": p_peer(d)} for d in range(1, n_plane)]
    for peer in peers:
        pl.semaphore_signal(barrier, inc=1, device_id=peer, device_id_type=MESH)

    coul_rows = n // (NX * NY)
    first_row = (x * NY + y) * coul_rows
    coul_tile = pl.multiple_of(first_row // 16 * 16, 16)
    loads = [
        pltpu.make_async_copy(orb_hbm, orb, s_in.at[0]),
        pltpu.make_async_copy(coulomb_hbm.at[pl.ds(coul_tile, 16)], coulomb, s_in.at[1]),
        pltpu.make_async_copy(ids_hbm, ids_ref, s_in.at[2]),
        pltpu.make_async_copy(labels_hbm, labels, s_in.at[3]),
        pltpu.make_async_copy(slim_hbm, slim, s_in.at[4]),
        pltpu.make_async_copy(wide_hbm, wide, s_in.at[5]),
    ]
    for load in loads:
        load.start()
    loads[0].wait()
    orb16[...] = orb[...].astype(BF16)
    pl.semaphore_wait(barrier, len(peers))

    def start(copy):
        copy.start()

    def arrived(region, sem):
        remote(region, region, sem, sem, {"plane": p_peer(1)}).wait_recv()

    def sent(region, sem):
        remote(region, region, sem, sem, {"plane": p_peer(1)}).wait_send()

    def x_copy(p, target, slot):
        first, count = pieces[p]
        chunk = count // NX
        return remote(
            orb16.at[pl.ds(first + target * chunk, chunk)], in_x[p].at[slot],
            s_x.at[p], r_x.at[p], at_band(target, zh, y),
        )

    def send_x(p):
        for d in far_first(NX):
            start(x_copy(p, x_peer(d), x))
        first, count = pieces[p]
        chunk = count // NX
        in_x[p][x] = orb16[pl.ds(first + x * chunk, chunk), :]

    root = [roots_ref[s] for s in range(STEPS)]
    root_y = [lax.rem(r, NY) for r in root]
    root_z = [lax.rem(r // NY, NZ) for r in root]
    root_x = [r // (NY * NZ) for r in root]

    def send_y(p):
        arrived(in_x[p].at[pl.ds(0, NX - 1)], r_x.at[p])
        for s in range(STEPS):
            sel[p][s] = pick(root_x[s], [in_x[p][k] for k in range(NX)])
        chunk = pieces[p][1] // (NX * NY)
        for d in far_first(NY):
            t = y_peer(d)
            start(remote(
                sel[p].at[:, pl.ds(t * chunk, chunk)], in_y[p].at[y],
                s_y.at[p], r_y.at[p], at_band(x, zh, t),
            ))
        in_y[p][y] = sel[p][:, pl.ds(y * chunk, chunk), :]

    def z_copy(p):
        return remote(
            cand[p], in_z[p], s_z.at[p], r_z.at[p], at_band(x, lax.rem(zh + 1, NZ), y)
        )

    def send_z(p):
        arrived(in_y[p].at[pl.ds(0, NY - 1)], r_y.at[p])
        for s in range(STEPS):
            cand[p][s] = pick(root_y[s], [in_y[p][k, s] for k in range(NY)])
        start(z_copy(p))

    def send_gy(p):
        z_copy(p).wait_recv()
        first, count = pieces[p]
        chunk = count // (NX * NY)
        at = pl.ds(first + (x * NY + y) * chunk, chunk)
        for s in range(STEPS):
            shared[s, at, :] = jnp.where(root_z[s] == zh, cand[p][s], in_z[p][s])
        block = shared.at[:, at]
        for d in far_first(NY):
            start(remote(block, block, s_gy.at[p], r_gy.at[p], at_band(x, zh, y_peer(d))))

    def wait_gy(p):
        first, count = pieces[p]
        chunk = count // (NX * NY)
        arrived(shared.at[:, pl.ds(first + x * NY * chunk, (NY - 1) * chunk)], r_gy.at[p])

    def send_gx(p, s):
        first, count = pieces[p]
        block = shared.at[s, pl.ds(first + x * (count // NX), count // NX)]
        for d in far_first(NX):
            start(remote(block, block, s_gx.at[p, s], r_gx.at[p, s], at_band(x_peer(d), zh, y)))

    def wait_gx(p, s):
        first, count = pieces[p]
        arrived(shared.at[s, pl.ds(first, count // NX * (NX - 1))], r_gx.at[p, s])

    def p_copy(target, slot):
        return remote(part.at[target], in_part.at[slot], s_p, r_p, {"plane": target})

    slots = ids_ref.shape[1]
    piece = -(-slots // (128 * PIECES)) * 128

    def add_part(i):
        if i == 0:
            loads[1].wait()
            loads[2].wait()
            loads[3].wait()
        at = slice(i * piece, min((i + 1) * piece, slots))
        ids = ids_ref[pl.ds(plane, 1), at]
        valid = ids >= 0
        id_h = jnp.where(valid, ids // n, -1)
        id_g = jnp.where(valid, lax.rem(ids, n), 0)
        lane = jnp.where(id_g == 0, 0, jnp.where(id_g <= n // 2, 2 * id_g - 1, 2 * (n - id_g)))
        reverse = (jnp.minimum(id_h, n - id_h) >= edge) | (id_h == edge_row)
        lane = jnp.where(reverse, n - 1 - lane, lane)
        iota = lax.broadcasted_iota(jnp.int32, (n, ids.shape[1]), 0)
        hot_h = (labels[:, 0:1] == id_h) | (labels[:, 1:2] == id_h)
        hot_g = jnp.where(iota == lane, 1.0, 0.0).astype(BF16)
        tile = coulomb[:, at].astype(F32)
        own = tile[:coul_rows]
        for k in range(1, 16 // coul_rows):
            inside = first_row - coul_tile == k * coul_rows
            own = jnp.where(inside, tile[k * coul_rows : (k + 1) * coul_rows], own)
        left = jnp.concatenate(
            [jnp.where(hot_h, own[k : k + 1], 0.0).astype(BF16) for k in range(coul_rows)], 0
        )
        flat = lax.dot_general(
            left, hot_g, (((1,), (1,)), ((), ())), preferred_element_type=F32
        )
        flat_sum[...] = flat if i == 0 else flat_sum[...] + flat

    def send_part():
        for k in range(coul_rows):
            for o in range(n_plane):
                at = slice(k * n + o * width, k * n + (o + 1) * width)
                part[o, k * width : (k + 1) * width, :] = flat_sum[at, :].astype(BF16)
        for t in owners:
            start(p_copy(t, plane))
        in_part[plane] = part[plane]

    coul_x, coul_y = rows // NX, rows // (NX * NY)

    def dy_copy(target, owner):
        block = coul16.at[pl.ds(x * coul_x + owner * coul_y, coul_y)]
        return remote(block, block, s_dy, r_dy, at_band(x, zh, target))

    def send_dy():
        arrived(in_part.at[pl.ds(0, n_plane - 1)], r_p)
        summed = in_part[0].astype(F32)
        for o in range(1, n_plane):
            summed = summed + in_part[o].astype(F32)
        coul16[pl.ds(x * coul_x + y * coul_y, coul_y), :] = summed.astype(BF16)
        for d in far_first(NY):
            start(dy_copy(y_peer(d), y))

    def dx_copy(target, owner):
        block = coul16.at[pl.ds(owner * coul_x, coul_x)]
        return remote(block, block, s_dx, r_dx, at_band(target, zh, y))

    def send_dx():
        arrived(coul16.at[pl.ds(x * coul_x, (NY - 1) * coul_y)], r_dy)
        for d in far_first(NX):
            start(dx_copy(x_peer(d), x))

    def wait_dense():
        arrived(coul16.at[pl.ds(0, (NX - 1) * coul_x)], r_dx)
        dense[...] = coul16[...].astype(F32)

    half = width // GROUPS
    block = per_owner * half

    def f_copy(g, s, target, slot):
        return remote(
            send_f.at[s, g, target], recv_f.at[s, g, slot],
            s_f.at[g, s], r_f.at[g, s], {"plane": target},
        )

    def wait_group(g, s, i):
        if g == 0:
            wait_gx(i, s)
        elif i == 0:
            wait_gx(2, s)

    def forward(g, s):
        both = wide[:n, :]
        first, second = slim[:n_packed, :], slim[n : n + n_packed, :]
        in_first = lax.broadcasted_iota(jnp.int32, (n_packed, n), 1) < labels[:n_packed, 2:3]
        group = 4

        for i in range(half // group):
            wait_group(g, s, i)
            at = slice(g * rows_g + i * group * n, g * rows_g + (i + 1) * group * n)
            pair = (orb[at, :] * shared[s, at, :].astype(F32)).astype(BF16)
            along = dot(pair, both).astype(BF16)
            for k in range(group):
                plane_k = along[k * n : (k + 1) * n]
                packed = jnp.where(in_first, dot(first, plane_k[:, :n]), dot(second, plane_k[:, n:]))
                grid_a[pl.ds(i * group + k, n_packed, stride=half), :] = packed
        for t in owners:
            send_f[s, g, t] = grid_a[pl.ds(pl.multiple_of(t * block, block), block), :].astype(BF16)
            start(f_copy(g, s, t, plane))
        at = pl.ds(pl.multiple_of(plane * block, block), block)
        recv_f[s, g, plane] = grid_a[at, :].astype(BF16)

    def b_copy(g, s, target, slot):
        return remote(
            send_b.at[s, g, target], recv_b.at[s, g, slot],
            s_b.at[g, s], r_b.at[g, s], {"plane": target},
        )

    def middle(s):
        for g in range(GROUPS):
            arrived(recv_f.at[s, g, pl.ds(0, n_plane - 1)], r_f.at[g, s])
        twin, cas = wide[n : 3 * n, :], slim[4 * n : 5 * n, :]
        for j in range(per_owner // 2):
            at = slice(j * 2 * half, (j + 1) * 2 * half)
            spectrum = dot(twin, recv_f[s, :, :, at, :].reshape(2 * n, n))
            back = []
            for h in range(2):
                coul = dense[pl.ds(2 * j + h, n, stride=width), :]
                scaled = (spectrum[h * n : (h + 1) * n] * coul).astype(BF16)
                back.append((dot(cas, scaled) * (1.0 / n)).reshape(n_plane, GROUPS, half, n))
            for g in range(GROUPS):
                for q in range(n_plane):
                    both = jnp.concatenate([back[0][q, g], back[1][q, g]], 0)
                    send_b[s, g, q, at, :] = both.astype(BF16)
        for g in range(GROUPS):
            for t in owners:
                start(b_copy(g, s, t, plane))
            recv_b[s, g, plane] = send_b[s, g, plane]

    def inverse(g, s):
        arrived(recv_b.at[s, g, pl.ds(0, n_plane - 1)], r_b.at[g, s])
        first, second = wide[3 * n :, :n], wide[3 * n :, n:]
        both = slim[2 * n : 4 * n, :]
        in_first = lax.broadcasted_iota(jnp.int32, (n, n), 1) < labels[:, 2:3]
        grid_b[: n_packed * half, :] = recv_b[s, g].reshape(n_packed * half, n).astype(F32)
        group = 4

        def step(i, _):
            for k in range(group):
                xi = i * group + k
                packed = grid_b[pl.ds(xi, n, stride=half), :]
                from_first = dot(first, jnp.where(in_first, packed, 0.0).astype(BF16))
                from_second = dot(second, jnp.where(in_first, 0.0, packed).astype(BF16))
                inverse_y = jnp.concatenate([from_first, from_second], 1) * (1.0 / n)
                at = pl.ds(pl.multiple_of(g * rows_g + xi * n, n), n)
                potential = dot(inverse_y.astype(BF16), both) * (1.0 / n)
                term = potential * shared[s, at, :].astype(F32)
                if s == 0:
                    total[at, :] = term
                else:
                    out_ref[at, :] = (total[at, :] + term).astype(BF16)
            return 0

        lax.fori_loop(0, half // group, step, 0)

    for p in range(3):
        send_x(p)
    add_part(0)
    add_part(1)
    send_y(0)
    send_y(1)
    for i in range(2, PIECES):
        add_part(i)
    send_z(0)
    send_y(2)
    send_z(1)
    send_part()
    send_gy(0)
    send_z(2)
    send_gy(1)
    loads[4].wait()
    loads[5].wait()
    wait_gy(0)
    send_gx(0, 0)
    send_gy(2)
    wait_gy(1)
    send_gx(1, 0)
    send_gx(0, 1)
    send_gx(1, 1)
    send_dy()
    forward(0, 0)
    wait_gy(2)
    send_gx(2, 0)
    send_gx(2, 1)
    forward(0, 1)
    send_dx()
    forward(1, 0)
    forward(1, 1)
    for p, (_, count) in enumerate(pieces):
        sent(in_x[p].at[pl.ds(0, NX - 1)], s_x.at[p])
        sent(in_y[p].at[pl.ds(0, NY - 1)], s_y.at[p])
        sent(in_z[p], s_z.at[p])
        sent(shared.at[:, pl.ds(0, (NY - 1) * (count // (NX * NY)))], s_gy.at[p])
        for s in range(STEPS):
            sent(shared.at[s, pl.ds(0, (NX - 1) * (count // NX))], s_gx.at[p, s])
    sent(in_part.at[pl.ds(0, n_plane - 1)], s_p)
    grid_b[n_packed * half :, :] = jnp.zeros(((n - n_packed) * half, n), F32)
    wait_dense()
    middle(0)
    sent(coul16.at[pl.ds(0, (NY - 1) * coul_y)], s_dy)
    sent(coul16.at[pl.ds(0, (NX - 1) * coul_x)], s_dx)
    middle(1)
    for g in range(GROUPS):
        for s in range(STEPS):
            sent(recv_f.at[s, g, pl.ds(0, n_plane - 1)], s_f.at[g, s])
    inverse(0, 0)
    inverse(1, 0)
    inverse(0, 1)
    inverse(1, 1)
    for g in range(GROUPS):
        for s in range(STEPS):
            sent(recv_b.at[s, g, pl.ds(0, n_plane - 1)], s_b.at[g, s])


def on_device(orbitals, coulomb, stick_lists, roots):
    _, width, n, _ = orbitals.shape
    n_plane = n // width
    rows = width * n
    rows_g = rows // GROUPS
    counts = [count for _, count in broadcast_pieces(rows)]
    coul_block = n // (NX * NY) * width
    per_owner = packing(n, n_plane)[1]
    wide, slim, labels = tables(n, n_plane)
    hbm = pl.BlockSpec(memory_space=pl.ANY)
    vmem = pl.BlockSpec(memory_space=pltpu.VMEM)
    dma = pltpu.SemaphoreType.DMA

    def pair_of_sems(*shape):
        return [dma(shape), dma(shape)]

    gs = (GROUPS, STEPS)
    spectra = pltpu.VMEM((STEPS, GROUPS, n_plane, per_owner * width // GROUPS, n), BF16)
    out = pl.pallas_call(
        functools.partial(kernel, n, n_plane),
        out_shape=jax.ShapeDtypeStruct((rows, n), BF16),
        in_specs=[pl.BlockSpec(memory_space=pltpu.SMEM)] + [hbm] * 6,
        out_specs=vmem,
        scratch_shapes=[
            pltpu.VMEM((rows, n), F32),
            pltpu.VMEM(wide.shape, BF16),
            pltpu.VMEM(slim.shape, BF16),
            pltpu.VMEM(labels.shape, jnp.int32),
            pltpu.VMEM((16, coulomb.shape[1]), BF16),
            pltpu.VMEM(stick_lists.shape, jnp.int32),
            pltpu.VMEM((rows, n), BF16),
            *[pltpu.VMEM((NX, count // NX, n), BF16) for count in counts],
            *[pltpu.VMEM((STEPS, count // NX, n), BF16) for count in counts],
            *[pltpu.VMEM((NY, STEPS, count // (NX * NY), n), BF16) for count in counts],
            *[pltpu.VMEM((STEPS, count // (NX * NY), n), BF16) for count in counts * 2],
            pltpu.VMEM((STEPS, rows, n), BF16),
            pltpu.VMEM((n // (NX * NY) * n, n), F32),
            pltpu.VMEM((n_plane, coul_block, n), BF16),
            pltpu.VMEM((n_plane, coul_block, n), BF16),
            pltpu.VMEM((rows, n), BF16),
            pltpu.VMEM((rows, n), F32),
            pltpu.VMEM((rows_g, n), F32),
            pltpu.VMEM((rows_g, n), F32),
            spectra, spectra, spectra, spectra,
            pltpu.VMEM((rows, n), F32),
            dma((6,)),
            *pair_of_sems(len(counts)),
            *pair_of_sems(len(counts)),
            *pair_of_sems(len(counts)),
            *pair_of_sems(len(counts)),
            *pair_of_sems(len(counts), STEPS),
            dma, dma, dma, dma, dma, dma,
            *pair_of_sems(*gs),
            *pair_of_sems(*gs),
        ],
        compiler_params=pltpu.CompilerParams(
            collective_id=0, has_side_effects=True, vmem_limit_bytes=57 * 1024 * 1024
        ),
        name="exchange",
    )(
        roots, orbitals.reshape(rows, n),
        wide, slim, labels, coulomb, stick_lists,
    )
    return out.reshape(1, width, n, n)


def solution(mesh):
    in_specs = (P("band", "plane", None, None), P(None, "plane"), P(), P())
    out_specs = P("band", "plane", None, None)
    return jax.shard_map(
        on_device, mesh=mesh, in_specs=in_specs, out_specs=out_specs, check_vma=False
    )
```

```python
import functools
import math

import jax
import jax.numpy as jnp
import numpy as np
from jax import lax
from jax.experimental import pallas as pl
from jax.experimental.pallas import tpu as pltpu
from jax.sharding import PartitionSpec as P

NX, NZ, NY = 4, 2, 8
STICKS = 12288
GROUPS = 2
STEPS = 2
PIECES = 3
MESH = pl.DeviceIdType.MESH
F32, BF16 = jnp.float32, jnp.bfloat16


def cas_table(n):
    k = np.arange(n)
    angles = 2.0 * math.pi / n * ((k[:, None] * k[None, :]) % n)
    return np.asarray(np.cos(angles) + np.sin(angles), np.float32)


def pair_table(n, width):
    cas = cas_table(n)
    half = width // GROUPS
    table = np.zeros((2, n, GROUPS, n // width, 2, half), np.float32)
    by_x = cas.reshape(n, n // width, GROUPS, half).transpose(0, 2, 1, 3)
    for h in range(2):
        table[h, :, :, :, h, :] = by_x
    return table.reshape(2 * n, 2 * n)


def packing(n, n_plane):
    signed = np.minimum(np.arange(n), n - np.arange(n))
    squares = signed[:, None] ** 2 + signed[None, :] ** 2
    kept = (squares <= np.sort(squares.reshape(-1))[STICKS - 1]).sum(1)
    best = None
    for t in range(1, n // 2 + 1):
        for extra in ([], [n - t + 1]):
            second = [h for h in range(n) if kept[h] and (signed[h] >= t or h in extra)]
            firsts = [h for h in range(n) if kept[h] and h not in second]
            free, mate = sorted(firsts, key=lambda h: -kept[h]), {}
            for h in sorted(second, key=lambda h: -kept[h]):
                host = next((f for f in free if kept[f] + kept[h] <= n), None)
                if host is None:
                    break
                free.remove(host)
                mate[host] = h
            else:
                if best is None or len(firsts) < len(best[0]):
                    best = firsts, mate, t, extra
    firsts, mate, t, extra = best
    per_owner = -(-len(firsts) // (2 * n_plane)) * 2
    table = -np.ones((per_owner * n_plane, 3), np.int64)
    for row, h in enumerate(firsts):
        table[row] = h, mate.get(h, -1), kept[h]
    return table, per_owner, t, (extra or [-1])[0]


def tables(n, n_plane):
    width = n // n_plane
    cas = cas_table(n)
    rows, per_owner, _, _ = packing(n, n_plane)
    order = sorted(range(n), key=lambda g: (min(g, n - g), g > n // 2))
    both = np.concatenate([cas[:, order], cas[:, order[::-1]]], 1)
    first, second = np.zeros((n, n), np.float32), np.zeros((n, n), np.float32)
    for row, (h, other, _) in enumerate(rows):
        if h >= 0:
            first[row] = cas[h]
        if other >= 0:
            second[row] = cas[other]
    wide = np.concatenate([both, pair_table(n, width), np.concatenate([first.T, second.T], 1) / n], 0)
    slim = np.concatenate([first, second, both.T / n, cas / n], 0)
    labels = np.full((n, 128), -7, np.int32)
    for row, (h, other, length) in enumerate(rows):
        place = row // per_owner * width + row % per_owner
        labels[place, 0] = h if h >= 0 else -7
        labels[place, 1] = other if other >= 0 else -7
    labels[:, 2] = n
    labels[: len(rows), 2] = np.where(rows[:, 2] < 0, n, rows[:, 2])
    return jnp.asarray(wide).astype(BF16), jnp.asarray(slim).astype(BF16), jnp.asarray(labels)


def dot(a, b):
    return jnp.dot(a, b, preferred_element_type=F32)


def broadcast_pieces(rows):
    return [(0, rows // 4), (rows // 4, rows // 4), (rows // 2, rows // 2)]


def far_first(count):
    return sorted(range(1, count), key=lambda d: -min(d, count - d))


def pick(index, values):
    out = values[0]
    for k in range(1, len(values)):
        out = jnp.where(index == k, values[k], out)
    return out


def remote(src, dst, send_sem, recv_sem, device):
    return pltpu.make_async_remote_copy(
        src_ref=src, dst_ref=dst, send_sem=send_sem, recv_sem=recv_sem,
        device_id=device, device_id_type=MESH,
    )


def kernel(
    n, n_plane,
    roots_ref, orb_hbm, wide_hbm, slim_hbm, labels_hbm, coulomb_hbm, ids_hbm, out_ref,
    orb, wide, slim, labels, coulomb, ids_ref,
    orb16, in_x0, in_x1, in_x2, sel0, sel1, sel2, in_y0, in_y1, in_y2,
    cand0, cand1, cand2, in_z0, in_z1, in_z2, shared,
    flat_sum, part, in_part, coul16, dense, grid_a, grid_b, send_f, recv_f, send_b, recv_b, total,
    s_in, s_x, r_x, s_y, r_y, s_z, r_z, s_gy, r_gy, s_gx, r_gx,
    s_p, r_p, s_dy, r_dy, s_dx, r_dx, s_f, r_f, s_b, r_b,
):
    width = n // n_plane
    rows = width * n
    rows_g = rows // GROUPS
    _, per_owner, edge, edge_row = packing(n, n_plane)
    n_packed = per_owner * n_plane
    in_x, sel, in_y = [in_x0, in_x1, in_x2], [sel0, sel1, sel2], [in_y0, in_y1, in_y2]
    cand, in_z = [cand0, cand1, cand2], [in_z0, in_z1, in_z2]
    pieces = broadcast_pieces(rows)
    band, plane = lax.axis_index("band"), lax.axis_index("plane")
    y = lax.rem(band, NY)
    zh = lax.rem(band // NY, NZ)
    x = band // (NY * NZ)

    def at_band(bx, bz, by):
        return {"band": (bx * NZ + bz) * NY + by}

    def x_peer(d):
        return lax.rem(x + d, NX)

    def y_peer(d):
        return lax.rem(y + d, NY)

    def p_peer(d):
        return lax.rem(plane + d, n_plane)

    bits = [lax.rem(plane // (1 << k), 2) for k in range(n_plane.bit_length() - 1)]
    owners = []
    for flip in sorted(range(1, n_plane), key=lambda f: (-(f >> 1), f)):
        t = 0
        for k, bit in enumerate(bits):
            t = t + (1 << k) * (1 - bit if flip >> k & 1 else bit)
        owners.append(t)

    barrier = pltpu.get_barrier_semaphore()
    peers = [at_band(x_peer(d), zh, y) for d in far_first(NX)]
    peers += [at_band(x, zh, y_peer(d)) for d in far_first(NY)]
    peers += [at_band(x, lax.rem(zh + d, NZ), y) for d in range(1, NZ)]
    peers += [{"plane": p_peer(d)} for d in range(1, n_plane)]
    for peer in peers:
        pl.semaphore_signal(barrier, inc=1, device_id=peer, device_id_type=MESH)

    coul_rows = n // (NX * NY)
    first_row = (x * NY + y) * coul_rows
    coul_tile = pl.multiple_of(first_row // 16 * 16, 16)
    loads = [
        pltpu.make_async_copy(orb_hbm, orb, s_in.at[0]),
        pltpu.make_async_copy(coulomb_hbm.at[pl.ds(coul_tile, 16)], coulomb, s_in.at[1]),
        pltpu.make_async_copy(ids_hbm, ids_ref, s_in.at[2]),
        pltpu.make_async_copy(labels_hbm, labels, s_in.at[3]),
        pltpu.make_async_copy(slim_hbm, slim, s_in.at[4]),
        pltpu.make_async_copy(wide_hbm, wide, s_in.at[5]),
    ]
    for load in loads:
        load.start()
    loads[0].wait()
    orb16[...] = orb[...].astype(BF16)
    pl.semaphore_wait(barrier, len(peers))

    def start(copy):
        copy.start()

    def arrived(region, sem):
        remote(region, region, sem, sem, {"plane": p_peer(1)}).wait_recv()

    def sent(region, sem):
        remote(region, region, sem, sem, {"plane": p_peer(1)}).wait_send()

    def x_copy(p, target, slot):
        first, count = pieces[p]
        chunk = count // NX
        return remote(
            orb16.at[pl.ds(first + target * chunk, chunk)], in_x[p].at[slot],
            s_x.at[p], r_x.at[p], at_band(target, zh, y),
        )

    def send_x(p):
        for d in far_first(NX):
            start(x_copy(p, x_peer(d), x))
        first, count = pieces[p]
        chunk = count // NX
        in_x[p][x] = orb16[pl.ds(first + x * chunk, chunk), :]

    root = [roots_ref[s] for s in range(STEPS)]
    root_y = [lax.rem(r, NY) for r in root]
    root_z = [lax.rem(r // NY, NZ) for r in root]
    root_x = [r // (NY * NZ) for r in root]

    def send_y(p):
        arrived(in_x[p].at[pl.ds(0, NX - 1)], r_x.at[p])
        for s in range(STEPS):
            sel[p][s] = pick(root_x[s], [in_x[p][k] for k in range(NX)])
        chunk = pieces[p][1] // (NX * NY)
        for d in far_first(NY):
            t = y_peer(d)
            start(remote(
                sel[p].at[:, pl.ds(t * chunk, chunk)], in_y[p].at[y],
                s_y.at[p], r_y.at[p], at_band(x, zh, t),
            ))
        in_y[p][y] = sel[p][:, pl.ds(y * chunk, chunk), :]

    def z_copy(p):
        return remote(
            cand[p], in_z[p], s_z.at[p], r_z.at[p], at_band(x, lax.rem(zh + 1, NZ), y)
        )

    def send_z(p):
        arrived(in_y[p].at[pl.ds(0, NY - 1)], r_y.at[p])
        for s in range(STEPS):
            cand[p][s] = pick(root_y[s], [in_y[p][k, s] for k in range(NY)])
        start(z_copy(p))

    def send_gy(p):
        z_copy(p).wait_recv()
        first, count = pieces[p]
        chunk = count // (NX * NY)
        at = pl.ds(first + (x * NY + y) * chunk, chunk)
        for s in range(STEPS):
            shared[s, at, :] = jnp.where(root_z[s] == zh, cand[p][s], in_z[p][s])
        block = shared.at[:, at]
        for d in far_first(NY):
            start(remote(block, block, s_gy.at[p], r_gy.at[p], at_band(x, zh, y_peer(d))))

    def wait_gy(p):
        first, count = pieces[p]
        chunk = count // (NX * NY)
        arrived(shared.at[:, pl.ds(first + x * NY * chunk, (NY - 1) * chunk)], r_gy.at[p])

    def send_gx(p, s):
        first, count = pieces[p]
        block = shared.at[s, pl.ds(first + x * (count // NX), count // NX)]
        for d in far_first(NX):
            start(remote(block, block, s_gx.at[p, s], r_gx.at[p, s], at_band(x_peer(d), zh, y)))

    def wait_gx(p, s):
        first, count = pieces[p]
        arrived(shared.at[s, pl.ds(first, count // NX * (NX - 1))], r_gx.at[p, s])

    def p_copy(target, slot):
        return remote(part.at[target], in_part.at[slot], s_p, r_p, {"plane": target})

    slots = ids_ref.shape[1]
    piece = -(-slots // (128 * PIECES)) * 128

    def add_part(i):
        if i == 0:
            loads[1].wait()
            loads[2].wait()
            loads[3].wait()
        at = slice(i * piece, min((i + 1) * piece, slots))
        ids = ids_ref[pl.ds(plane, 1), at]
        valid = ids >= 0
        id_h = jnp.where(valid, ids // n, -1)
        id_g = jnp.where(valid, lax.rem(ids, n), 0)
        lane = jnp.where(id_g == 0, 0, jnp.where(id_g <= n // 2, 2 * id_g - 1, 2 * (n - id_g)))
        reverse = (jnp.minimum(id_h, n - id_h) >= edge) | (id_h == edge_row)
        lane = jnp.where(reverse, n - 1 - lane, lane)
        iota = lax.broadcasted_iota(jnp.int32, (n, ids.shape[1]), 0)
        hot_h = (labels[:, 0:1] == id_h) | (labels[:, 1:2] == id_h)
        hot_g = jnp.where(iota == lane, 1.0, 0.0).astype(BF16)
        tile = coulomb[:, at].astype(F32)
        own = tile[:coul_rows]
        for k in range(1, 16 // coul_rows):
            inside = first_row - coul_tile == k * coul_rows
            own = jnp.where(inside, tile[k * coul_rows : (k + 1) * coul_rows], own)
        left = jnp.concatenate(
            [jnp.where(hot_h, own[k : k + 1], 0.0).astype(BF16) for k in range(coul_rows)], 0
        )
        flat = lax.dot_general(
            left, hot_g, (((1,), (1,)), ((), ())), preferred_element_type=F32
        )
        flat_sum[...] = flat if i == 0 else flat_sum[...] + flat

    def send_part():
        for k in range(coul_rows):
            for o in range(n_plane):
                at = slice(k * n + o * width, k * n + (o + 1) * width)
                part[o, k * width : (k + 1) * width, :] = flat_sum[at, :].astype(BF16)
        for t in owners:
            start(p_copy(t, plane))
        in_part[plane] = part[plane]

    coul_x, coul_y = rows // NX, rows // (NX * NY)

    def dy_copy(target, owner):
        block = coul16.at[pl.ds(x * coul_x + owner * coul_y, coul_y)]
        return remote(block, block, s_dy, r_dy, at_band(x, zh, target))

    def send_dy():
        arrived(in_part.at[pl.ds(0, n_plane - 1)], r_p)
        summed = in_part[0].astype(F32)
        for o in range(1, n_plane):
            summed = summed + in_part[o].astype(F32)
        coul16[pl.ds(x * coul_x + y * coul_y, coul_y), :] = summed.astype(BF16)
        for d in far_first(NY):
            start(dy_copy(y_peer(d), y))

    def dx_copy(target, owner):
        block = coul16.at[pl.ds(owner * coul_x, coul_x)]
        return remote(block, block, s_dx, r_dx, at_band(target, zh, y))

    def send_dx():
        arrived(coul16.at[pl.ds(x * coul_x, (NY - 1) * coul_y)], r_dy)
        for d in far_first(NX):
            start(dx_copy(x_peer(d), x))

    def wait_dense():
        arrived(coul16.at[pl.ds(0, (NX - 1) * coul_x)], r_dx)
        dense[...] = coul16[...].astype(F32)

    half = width // GROUPS
    block = per_owner * half

    def f_copy(g, s, target, slot):
        return remote(
            send_f.at[s, g, target], recv_f.at[s, g, slot],
            s_f.at[g, s], r_f.at[g, s], {"plane": target},
        )

    def wait_group(g, s, i):
        if g == 0:
            wait_gx(i, s)
        elif i == 0:
            wait_gx(2, s)

    def forward(g, s):
        both = wide[:n, :]
        first, second = slim[:n_packed, :], slim[n : n + n_packed, :]
        in_first = lax.broadcasted_iota(jnp.int32, (n_packed, n), 1) < labels[:n_packed, 2:3]
        group = 4

        for i in range(half // group):
            wait_group(g, s, i)
            at = slice(g * rows_g + i * group * n, g * rows_g + (i + 1) * group * n)
            pair = (orb[at, :] * shared[s, at, :].astype(F32)).astype(BF16)
            along = dot(pair, both).astype(BF16)
            planes = [along[k * n : (k + 1) * n] for k in range(group)]
            from_first = dot(first, jnp.concatenate([plane_k[:, :n] for plane_k in planes], 1))
            from_second = dot(second, jnp.concatenate([plane_k[:, n:] for plane_k in planes], 1))
            for k in range(group):
                at = slice(k * n, (k + 1) * n)
                packed = jnp.where(in_first, from_first[:, at], from_second[:, at])
                grid_a[pl.ds(i * group + k, n_packed, stride=half), :] = packed
        for t in owners:
            send_f[s, g, t] = grid_a[pl.ds(pl.multiple_of(t * block, block), block), :].astype(BF16)
            start(f_copy(g, s, t, plane))
        at = pl.ds(pl.multiple_of(plane * block, block), block)
        recv_f[s, g, plane] = grid_a[at, :].astype(BF16)

    def b_copy(g, s, target, slot):
        return remote(
            send_b.at[s, g, target], recv_b.at[s, g, slot],
            s_b.at[g, s], r_b.at[g, s], {"plane": target},
        )

    def middle(s):
        for g in range(GROUPS):
            arrived(recv_f.at[s, g, pl.ds(0, n_plane - 1)], r_f.at[g, s])
        twin, cas = wide[n : 3 * n, :], slim[4 * n : 5 * n, :]
        pairs = per_owner // 2
        for first_pair in range(0, pairs, 2):
            js = range(first_pair, min(first_pair + 2, pairs))
            at = [slice(j * 2 * half, (j + 1) * 2 * half) for j in js]
            sticks = [recv_f[s, :, :, a, :].reshape(2 * n, n) for a in at]
            spectrum = dot(twin, jnp.concatenate(sticks, 1))
            scaled = []
            for k, j in enumerate(js):
                for h in range(2):
                    coul = dense[pl.ds(2 * j + h, n, stride=width), :]
                    part_h = spectrum[h * n : (h + 1) * n, k * n : (k + 1) * n]
                    scaled.append((part_h * coul).astype(BF16))
            back = dot(cas, jnp.concatenate(scaled, 1))
            for k in range(len(js)):
                two = [
                    back[:, (2 * k + h) * n : (2 * k + h + 1) * n].reshape(n_plane, GROUPS, half, n)
                    for h in range(2)
                ]
                for g in range(GROUPS):
                    for q in range(n_plane):
                        both = jnp.concatenate([two[0][q, g], two[1][q, g]], 0)
                        send_b[s, g, q, at[k], :] = both.astype(BF16)
        for g in range(GROUPS):
            for t in owners:
                start(b_copy(g, s, t, plane))
            recv_b[s, g, plane] = send_b[s, g, plane]

    def inverse(g, s):
        arrived(recv_b.at[s, g, pl.ds(0, n_plane - 1)], r_b.at[g, s])
        first, second = wide[3 * n :, :n], wide[3 * n :, n:]
        both = slim[2 * n : 4 * n, :]
        in_first = lax.broadcasted_iota(jnp.int32, (n, n), 1) < labels[:, 2:3]
        grid_b[: n_packed * half, :] = recv_b[s, g].reshape(n_packed * half, n).astype(F32)
        group = 4

        for i in range(half // group):
            packed = [grid_b[pl.ds(i * group + k, n, stride=half), :] for k in range(group)]
            own = [jnp.where(in_first, one, 0.0).astype(BF16) for one in packed]
            other = [jnp.where(in_first, 0.0, one).astype(BF16) for one in packed]
            from_first = dot(first, jnp.concatenate(own, 1))
            from_second = dot(second, jnp.concatenate(other, 1))
            inverse_y = []
            for k in range(group):
                at = slice(k * n, (k + 1) * n)
                inverse_y.append(jnp.concatenate([from_first[:, at], from_second[:, at]], 1).astype(BF16))
            at = slice(g * rows_g + i * group * n, g * rows_g + (i + 1) * group * n)
            term = dot(jnp.concatenate(inverse_y, 0), both) * shared[s, at, :].astype(F32)
            if s == 0:
                total[at, :] = term
            else:
                out_ref[at, :] = (total[at, :] + term).astype(BF16)

    for p in range(3):
        send_x(p)
    add_part(0)
    add_part(1)
    send_y(0)
    send_y(1)
    for i in range(2, PIECES):
        add_part(i)
    send_z(0)
    send_y(2)
    send_z(1)
    send_part()
    send_gy(0)
    send_z(2)
    send_gy(1)
    loads[4].wait()
    loads[5].wait()
    wait_gy(0)
    send_gx(0, 0)
    send_gy(2)
    wait_gy(1)
    send_gx(1, 0)
    send_gx(0, 1)
    send_gx(1, 1)
    send_dy()
    forward(0, 0)
    wait_gy(2)
    send_gx(2, 0)
    send_gx(2, 1)
    forward(0, 1)
    send_dx()
    forward(1, 0)
    forward(1, 1)
    for p, (_, count) in enumerate(pieces):
        sent(in_x[p].at[pl.ds(0, NX - 1)], s_x.at[p])
        sent(in_y[p].at[pl.ds(0, NY - 1)], s_y.at[p])
        sent(in_z[p], s_z.at[p])
        sent(shared.at[:, pl.ds(0, (NY - 1) * (count // (NX * NY)))], s_gy.at[p])
        for s in range(STEPS):
            sent(shared.at[s, pl.ds(0, (NX - 1) * (count // NX))], s_gx.at[p, s])
    sent(in_part.at[pl.ds(0, n_plane - 1)], s_p)
    grid_b[n_packed * half :, :] = jnp.zeros(((n - n_packed) * half, n), F32)
    wait_dense()
    middle(0)
    sent(coul16.at[pl.ds(0, (NY - 1) * coul_y)], s_dy)
    sent(coul16.at[pl.ds(0, (NX - 1) * coul_x)], s_dx)
    middle(1)
    for g in range(GROUPS):
        for s in range(STEPS):
            sent(recv_f.at[s, g, pl.ds(0, n_plane - 1)], s_f.at[g, s])
    inverse(0, 0)
    inverse(1, 0)
    inverse(0, 1)
    inverse(1, 1)
    for g in range(GROUPS):
        for s in range(STEPS):
            sent(recv_b.at[s, g, pl.ds(0, n_plane - 1)], s_b.at[g, s])


def on_device(orbitals, coulomb, stick_lists, roots):
    _, width, n, _ = orbitals.shape
    n_plane = n // width
    rows = width * n
    rows_g = rows // GROUPS
    counts = [count for _, count in broadcast_pieces(rows)]
    coul_block = n // (NX * NY) * width
    per_owner = packing(n, n_plane)[1]
    wide, slim, labels = tables(n, n_plane)
    hbm = pl.BlockSpec(memory_space=pl.ANY)
    vmem = pl.BlockSpec(memory_space=pltpu.VMEM)
    dma = pltpu.SemaphoreType.DMA

    def pair_of_sems(*shape):
        return [dma(shape), dma(shape)]

    gs = (GROUPS, STEPS)
    spectra = pltpu.VMEM((STEPS, GROUPS, n_plane, per_owner * width // GROUPS, n), BF16)
    out = pl.pallas_call(
        functools.partial(kernel, n, n_plane),
        out_shape=jax.ShapeDtypeStruct((rows, n), BF16),
        in_specs=[pl.BlockSpec(memory_space=pltpu.SMEM)] + [hbm] * 6,
        out_specs=vmem,
        scratch_shapes=[
            pltpu.VMEM((rows, n), F32),
            pltpu.VMEM(wide.shape, BF16),
            pltpu.VMEM(slim.shape, BF16),
            pltpu.VMEM(labels.shape, jnp.int32),
            pltpu.VMEM((16, coulomb.shape[1]), BF16),
            pltpu.VMEM(stick_lists.shape, jnp.int32),
            pltpu.VMEM((rows, n), BF16),
            *[pltpu.VMEM((NX, count // NX, n), BF16) for count in counts],
            *[pltpu.VMEM((STEPS, count // NX, n), BF16) for count in counts],
            *[pltpu.VMEM((NY, STEPS, count // (NX * NY), n), BF16) for count in counts],
            *[pltpu.VMEM((STEPS, count // (NX * NY), n), BF16) for count in counts * 2],
            pltpu.VMEM((STEPS, rows, n), BF16),
            pltpu.VMEM((n // (NX * NY) * n, n), F32),
            pltpu.VMEM((n_plane, coul_block, n), BF16),
            pltpu.VMEM((n_plane, coul_block, n), BF16),
            pltpu.VMEM((rows, n), BF16),
            pltpu.VMEM((rows, n), F32),
            pltpu.VMEM((rows_g, n), F32),
            pltpu.VMEM((rows_g, n), F32),
            spectra, spectra, spectra, spectra,
            pltpu.VMEM((rows, n), F32),
            dma((6,)),
            *pair_of_sems(len(counts)),
            *pair_of_sems(len(counts)),
            *pair_of_sems(len(counts)),
            *pair_of_sems(len(counts)),
            *pair_of_sems(len(counts), STEPS),
            dma, dma, dma, dma, dma, dma,
            *pair_of_sems(*gs),
            *pair_of_sems(*gs),
        ],
        compiler_params=pltpu.CompilerParams(
            collective_id=0, has_side_effects=True, vmem_limit_bytes=57 * 1024 * 1024
        ),
        name="exchange",
    )(
        roots, orbitals.reshape(rows, n),
        wide, slim, labels, coulomb, stick_lists,
    )
    return out.reshape(1, width, n, n)


def solution(mesh):
    in_specs = (P("band", "plane", None, None), P(None, "plane"), P(), P())
    out_specs = P("band", "plane", None, None)
    return jax.shard_map(
        on_device, mesh=mesh, in_specs=in_specs, out_specs=out_specs, check_vma=False
    )
```

```python
import functools
import math

import jax
import jax.numpy as jnp
import numpy as np
from jax import lax
from jax.experimental import pallas as pl
from jax.experimental.pallas import tpu as pltpu
from jax.sharding import PartitionSpec as P

NX, NZ, NY = 4, 2, 8
STICKS = 12288
GROUPS = 2
STEPS = 2
PIECES = 3
MESH = pl.DeviceIdType.MESH
F32, BF16 = jnp.float32, jnp.bfloat16


def cas_table(n):
    k = np.arange(n)
    angles = 2.0 * math.pi / n * ((k[:, None] * k[None, :]) % n)
    return np.asarray(np.cos(angles) + np.sin(angles), np.float32)


def pair_table(n, width):
    cas = cas_table(n)
    half = width // GROUPS
    table = np.zeros((2, n, GROUPS, n // width, 2, half), np.float32)
    by_x = cas.reshape(n, n // width, GROUPS, half).transpose(0, 2, 1, 3)
    for h in range(2):
        table[h, :, :, :, h, :] = by_x
    return table.reshape(2 * n, 2 * n)


def packing(n, n_plane):
    signed = np.minimum(np.arange(n), n - np.arange(n))
    squares = signed[:, None] ** 2 + signed[None, :] ** 2
    kept = (squares <= np.sort(squares.reshape(-1))[STICKS - 1]).sum(1)
    best = None
    for t in range(1, n // 2 + 1):
        for extra in ([], [n - t + 1]):
            second = [h for h in range(n) if kept[h] and (signed[h] >= t or h in extra)]
            firsts = [h for h in range(n) if kept[h] and h not in second]
            free, mate = sorted(firsts, key=lambda h: -kept[h]), {}
            for h in sorted(second, key=lambda h: -kept[h]):
                host = next((f for f in free if kept[f] + kept[h] <= n), None)
                if host is None:
                    break
                free.remove(host)
                mate[host] = h
            else:
                if best is None or len(firsts) < len(best[0]):
                    best = firsts, mate, t, extra
    firsts, mate, t, extra = best
    pairs = -(-len(firsts) // 2)
    per_owner = -(-pairs // n_plane) * 2
    n_small = per_owner // 2 * n_plane - pairs
    period = n_plane // n_small if n_small and n_plane % n_small == 0 else 0
    table = -np.ones((per_owner * n_plane, 3), np.int64)
    left = list(firsts)
    for owner in range(n_plane):
        count = per_owner - 2 if period and owner % period == period - 1 else per_owner
        for k in range(min(count, len(left))):
            h = left.pop(0)
            table[owner * per_owner + k] = h, mate.get(h, -1), kept[h]
    return table, per_owner, period, t, (extra or [-1])[0]


def tables(n, n_plane):
    width = n // n_plane
    cas = cas_table(n)
    rows, per_owner = packing(n, n_plane)[:2]
    order = sorted(range(n), key=lambda g: (min(g, n - g), g > n // 2))
    both = np.concatenate([cas[:, order], cas[:, order[::-1]]], 1)
    first, second = np.zeros((n, n), np.float32), np.zeros((n, n), np.float32)
    for row, (h, other, _) in enumerate(rows):
        if h >= 0:
            first[row] = cas[h]
        if other >= 0:
            second[row] = cas[other]
    wide = np.concatenate([both, pair_table(n, width), np.concatenate([first.T, second.T], 1) / n], 0)
    slim = np.concatenate([first, second, both.T / n, cas / n], 0)
    labels = np.full((n, 128), -7, np.int32)
    for row, (h, other, length) in enumerate(rows):
        place = row // per_owner * width + row % per_owner
        labels[place, 0] = h if h >= 0 else -7
        labels[place, 1] = other if other >= 0 else -7
    labels[:, 2] = n
    labels[: len(rows), 2] = np.where(rows[:, 2] < 0, n, rows[:, 2])
    return jnp.asarray(wide).astype(BF16), jnp.asarray(slim).astype(BF16), jnp.asarray(labels)


def dot(a, b):
    return jnp.dot(a, b, preferred_element_type=F32)


def broadcast_pieces(rows):
    return [(0, rows // 4), (rows // 4, rows // 4), (rows // 2, rows // 2)]


def far_first(count):
    return sorted(range(1, count), key=lambda d: -min(d, count - d))


def pick(index, values):
    out = values[0]
    for k in range(1, len(values)):
        out = jnp.where(index == k, values[k], out)
    return out


def remote(src, dst, send_sem, recv_sem, device):
    return pltpu.make_async_remote_copy(
        src_ref=src, dst_ref=dst, send_sem=send_sem, recv_sem=recv_sem,
        device_id=device, device_id_type=MESH,
    )


def kernel(
    n, n_plane,
    roots_ref, orb_hbm, wide_hbm, slim_hbm, labels_hbm, coulomb_hbm, ids_hbm, out_ref,
    orb, wide, slim, labels, coulomb, ids_ref,
    orb16, in_x0, in_x1, in_x2, sel0, sel1, sel2, in_y0, in_y1, in_y2,
    cand0, cand1, cand2, in_z0, in_z1, in_z2, shared,
    flat_sum, part, in_part, coul16, dense, grid_a, grid_b, send_f, recv_f, send_b, recv_b, total,
    s_orb, s_in, s_x, r_x, s_y, r_y, s_z, r_z, s_gy, r_gy, s_gx, r_gx,
    s_p, r_p, s_dy, r_dy, s_dx, r_dx, s_f, r_f, s_b, r_b,
):
    width = n // n_plane
    rows = width * n
    rows_g = rows // GROUPS
    _, per_owner, period, edge, edge_row = packing(n, n_plane)
    n_packed = per_owner * n_plane
    in_x, sel, in_y = [in_x0, in_x1, in_x2], [sel0, sel1, sel2], [in_y0, in_y1, in_y2]
    cand, in_z = [cand0, cand1, cand2], [in_z0, in_z1, in_z2]
    pieces = broadcast_pieces(rows)
    band, plane = lax.axis_index("band"), lax.axis_index("plane")
    y = lax.rem(band, NY)
    zh = lax.rem(band // NY, NZ)
    x = band // (NY * NZ)

    def at_band(bx, bz, by):
        return {"band": (bx * NZ + bz) * NY + by}

    def x_peer(d):
        return lax.rem(x + d, NX)

    def y_peer(d):
        return lax.rem(y + d, NY)

    def p_peer(d):
        return lax.rem(plane + d, n_plane)

    bits = [lax.rem(plane // (1 << k), 2) for k in range(n_plane.bit_length() - 1)]
    owners = []
    for flip in sorted(range(1, n_plane), key=lambda f: (-(f >> 1), f)):
        t = 0
        for k, bit in enumerate(bits):
            t = t + (1 << k) * (1 - bit if flip >> k & 1 else bit)
        owners.append(t)

    barrier = pltpu.get_barrier_semaphore()
    peers = [at_band(x_peer(d), zh, y) for d in far_first(NX)]
    peers += [at_band(x, zh, y_peer(d)) for d in far_first(NY)]
    peers += [at_band(x, lax.rem(zh + d, NZ), y) for d in range(1, NZ)]
    peers += [{"plane": p_peer(d)} for d in range(1, n_plane)]
    for peer in peers:
        pl.semaphore_signal(barrier, inc=1, device_id=peer, device_id_type=MESH)

    coul_rows = n // (NX * NY)
    first_row = (x * NY + y) * coul_rows
    coul_tile = pl.multiple_of(first_row // 16 * 16, 16)
    orb_loads = [
        pltpu.make_async_copy(orb_hbm.at[pl.ds(*at)], orb.at[pl.ds(*at)], s_orb.at[p])
        for p, at in enumerate(pieces)
    ]
    loads = [
        pltpu.make_async_copy(coulomb_hbm.at[pl.ds(coul_tile, 16)], coulomb, s_in.at[0]),
        pltpu.make_async_copy(ids_hbm, ids_ref, s_in.at[1]),
        pltpu.make_async_copy(labels_hbm, labels, s_in.at[2]),
        pltpu.make_async_copy(slim_hbm, slim, s_in.at[3]),
        pltpu.make_async_copy(wide_hbm, wide, s_in.at[4]),
    ]
    for load in orb_loads + loads:
        load.start()

    def round_piece(p):
        first, count = pieces[p]
        orb_loads[p].wait()
        orb16[first : first + count, :] = orb[first : first + count, :].astype(BF16)

    round_piece(0)
    pl.semaphore_wait(barrier, len(peers))

    def start(copy):
        copy.start()

    def arrived(region, sem):
        remote(region, region, sem, sem, {"plane": p_peer(1)}).wait_recv()

    def sent(region, sem):
        remote(region, region, sem, sem, {"plane": p_peer(1)}).wait_send()

    def x_copy(p, target, slot):
        first, count = pieces[p]
        chunk = count // NX
        return remote(
            orb16.at[pl.ds(first + target * chunk, chunk)], in_x[p].at[slot],
            s_x.at[p], r_x.at[p], at_band(target, zh, y),
        )

    def send_x(p):
        for d in far_first(NX):
            start(x_copy(p, x_peer(d), x))
        first, count = pieces[p]
        chunk = count // NX
        in_x[p][x] = orb16[pl.ds(first + x * chunk, chunk), :]

    root = [roots_ref[s] for s in range(STEPS)]
    root_y = [lax.rem(r, NY) for r in root]
    root_z = [lax.rem(r // NY, NZ) for r in root]
    root_x = [r // (NY * NZ) for r in root]

    def send_y(p):
        arrived(in_x[p].at[pl.ds(0, NX - 1)], r_x.at[p])
        for s in range(STEPS):
            sel[p][s] = pick(root_x[s], [in_x[p][k] for k in range(NX)])
        chunk = pieces[p][1] // (NX * NY)
        for d in far_first(NY):
            t = y_peer(d)
            start(remote(
                sel[p].at[:, pl.ds(t * chunk, chunk)], in_y[p].at[y],
                s_y.at[p], r_y.at[p], at_band(x, zh, t),
            ))
        in_y[p][y] = sel[p][:, pl.ds(y * chunk, chunk), :]

    def z_copy(p):
        return remote(
            cand[p], in_z[p], s_z.at[p], r_z.at[p], at_band(x, lax.rem(zh + 1, NZ), y)
        )

    def send_z(p):
        arrived(in_y[p].at[pl.ds(0, NY - 1)], r_y.at[p])
        for s in range(STEPS):
            cand[p][s] = pick(root_y[s], [in_y[p][k, s] for k in range(NY)])
        start(z_copy(p))

    def send_gy(p):
        z_copy(p).wait_recv()
        first, count = pieces[p]
        chunk = count // (NX * NY)
        at = pl.ds(first + (x * NY + y) * chunk, chunk)
        for s in range(STEPS):
            shared[s, at, :] = jnp.where(root_z[s] == zh, cand[p][s], in_z[p][s])
        block = shared.at[:, at]
        for d in far_first(NY):
            start(remote(block, block, s_gy.at[p], r_gy.at[p], at_band(x, zh, y_peer(d))))

    def wait_gy(p):
        first, count = pieces[p]
        chunk = count // (NX * NY)
        arrived(shared.at[:, pl.ds(first + x * NY * chunk, (NY - 1) * chunk)], r_gy.at[p])

    def send_gx(p, s):
        first, count = pieces[p]
        block = shared.at[s, pl.ds(first + x * (count // NX), count // NX)]
        for d in far_first(NX):
            start(remote(block, block, s_gx.at[p, s], r_gx.at[p, s], at_band(x_peer(d), zh, y)))

    def wait_gx(p, s):
        first, count = pieces[p]
        arrived(shared.at[s, pl.ds(first, count // NX * (NX - 1))], r_gx.at[p, s])

    def p_copy(target, slot):
        return remote(part.at[target], in_part.at[slot], s_p, r_p, {"plane": target})

    slots = ids_ref.shape[1]
    piece = -(-slots // (128 * PIECES)) * 128

    def add_part(i):
        if i == 0:
            loads[0].wait()
            loads[1].wait()
            loads[2].wait()
        at = slice(i * piece, min((i + 1) * piece, slots))
        ids = ids_ref[pl.ds(plane, 1), at]
        valid = ids >= 0
        id_h = jnp.where(valid, ids // n, -1)
        id_g = jnp.where(valid, lax.rem(ids, n), 0)
        lane = jnp.where(id_g == 0, 0, jnp.where(id_g <= n // 2, 2 * id_g - 1, 2 * (n - id_g)))
        reverse = (jnp.minimum(id_h, n - id_h) >= edge) | (id_h == edge_row)
        lane = jnp.where(reverse, n - 1 - lane, lane)
        iota = lax.broadcasted_iota(jnp.int32, (n, ids.shape[1]), 0)
        hot_h = (labels[:, 0:1] == id_h) | (labels[:, 1:2] == id_h)
        hot_g = jnp.where(iota == lane, 1.0, 0.0).astype(BF16)
        tile = coulomb[:, at].astype(F32)
        own = tile[:coul_rows]
        for k in range(1, 16 // coul_rows):
            inside = first_row - coul_tile == k * coul_rows
            own = jnp.where(inside, tile[k * coul_rows : (k + 1) * coul_rows], own)
        left = jnp.concatenate(
            [jnp.where(hot_h, own[k : k + 1], 0.0).astype(BF16) for k in range(coul_rows)], 0
        )
        flat = lax.dot_general(
            left, hot_g, (((1,), (1,)), ((), ())), preferred_element_type=F32
        )
        flat_sum[...] = flat if i == 0 else flat_sum[...] + flat

    def send_part():
        for k in range(coul_rows):
            for o in range(n_plane):
                at = slice(k * n + o * width, k * n + (o + 1) * width)
                part[o, k * width : (k + 1) * width, :] = flat_sum[at, :].astype(BF16)
        for t in owners:
            start(p_copy(t, plane))
        in_part[plane] = part[plane]

    coul_x, coul_y = rows // NX, rows // (NX * NY)

    def dy_copy(target, owner):
        block = coul16.at[pl.ds(x * coul_x + owner * coul_y, coul_y)]
        return remote(block, block, s_dy, r_dy, at_band(x, zh, target))

    def send_dy():
        arrived(in_part.at[pl.ds(0, n_plane - 1)], r_p)
        summed = in_part[0].astype(F32)
        for o in range(1, n_plane):
            summed = summed + in_part[o].astype(F32)
        coul16[pl.ds(x * coul_x + y * coul_y, coul_y), :] = summed.astype(BF16)
        for d in far_first(NY):
            start(dy_copy(y_peer(d), y))

    def dx_copy(target, owner):
        block = coul16.at[pl.ds(owner * coul_x, coul_x)]
        return remote(block, block, s_dx, r_dx, at_band(target, zh, y))

    def send_dx():
        arrived(coul16.at[pl.ds(x * coul_x, (NY - 1) * coul_y)], r_dy)
        for d in far_first(NX):
            start(dx_copy(x_peer(d), x))

    def wait_dense():
        arrived(coul16.at[pl.ds(0, (NX - 1) * coul_x)], r_dx)
        dense[...] = coul16[...].astype(F32)

    half = width // GROUPS
    block = per_owner * half
    small_block = block - 2 * half
    own_small = lax.rem(plane, period) == period - 1 if period else False
    n_small = n_plane // period if period else 0

    def sized(small, body):
        if not period:
            body(block)
            return
        pl.when(small)(lambda: body(small_block))
        pl.when(jnp.logical_not(small))(lambda: body(block))

    def of_owners(wait):
        every = block * (n_plane - 1) - 2 * half * n_small
        if not period:
            wait(orb16.at[pl.ds(0, every)])
            return
        pl.when(own_small)(lambda: wait(orb16.at[pl.ds(0, every + 2 * half)]))
        pl.when(jnp.logical_not(own_small))(lambda: wait(orb16.at[pl.ds(0, every)]))

    def of_own(wait):
        sized(own_small, lambda count: wait(orb16.at[pl.ds(0, count * (n_plane - 1))]))

    def send_block(from_ref, to_ref, count, sems, target):
        at = pl.ds(0, count)
        start(remote(from_ref.at[at], to_ref.at[at], sems[0], sems[1], {"plane": target}))

    def wait_group(g, s, i):
        if g == 0:
            wait_gx(i, s)
        elif i == 0:
            wait_gx(2, s)

    def forward(g, s):
        both = wide[:n, :]
        first, second = slim[:n_packed, :], slim[n : n + n_packed, :]
        in_first = lax.broadcasted_iota(jnp.int32, (n_packed, n), 1) < labels[:n_packed, 2:3]
        group = 4

        for i in range(half // group):
            wait_group(g, s, i)
            at = slice(g * rows_g + i * group * n, g * rows_g + (i + 1) * group * n)
            pair = (orb[at, :] * shared[s, at, :].astype(F32)).astype(BF16)
            along = dot(pair, both).astype(BF16)
            planes = [along[k * n : (k + 1) * n] for k in range(group)]
            from_first = dot(first, jnp.concatenate([plane_k[:, :n] for plane_k in planes], 1))
            from_second = dot(second, jnp.concatenate([plane_k[:, n:] for plane_k in planes], 1))
            for k in range(group):
                at = slice(k * n, (k + 1) * n)
                packed = jnp.where(in_first, from_first[:, at], from_second[:, at])
                grid_a[pl.ds(i * group + k, n_packed, stride=half), :] = packed
        for t in owners:
            send_f[s, g, t] = grid_a[pl.ds(pl.multiple_of(t * block, block), block), :].astype(BF16)
            small = lax.rem(t, period) == period - 1 if period else False
            sems = (s_f.at[g, s], r_f.at[g, s])
            sized(small, lambda count: send_block(
                send_f.at[s, g, t], recv_f.at[s, g, plane], count, sems, t))
        at = pl.ds(pl.multiple_of(plane * block, block), block)
        recv_f[s, g, plane] = grid_a[at, :].astype(BF16)

    def middle(s):
        for g in range(GROUPS):
            of_own(lambda region: arrived(region, r_f.at[g, s]))
        twin, cas = wide[n : 3 * n, :], slim[4 * n : 5 * n, :]
        pairs = per_owner // 2
        for first_pair in range(0, pairs, 2):
            js = range(first_pair, min(first_pair + 2, pairs))
            at = [slice(j * 2 * half, (j + 1) * 2 * half) for j in js]
            sticks = [recv_f[s, :, :, a, :].reshape(2 * n, n) for a in at]
            if period and js[-1] == pairs - 1:
                sticks[-1] = jnp.where(own_small, jnp.zeros_like(sticks[-1]), sticks[-1])
            spectrum = dot(twin, jnp.concatenate(sticks, 1))
            scaled = []
            for k, j in enumerate(js):
                for h in range(2):
                    coul = dense[pl.ds(2 * j + h, n, stride=width), :]
                    part_h = spectrum[h * n : (h + 1) * n, k * n : (k + 1) * n]
                    scaled.append((part_h * coul).astype(BF16))
            back = dot(cas, jnp.concatenate(scaled, 1))
            for k in range(len(js)):
                two = [
                    back[:, (2 * k + h) * n : (2 * k + h + 1) * n].reshape(n_plane, GROUPS, half, n)
                    for h in range(2)
                ]
                for g in range(GROUPS):
                    for q in range(n_plane):
                        both = jnp.concatenate([two[0][q, g], two[1][q, g]], 0)
                        send_b[s, g, q, at[k], :] = both.astype(BF16)
        for g in range(GROUPS):
            def send_all(count):
                for t in owners:
                    sems = (s_b.at[g, s], r_b.at[g, s])
                    send_block(send_b.at[s, g, t], recv_b.at[s, g, plane], count, sems, t)

            sized(own_small, send_all)
            recv_b[s, g, plane] = send_b[s, g, plane]

    def inverse(g, s):
        of_owners(lambda region: arrived(region, r_b.at[g, s]))
        first, second = wide[3 * n :, :n], wide[3 * n :, n:]
        both = slim[2 * n : 4 * n, :]
        in_first = lax.broadcasted_iota(jnp.int32, (n, n), 1) < labels[:, 2:3]
        grid_b[: n_packed * half, :] = recv_b[s, g].reshape(n_packed * half, n).astype(F32)
        group = 4

        for i in range(half // group):
            packed = [grid_b[pl.ds(i * group + k, n, stride=half), :] for k in range(group)]
            own = [jnp.where(in_first, one, 0.0).astype(BF16) for one in packed]
            other = [jnp.where(in_first, 0.0, one).astype(BF16) for one in packed]
            from_first = dot(first, jnp.concatenate(own, 1))
            from_second = dot(second, jnp.concatenate(other, 1))
            inverse_y = []
            for k in range(group):
                at = slice(k * n, (k + 1) * n)
                inverse_y.append(jnp.concatenate([from_first[:, at], from_second[:, at]], 1).astype(BF16))
            at = slice(g * rows_g + i * group * n, g * rows_g + (i + 1) * group * n)
            term = dot(jnp.concatenate(inverse_y, 0), both) * shared[s, at, :].astype(F32)
            if s == 0:
                total[at, :] = term
            else:
                out_ref[at, :] = (total[at, :] + term).astype(BF16)

    send_x(0)
    round_piece(1)
    send_x(1)
    round_piece(2)
    send_x(2)
    add_part(0)
    add_part(1)
    send_y(0)
    send_y(1)
    for i in range(2, PIECES):
        add_part(i)
    send_z(0)
    send_y(2)
    send_z(1)
    send_part()
    send_gy(0)
    send_z(2)
    send_gy(1)
    loads[3].wait()
    loads[4].wait()
    wait_gy(0)
    send_gx(0, 0)
    wait_gy(1)
    send_gx(1, 0)
    send_gy(2)
    send_gx(0, 1)
    send_gx(1, 1)
    send_dy()
    forward(0, 0)
    wait_gy(2)
    send_gx(2, 0)
    send_gx(2, 1)
    forward(0, 1)
    send_dx()
    forward(1, 0)
    forward(1, 1)
    for p, (_, count) in enumerate(pieces):
        sent(in_x[p].at[pl.ds(0, NX - 1)], s_x.at[p])
        sent(in_y[p].at[pl.ds(0, NY - 1)], s_y.at[p])
        sent(in_z[p], s_z.at[p])
        sent(shared.at[:, pl.ds(0, (NY - 1) * (count // (NX * NY)))], s_gy.at[p])
        for s in range(STEPS):
            sent(shared.at[s, pl.ds(0, (NX - 1) * (count // NX))], s_gx.at[p, s])
    sent(in_part.at[pl.ds(0, n_plane - 1)], s_p)
    grid_b[n_packed * half :, :] = jnp.zeros(((n - n_packed) * half, n), F32)
    for q in range(n_plane):
        if period and q % period == period - 1:
            recv_b[:, :, q, small_block:, :] = jnp.zeros((STEPS, GROUPS, 2 * half, n), BF16)
    wait_dense()
    middle(0)
    sent(coul16.at[pl.ds(0, (NY - 1) * coul_y)], s_dy)
    sent(coul16.at[pl.ds(0, (NX - 1) * coul_x)], s_dx)
    middle(1)
    for g in range(GROUPS):
        for s in range(STEPS):
            of_owners(lambda region: sent(region, s_f.at[g, s]))
    inverse(0, 0)
    inverse(1, 0)
    inverse(0, 1)
    inverse(1, 1)
    for g in range(GROUPS):
        for s in range(STEPS):
            of_own(lambda region: sent(region, s_b.at[g, s]))


def on_device(orbitals, coulomb, stick_lists, roots):
    _, width, n, _ = orbitals.shape
    n_plane = n // width
    rows = width * n
    rows_g = rows // GROUPS
    counts = [count for _, count in broadcast_pieces(rows)]
    coul_block = n // (NX * NY) * width
    per_owner = packing(n, n_plane)[1]
    wide, slim, labels = tables(n, n_plane)
    hbm = pl.BlockSpec(memory_space=pl.ANY)
    vmem = pl.BlockSpec(memory_space=pltpu.VMEM)
    dma = pltpu.SemaphoreType.DMA

    def pair_of_sems(*shape):
        return [dma(shape), dma(shape)]

    gs = (GROUPS, STEPS)
    spectra = pltpu.VMEM((STEPS, GROUPS, n_plane, per_owner * width // GROUPS, n), BF16)
    out = pl.pallas_call(
        functools.partial(kernel, n, n_plane),
        out_shape=jax.ShapeDtypeStruct((rows, n), BF16),
        in_specs=[pl.BlockSpec(memory_space=pltpu.SMEM)] + [hbm] * 6,
        out_specs=vmem,
        scratch_shapes=[
            pltpu.VMEM((rows, n), F32),
            pltpu.VMEM(wide.shape, BF16),
            pltpu.VMEM(slim.shape, BF16),
            pltpu.VMEM(labels.shape, jnp.int32),
            pltpu.VMEM((16, coulomb.shape[1]), BF16),
            pltpu.VMEM(stick_lists.shape, jnp.int32),
            pltpu.VMEM((rows, n), BF16),
            *[pltpu.VMEM((NX, count // NX, n), BF16) for count in counts],
            *[pltpu.VMEM((STEPS, count // NX, n), BF16) for count in counts],
            *[pltpu.VMEM((NY, STEPS, count // (NX * NY), n), BF16) for count in counts],
            *[pltpu.VMEM((STEPS, count // (NX * NY), n), BF16) for count in counts * 2],
            pltpu.VMEM((STEPS, rows, n), BF16),
            pltpu.VMEM((n // (NX * NY) * n, n), F32),
            pltpu.VMEM((n_plane, coul_block, n), BF16),
            pltpu.VMEM((n_plane, coul_block, n), BF16),
            pltpu.VMEM((rows, n), BF16),
            pltpu.VMEM((rows, n), F32),
            pltpu.VMEM((rows_g, n), F32),
            pltpu.VMEM((rows_g, n), F32),
            spectra, spectra, spectra, spectra,
            pltpu.VMEM((rows, n), F32),
            dma((len(counts),)),
            dma((5,)),
            *pair_of_sems(len(counts)),
            *pair_of_sems(len(counts)),
            *pair_of_sems(len(counts)),
            *pair_of_sems(len(counts)),
            *pair_of_sems(len(counts), STEPS),
            dma, dma, dma, dma, dma, dma,
            *pair_of_sems(*gs),
            *pair_of_sems(*gs),
        ],
        compiler_params=pltpu.CompilerParams(
            collective_id=0, has_side_effects=True, vmem_limit_bytes=57 * 1024 * 1024
        ),
        name="exchange",
    )(
        roots, orbitals.reshape(rows, n),
        wide, slim, labels, coulomb, stick_lists,
    )
    return out.reshape(1, width, n, n)


def solution(mesh):
    in_specs = (P("band", "plane", None, None), P(None, "plane"), P(), P())
    out_specs = P("band", "plane", None, None)
    return jax.shard_map(
        on_device, mesh=mesh, in_specs=in_specs, out_specs=out_specs, check_vma=False
    )
```

```python
import functools
import math

import jax
import jax.numpy as jnp
import numpy as np
from jax import lax
from jax.experimental import pallas as pl
from jax.experimental.pallas import tpu as pltpu
from jax.sharding import PartitionSpec as P

NX, NZ, NY = 4, 2, 8
STICKS = 12288
GROUPS = 2
STEPS = 2
PIECES = 3
MESH = pl.DeviceIdType.MESH
F32, BF16 = jnp.float32, jnp.bfloat16


def cas_table(n):
    k = np.arange(n)
    angles = 2.0 * math.pi / n * ((k[:, None] * k[None, :]) % n)
    return np.asarray(np.cos(angles) + np.sin(angles), np.float32)


def pair_table(n, width):
    cas = cas_table(n)
    half = width // GROUPS
    table = np.zeros((2, n, GROUPS, n // width, 2, half), np.float32)
    by_x = cas.reshape(n, n // width, GROUPS, half).transpose(0, 2, 1, 3)
    for h in range(2):
        table[h, :, :, :, h, :] = by_x
    return table.reshape(2 * n, 2 * n)


def packing(n, n_plane):
    signed = np.minimum(np.arange(n), n - np.arange(n))
    squares = signed[:, None] ** 2 + signed[None, :] ** 2
    kept = (squares <= np.sort(squares.reshape(-1))[STICKS - 1]).sum(1)
    best = None
    for t in range(1, n // 2 + 1):
        for extra in ([], [n - t + 1]):
            second = [h for h in range(n) if kept[h] and (signed[h] >= t or h in extra)]
            firsts = [h for h in range(n) if kept[h] and h not in second]
            free, mate = sorted(firsts, key=lambda h: -kept[h]), {}
            for h in sorted(second, key=lambda h: -kept[h]):
                host = next((f for f in free if kept[f] + kept[h] <= n), None)
                if host is None:
                    break
                free.remove(host)
                mate[host] = h
            else:
                if best is None or len(firsts) < len(best[0]):
                    best = firsts, mate, t, extra
    firsts, mate, t, extra = best
    pairs = -(-len(firsts) // 2)
    per_owner = -(-pairs // n_plane) * 2
    n_small = per_owner // 2 * n_plane - pairs
    period = n_plane // n_small if n_small and n_plane % n_small == 0 else 0
    table = -np.ones((per_owner * n_plane, 3), np.int64)
    left = list(firsts)
    for owner in range(n_plane):
        count = per_owner - 2 if period and owner % period == period - 1 else per_owner
        for k in range(min(count, len(left))):
            h = left.pop(0)
            table[owner * per_owner + k] = h, mate.get(h, -1), kept[h]
    return table, per_owner, period, t, (extra or [-1])[0]


def tables(n, n_plane):
    width = n // n_plane
    cas = cas_table(n)
    rows, per_owner = packing(n, n_plane)[:2]
    order = sorted(range(n), key=lambda g: (min(g, n - g), g > n // 2))
    both = np.concatenate([cas[:, order], cas[:, order[::-1]]], 1)
    first, second = np.zeros((n, n), np.float32), np.zeros((n, n), np.float32)
    for row, (h, other, _) in enumerate(rows):
        if h >= 0:
            first[row] = cas[h]
        if other >= 0:
            second[row] = cas[other]
    wide = np.concatenate([both, pair_table(n, width), np.concatenate([first.T, second.T], 1) / n], 0)
    slim = np.concatenate([first, second, both.T / n, cas / n], 0)
    labels = np.full((n, 128), -7, np.int32)
    for row, (h, other, length) in enumerate(rows):
        place = row // per_owner * width + row % per_owner
        labels[place, 0] = h if h >= 0 else -7
        labels[place, 1] = other if other >= 0 else -7
    labels[:, 2] = n
    labels[: len(rows), 2] = np.where(rows[:, 2] < 0, n, rows[:, 2])
    return jnp.asarray(wide).astype(BF16), jnp.asarray(slim).astype(BF16), jnp.asarray(labels)


def dot(a, b):
    return jnp.dot(a, b, preferred_element_type=F32)


def broadcast_pieces(rows):
    return [(0, rows // 2), (rows // 2, rows // 2)]


def far_first(count):
    return sorted(range(1, count), key=lambda d: -min(d, count - d))


def pick(index, values):
    out = values[0]
    for k in range(1, len(values)):
        out = jnp.where(index == k, values[k], out)
    return out


def remote(src, dst, send_sem, recv_sem, device):
    return pltpu.make_async_remote_copy(
        src_ref=src, dst_ref=dst, send_sem=send_sem, recv_sem=recv_sem,
        device_id=device, device_id_type=MESH,
    )


def kernel(
    n, n_plane,
    roots_ref, orb_hbm, wide_hbm, slim_hbm, labels_hbm, coulomb_hbm, ids_hbm, out_ref,
    orb, wide, slim, labels, coulomb, ids_ref,
    orb16, in_x0, in_x1, sel0, sel1, in_y0, in_y1, cand0, cand1, in_z0, in_z1, shared,
    flat_sum, part, in_part, coul16, dense, grid_a, grid_b, send_f, recv_f, send_b, recv_b, total,
    s_orb, s_in, s_x, r_x, s_y, r_y, s_z, r_z, s_gy, r_gy, s_gx, r_gx,
    s_p, r_p, s_dy, r_dy, s_dx, r_dx, s_f, r_f, s_b, r_b,
):
    width = n // n_plane
    rows = width * n
    rows_g = rows // GROUPS
    _, per_owner, period, edge, edge_row = packing(n, n_plane)
    n_packed = per_owner * n_plane
    in_x, sel, in_y = [in_x0, in_x1], [sel0, sel1], [in_y0, in_y1]
    cand, in_z = [cand0, cand1], [in_z0, in_z1]
    pieces = broadcast_pieces(rows)
    band, plane = lax.axis_index("band"), lax.axis_index("plane")
    y = lax.rem(band, NY)
    zh = lax.rem(band // NY, NZ)
    x = band // (NY * NZ)

    def at_band(bx, bz, by):
        return {"band": (bx * NZ + bz) * NY + by}

    def x_peer(d):
        return lax.rem(x + d, NX)

    def y_peer(d):
        return lax.rem(y + d, NY)

    def p_peer(d):
        return lax.rem(plane + d, n_plane)

    bits = [lax.rem(plane // (1 << k), 2) for k in range(n_plane.bit_length() - 1)]
    owners = []
    for flip in sorted(range(1, n_plane), key=lambda f: (-(f >> 1), f)):
        t = 0
        for k, bit in enumerate(bits):
            t = t + (1 << k) * (1 - bit if flip >> k & 1 else bit)
        owners.append(t)

    barrier = pltpu.get_barrier_semaphore()
    peers = [at_band(x_peer(d), zh, y) for d in far_first(NX)]
    peers += [at_band(x, zh, y_peer(d)) for d in far_first(NY)]
    peers += [at_band(x, lax.rem(zh + d, NZ), y) for d in range(1, NZ)]
    peers += [{"plane": p_peer(d)} for d in range(1, n_plane)]
    for peer in peers:
        pl.semaphore_signal(barrier, inc=1, device_id=peer, device_id_type=MESH)

    coul_rows = n // (NX * NY)
    first_row = (x * NY + y) * coul_rows
    coul_tile = pl.multiple_of(first_row // 16 * 16, 16)
    orb_loads = [
        pltpu.make_async_copy(orb_hbm.at[pl.ds(*at)], orb.at[pl.ds(*at)], s_orb.at[p])
        for p, at in enumerate(pieces)
    ]
    loads = [
        pltpu.make_async_copy(coulomb_hbm.at[pl.ds(coul_tile, 16)], coulomb, s_in.at[0]),
        pltpu.make_async_copy(ids_hbm, ids_ref, s_in.at[1]),
        pltpu.make_async_copy(labels_hbm, labels, s_in.at[2]),
        pltpu.make_async_copy(slim_hbm, slim, s_in.at[3]),
        pltpu.make_async_copy(wide_hbm, wide, s_in.at[4]),
    ]
    for load in orb_loads + loads:
        load.start()

    def round_piece(p):
        first, count = pieces[p]
        orb_loads[p].wait()
        orb16[first : first + count, :] = orb[first : first + count, :].astype(BF16)

    round_piece(0)
    pl.semaphore_wait(barrier, len(peers))

    def start(copy):
        copy.start()

    def arrived(region, sem):
        remote(region, region, sem, sem, {"plane": p_peer(1)}).wait_recv()

    def sent(region, sem):
        remote(region, region, sem, sem, {"plane": p_peer(1)}).wait_send()

    def x_copy(p, target, slot):
        first, count = pieces[p]
        chunk = count // NX
        return remote(
            orb16.at[pl.ds(first + target * chunk, chunk)], in_x[p].at[slot],
            s_x.at[p], r_x.at[p], at_band(target, zh, y),
        )

    def send_x(p):
        for d in far_first(NX):
            start(x_copy(p, x_peer(d), x))
        first, count = pieces[p]
        chunk = count // NX
        in_x[p][x] = orb16[pl.ds(first + x * chunk, chunk), :]

    root = [roots_ref[s] for s in range(STEPS)]
    root_y = [lax.rem(r, NY) for r in root]
    root_z = [lax.rem(r // NY, NZ) for r in root]
    root_x = [r // (NY * NZ) for r in root]

    def send_y(p):
        arrived(in_x[p].at[pl.ds(0, NX - 1)], r_x.at[p])
        for s in range(STEPS):
            sel[p][s] = pick(root_x[s], [in_x[p][k] for k in range(NX)])
        chunk = pieces[p][1] // (NX * NY)
        for d in far_first(NY):
            t = y_peer(d)
            start(remote(
                sel[p].at[:, pl.ds(t * chunk, chunk)], in_y[p].at[y],
                s_y.at[p], r_y.at[p], at_band(x, zh, t),
            ))
        in_y[p][y] = sel[p][:, pl.ds(y * chunk, chunk), :]

    def z_copy(p):
        return remote(
            cand[p], in_z[p], s_z.at[p], r_z.at[p], at_band(x, lax.rem(zh + 1, NZ), y)
        )

    def send_z(p):
        arrived(in_y[p].at[pl.ds(0, NY - 1)], r_y.at[p])
        for s in range(STEPS):
            cand[p][s] = pick(root_y[s], [in_y[p][k, s] for k in range(NY)])
        start(z_copy(p))

    def send_gy(p):
        z_copy(p).wait_recv()
        first, count = pieces[p]
        chunk = count // (NX * NY)
        at = pl.ds(first + (x * NY + y) * chunk, chunk)
        for s in range(STEPS):
            shared[s, at, :] = jnp.where(root_z[s] == zh, cand[p][s], in_z[p][s])
        block = shared.at[:, at]
        for d in far_first(NY):
            start(remote(block, block, s_gy.at[p], r_gy.at[p], at_band(x, zh, y_peer(d))))

    def wait_gy(p):
        first, count = pieces[p]
        chunk = count // (NX * NY)
        arrived(shared.at[:, pl.ds(first + x * NY * chunk, (NY - 1) * chunk)], r_gy.at[p])

    def send_gx(p, s):
        first, count = pieces[p]
        block = shared.at[s, pl.ds(first + x * (count // NX), count // NX)]
        for d in far_first(NX):
            start(remote(block, block, s_gx.at[p, s], r_gx.at[p, s], at_band(x_peer(d), zh, y)))

    def wait_gx(p, s):
        first, count = pieces[p]
        arrived(shared.at[s, pl.ds(first, count // NX * (NX - 1))], r_gx.at[p, s])

    def p_copy(target, slot):
        return remote(part.at[target], in_part.at[slot], s_p, r_p, {"plane": target})

    slots = ids_ref.shape[1]
    piece = -(-slots // (128 * PIECES)) * 128

    def add_part(i):
        if i == 0:
            loads[0].wait()
            loads[1].wait()
            loads[2].wait()
        at = slice(i * piece, min((i + 1) * piece, slots))
        ids = ids_ref[pl.ds(plane, 1), at]
        valid = ids >= 0
        id_h = jnp.where(valid, ids // n, -1)
        id_g = jnp.where(valid, lax.rem(ids, n), 0)
        lane = jnp.where(id_g == 0, 0, jnp.where(id_g <= n // 2, 2 * id_g - 1, 2 * (n - id_g)))
        reverse = (jnp.minimum(id_h, n - id_h) >= edge) | (id_h == edge_row)
        lane = jnp.where(reverse, n - 1 - lane, lane)
        iota = lax.broadcasted_iota(jnp.int32, (n, ids.shape[1]), 0)
        hot_h = (labels[:, 0:1] == id_h) | (labels[:, 1:2] == id_h)
        hot_g = jnp.where(iota == lane, 1.0, 0.0).astype(BF16)
        tile = coulomb[:, at].astype(F32)
        own = tile[:coul_rows]
        for k in range(1, 16 // coul_rows):
            inside = first_row - coul_tile == k * coul_rows
            own = jnp.where(inside, tile[k * coul_rows : (k + 1) * coul_rows], own)
        left = jnp.concatenate(
            [jnp.where(hot_h, own[k : k + 1], 0.0).astype(BF16) for k in range(coul_rows)], 0
        )
        flat = lax.dot_general(
            left, hot_g, (((1,), (1,)), ((), ())), preferred_element_type=F32
        )
        flat_sum[...] = flat if i == 0 else flat_sum[...] + flat

    def send_part():
        for k in range(coul_rows):
            for o in range(n_plane):
                at = slice(k * n + o * width, k * n + (o + 1) * width)
                part[o, k * width : (k + 1) * width, :] = flat_sum[at, :].astype(BF16)
        for t in owners:
            start(p_copy(t, plane))
        in_part[plane] = part[plane]

    coul_x, coul_y = rows // NX, rows // (NX * NY)

    def dy_copy(target, owner):
        block = coul16.at[pl.ds(x * coul_x + owner * coul_y, coul_y)]
        return remote(block, block, s_dy, r_dy, at_band(x, zh, target))

    def send_dy():
        arrived(in_part.at[pl.ds(0, n_plane - 1)], r_p)
        summed = in_part[0].astype(F32)
        for o in range(1, n_plane):
            summed = summed + in_part[o].astype(F32)
        coul16[pl.ds(x * coul_x + y * coul_y, coul_y), :] = summed.astype(BF16)
        for d in far_first(NY):
            start(dy_copy(y_peer(d), y))

    def dx_copy(target, owner):
        block = coul16.at[pl.ds(owner * coul_x, coul_x)]
        return remote(block, block, s_dx, r_dx, at_band(target, zh, y))

    def send_dx():
        arrived(coul16.at[pl.ds(x * coul_x, (NY - 1) * coul_y)], r_dy)
        for d in far_first(NX):
            start(dx_copy(x_peer(d), x))

    def wait_dense():
        arrived(coul16.at[pl.ds(0, (NX - 1) * coul_x)], r_dx)
        dense[...] = coul16[...].astype(F32)

    half = width // GROUPS
    block = per_owner * half
    small_block = block - 2 * half
    own_small = lax.rem(plane, period) == period - 1 if period else False
    n_small = n_plane // period if period else 0

    def sized(small, body):
        if not period:
            body(block)
            return
        pl.when(small)(lambda: body(small_block))
        pl.when(jnp.logical_not(small))(lambda: body(block))

    def of_owners(wait):
        every = block * (n_plane - 1) - 2 * half * n_small
        if not period:
            wait(orb16.at[pl.ds(0, every)])
            return
        pl.when(own_small)(lambda: wait(orb16.at[pl.ds(0, every + 2 * half)]))
        pl.when(jnp.logical_not(own_small))(lambda: wait(orb16.at[pl.ds(0, every)]))

    def of_own(wait):
        sized(own_small, lambda count: wait(orb16.at[pl.ds(0, count * (n_plane - 1))]))

    def send_block(from_ref, to_ref, count, sems, target):
        at = pl.ds(0, count)
        start(remote(from_ref.at[at], to_ref.at[at], sems[0], sems[1], {"plane": target}))

    def wait_group(g, s, i):
        if i == 0:
            wait_gx(g, s)

    def forward(g, s):
        both = wide[:n, :]
        first, second = slim[:n_packed, :], slim[n : n + n_packed, :]
        in_first = lax.broadcasted_iota(jnp.int32, (n_packed, n), 1) < labels[:n_packed, 2:3]
        group = 4

        for i in range(half // group):
            wait_group(g, s, i)
            at = slice(g * rows_g + i * group * n, g * rows_g + (i + 1) * group * n)
            pair = (orb[at, :] * shared[s, at, :].astype(F32)).astype(BF16)
            along = dot(pair, both).astype(BF16)
            planes = [along[k * n : (k + 1) * n] for k in range(group)]
            from_first = dot(first, jnp.concatenate([plane_k[:, :n] for plane_k in planes], 1))
            from_second = dot(second, jnp.concatenate([plane_k[:, n:] for plane_k in planes], 1))
            for k in range(group):
                at = slice(k * n, (k + 1) * n)
                packed = jnp.where(in_first, from_first[:, at], from_second[:, at])
                grid_a[pl.ds(i * group + k, n_packed, stride=half), :] = packed
        for t in owners:
            send_f[s, g, t] = grid_a[pl.ds(pl.multiple_of(t * block, block), block), :].astype(BF16)
            small = lax.rem(t, period) == period - 1 if period else False
            sems = (s_f.at[g, s], r_f.at[g, s])
            sized(small, lambda count: send_block(
                send_f.at[s, g, t], recv_f.at[s, g, plane], count, sems, t))
        at = pl.ds(pl.multiple_of(plane * block, block), block)
        recv_f[s, g, plane] = grid_a[at, :].astype(BF16)

    def middle(s):
        for g in range(GROUPS):
            of_own(lambda region: arrived(region, r_f.at[g, s]))
        twin, cas = wide[n : 3 * n, :], slim[4 * n : 5 * n, :]
        pairs = per_owner // 2
        for first_pair in range(0, pairs, 2):
            js = range(first_pair, min(first_pair + 2, pairs))
            at = [slice(j * 2 * half, (j + 1) * 2 * half) for j in js]
            sticks = [recv_f[s, :, :, a, :].reshape(2 * n, n) for a in at]
            if period and js[-1] == pairs - 1:
                sticks[-1] = jnp.where(own_small, jnp.zeros_like(sticks[-1]), sticks[-1])
            spectrum = dot(twin, jnp.concatenate(sticks, 1))
            scaled = []
            for k, j in enumerate(js):
                for h in range(2):
                    coul = dense[pl.ds(2 * j + h, n, stride=width), :]
                    part_h = spectrum[h * n : (h + 1) * n, k * n : (k + 1) * n]
                    scaled.append((part_h * coul).astype(BF16))
            back = dot(cas, jnp.concatenate(scaled, 1))
            for k in range(len(js)):
                two = [
                    back[:, (2 * k + h) * n : (2 * k + h + 1) * n].reshape(n_plane, GROUPS, half, n)
                    for h in range(2)
                ]
                for g in range(GROUPS):
                    for q in range(n_plane):
                        both = jnp.concatenate([two[0][q, g], two[1][q, g]], 0)
                        send_b[s, g, q, at[k], :] = both.astype(BF16)
        for g in range(GROUPS):
            def send_all(count):
                for t in owners:
                    sems = (s_b.at[g, s], r_b.at[g, s])
                    send_block(send_b.at[s, g, t], recv_b.at[s, g, plane], count, sems, t)

            sized(own_small, send_all)
            recv_b[s, g, plane] = send_b[s, g, plane]

    def inverse(g, s):
        of_owners(lambda region: arrived(region, r_b.at[g, s]))
        first, second = wide[3 * n :, :n], wide[3 * n :, n:]
        both = slim[2 * n : 4 * n, :]
        in_first = lax.broadcasted_iota(jnp.int32, (n, n), 1) < labels[:, 2:3]
        grid_b[: n_packed * half, :] = recv_b[s, g].reshape(n_packed * half, n).astype(F32)
        group = 4

        for i in range(half // group):
            packed = [grid_b[pl.ds(i * group + k, n, stride=half), :] for k in range(group)]
            own = [jnp.where(in_first, one, 0.0).astype(BF16) for one in packed]
            other = [jnp.where(in_first, 0.0, one).astype(BF16) for one in packed]
            from_first = dot(first, jnp.concatenate(own, 1))
            from_second = dot(second, jnp.concatenate(other, 1))
            inverse_y = []
            for k in range(group):
                at = slice(k * n, (k + 1) * n)
                inverse_y.append(jnp.concatenate([from_first[:, at], from_second[:, at]], 1).astype(BF16))
            at = slice(g * rows_g + i * group * n, g * rows_g + (i + 1) * group * n)
            term = dot(jnp.concatenate(inverse_y, 0), both) * shared[s, at, :].astype(F32)
            if s == 0:
                total[at, :] = term
            else:
                out_ref[at, :] = (total[at, :] + term).astype(BF16)

    send_x(0)
    round_piece(1)
    send_x(1)
    for i in range(PIECES):
        add_part(i)
    send_y(0)
    send_part()
    send_y(1)
    send_z(0)
    send_z(1)
    send_gy(0)
    send_gy(1)
    loads[3].wait()
    loads[4].wait()
    wait_gy(0)
    send_gx(0, 0)
    wait_gy(1)
    send_gx(1, 0)
    send_dy()
    forward(0, 0)
    send_gx(0, 1)
    send_gx(1, 1)
    forward(1, 0)
    send_dx()
    forward(0, 1)
    forward(1, 1)
    for p, (_, count) in enumerate(pieces):
        sent(in_x[p].at[pl.ds(0, NX - 1)], s_x.at[p])
        sent(in_y[p].at[pl.ds(0, NY - 1)], s_y.at[p])
        sent(in_z[p], s_z.at[p])
        sent(shared.at[:, pl.ds(0, (NY - 1) * (count // (NX * NY)))], s_gy.at[p])
        for s in range(STEPS):
            sent(shared.at[s, pl.ds(0, (NX - 1) * (count // NX))], s_gx.at[p, s])
    sent(in_part.at[pl.ds(0, n_plane - 1)], s_p)
    grid_b[n_packed * half :, :] = jnp.zeros(((n - n_packed) * half, n), F32)
    for q in range(n_plane):
        if period and q % period == period - 1:
            recv_b[:, :, q, small_block:, :] = jnp.zeros((STEPS, GROUPS, 2 * half, n), BF16)
    wait_dense()
    middle(0)
    sent(coul16.at[pl.ds(0, (NY - 1) * coul_y)], s_dy)
    sent(coul16.at[pl.ds(0, (NX - 1) * coul_x)], s_dx)
    middle(1)
    for g in range(GROUPS):
        for s in range(STEPS):
            of_owners(lambda region: sent(region, s_f.at[g, s]))
    inverse(0, 0)
    inverse(1, 0)
    inverse(0, 1)
    inverse(1, 1)
    for g in range(GROUPS):
        for s in range(STEPS):
            of_own(lambda region: sent(region, s_b.at[g, s]))


def on_device(orbitals, coulomb, stick_lists, roots):
    _, width, n, _ = orbitals.shape
    n_plane = n // width
    rows = width * n
    rows_g = rows // GROUPS
    counts = [count for _, count in broadcast_pieces(rows)]
    coul_block = n // (NX * NY) * width
    per_owner = packing(n, n_plane)[1]
    wide, slim, labels = tables(n, n_plane)
    hbm = pl.BlockSpec(memory_space=pl.ANY)
    vmem = pl.BlockSpec(memory_space=pltpu.VMEM)
    dma = pltpu.SemaphoreType.DMA

    def pair_of_sems(*shape):
        return [dma(shape), dma(shape)]

    gs = (GROUPS, STEPS)
    spectra = pltpu.VMEM((STEPS, GROUPS, n_plane, per_owner * width // GROUPS, n), BF16)
    out = pl.pallas_call(
        functools.partial(kernel, n, n_plane),
        out_shape=jax.ShapeDtypeStruct((rows, n), BF16),
        in_specs=[pl.BlockSpec(memory_space=pltpu.SMEM)] + [hbm] * 6,
        out_specs=vmem,
        scratch_shapes=[
            pltpu.VMEM((rows, n), F32),
            pltpu.VMEM(wide.shape, BF16),
            pltpu.VMEM(slim.shape, BF16),
            pltpu.VMEM(labels.shape, jnp.int32),
            pltpu.VMEM((16, coulomb.shape[1]), BF16),
            pltpu.VMEM(stick_lists.shape, jnp.int32),
            pltpu.VMEM((rows, n), BF16),
            *[pltpu.VMEM((NX, count // NX, n), BF16) for count in counts],
            *[pltpu.VMEM((STEPS, count // NX, n), BF16) for count in counts],
            *[pltpu.VMEM((NY, STEPS, count // (NX * NY), n), BF16) for count in counts],
            *[pltpu.VMEM((STEPS, count // (NX * NY), n), BF16) for count in counts * 2],
            pltpu.VMEM((STEPS, rows, n), BF16),
            pltpu.VMEM((n // (NX * NY) * n, n), F32),
            pltpu.VMEM((n_plane, coul_block, n), BF16),
            pltpu.VMEM((n_plane, coul_block, n), BF16),
            pltpu.VMEM((rows, n), BF16),
            pltpu.VMEM((rows, n), F32),
            pltpu.VMEM((rows_g, n), F32),
            pltpu.VMEM((rows_g, n), F32),
            spectra, spectra, spectra, spectra,
            pltpu.VMEM((rows, n), F32),
            dma((len(counts),)),
            dma((5,)),
            *pair_of_sems(len(counts)),
            *pair_of_sems(len(counts)),
            *pair_of_sems(len(counts)),
            *pair_of_sems(len(counts)),
            *pair_of_sems(len(counts), STEPS),
            dma, dma, dma, dma, dma, dma,
            *pair_of_sems(*gs),
            *pair_of_sems(*gs),
        ],
        compiler_params=pltpu.CompilerParams(
            collective_id=0, has_side_effects=True, vmem_limit_bytes=53760 * 1024
        ),
        name="exchange",
    )(
        roots, orbitals.reshape(rows, n),
        wide, slim, labels, coulomb, stick_lists,
    )
    return out.reshape(1, width, n, n)


def solution(mesh):
    in_specs = (P("band", "plane", None, None), P(None, "plane"), P(), P())
    out_specs = P("band", "plane", None, None)
    return jax.shard_map(
        on_device, mesh=mesh, in_specs=in_specs, out_specs=out_specs, check_vma=False
    )
```

```python
import functools
import math

import jax
import jax.numpy as jnp
import numpy as np
from jax import lax
from jax.experimental import pallas as pl
from jax.experimental.pallas import tpu as pltpu
from jax.sharding import PartitionSpec as P

NX, NZ, NY = 4, 2, 8
STICKS = 12288
GROUPS = 2
STEPS = 2
PIECES = 3
MESH = pl.DeviceIdType.MESH
F32, BF16 = jnp.float32, jnp.bfloat16


def cas_table(n):
    k = np.arange(n)
    angles = 2.0 * math.pi / n * ((k[:, None] * k[None, :]) % n)
    return np.asarray(np.cos(angles) + np.sin(angles), np.float32)


def pair_table(n, width):
    cas = cas_table(n)
    half = width // GROUPS
    table = np.zeros((2, n, GROUPS, n // width, 2, half), np.float32)
    by_x = cas.reshape(n, n // width, GROUPS, half).transpose(0, 2, 1, 3)
    for h in range(2):
        table[h, :, :, :, h, :] = by_x
    return table.reshape(2 * n, 2 * n)


def packing(n, n_plane):
    signed = np.minimum(np.arange(n), n - np.arange(n))
    squares = signed[:, None] ** 2 + signed[None, :] ** 2
    kept = (squares <= np.sort(squares.reshape(-1))[STICKS - 1]).sum(1)
    best = None
    for t in range(1, n // 2 + 1):
        for extra in ([], [n - t + 1]):
            second = [h for h in range(n) if kept[h] and (signed[h] >= t or h in extra)]
            firsts = [h for h in range(n) if kept[h] and h not in second]
            free, mate = sorted(firsts, key=lambda h: -kept[h]), {}
            for h in sorted(second, key=lambda h: -kept[h]):
                host = next((f for f in free if kept[f] + kept[h] <= n), None)
                if host is None:
                    break
                free.remove(host)
                mate[host] = h
            else:
                if best is None or len(firsts) < len(best[0]):
                    best = firsts, mate, t, extra
    firsts, mate, t, extra = best
    pairs = -(-len(firsts) // 2)
    per_owner = -(-pairs // n_plane) * 2
    n_small = per_owner // 2 * n_plane - pairs
    period = n_plane // n_small if n_small and n_plane % n_small == 0 else 0
    table = -np.ones((per_owner * n_plane, 3), np.int64)
    left = list(firsts)
    for owner in range(n_plane):
        count = per_owner - 2 if period and owner % period == period - 1 else per_owner
        for k in range(min(count, len(left))):
            h = left.pop(0)
            table[owner * per_owner + k] = h, mate.get(h, -1), kept[h]
    return table, per_owner, period, t, (extra or [-1])[0]


def tables(n, n_plane):
    width = n // n_plane
    cas = cas_table(n)
    rows, per_owner = packing(n, n_plane)[:2]
    order = sorted(range(n), key=lambda g: (min(g, n - g), g > n // 2))
    both = np.concatenate([cas[:, order], cas[:, order[::-1]]], 1)
    first, second = np.zeros((n, n), np.float32), np.zeros((n, n), np.float32)
    for row, (h, other, _) in enumerate(rows):
        if h >= 0:
            first[row] = cas[h]
        if other >= 0:
            second[row] = cas[other]
    wide = np.concatenate([both, pair_table(n, width), np.concatenate([first.T, second.T], 1) / n], 0)
    slim = np.concatenate([first, second, both.T / n, cas / n], 0)
    labels = np.full((n, 128), -7, np.int32)
    for row, (h, other, length) in enumerate(rows):
        place = row // per_owner * width + row % per_owner
        labels[place, 0] = h if h >= 0 else -7
        labels[place, 1] = other if other >= 0 else -7
    labels[:, 2] = n
    labels[: len(rows), 2] = np.where(rows[:, 2] < 0, n, rows[:, 2])
    return jnp.asarray(wide).astype(BF16), jnp.asarray(slim).astype(BF16), jnp.asarray(labels)


def dot(a, b):
    return jnp.dot(a, b, preferred_element_type=F32)


def broadcast_pieces(rows):
    return [(0, rows // 4), (rows // 4, rows // 4), (rows // 2, rows // 2)]


def far_first(count):
    return sorted(range(1, count), key=lambda d: -min(d, count - d))


def pick(index, values):
    out = values[0]
    for k in range(1, len(values)):
        out = jnp.where(index == k, values[k], out)
    return out


def remote(src, dst, send_sem, recv_sem, device):
    return pltpu.make_async_remote_copy(
        src_ref=src, dst_ref=dst, send_sem=send_sem, recv_sem=recv_sem,
        device_id=device, device_id_type=MESH,
    )


def kernel(
    n, n_plane,
    roots_ref, orb_hbm, wide_hbm, slim_hbm, labels_hbm, coulomb_hbm, ids_hbm, out_ref,
    orb, wide, slim, labels, coulomb, ids_ref,
    orb16, in_x0, in_x1, in_x2, sel0, sel1, sel2, in_y0, in_y1, in_y2,
    cand0, cand1, cand2, in_z0, in_z1, in_z2, shared,
    flat_sum, part, in_part, coul16, dense, grid_a, grid_b, send_f, recv_f, send_b, recv_b, total,
    s_orb, s_in, s_x, r_x, s_y, r_y, s_z, r_z, s_gy, r_gy, s_gx, r_gx,
    s_p, r_p, s_dy, r_dy, s_dx, r_dx, s_f, r_f, s_b, r_b,
):
    width = n // n_plane
    rows = width * n
    rows_g = rows // GROUPS
    _, per_owner, period, edge, edge_row = packing(n, n_plane)
    n_packed = per_owner * n_plane
    in_x, sel, in_y = [in_x0, in_x1, in_x2], [sel0, sel1, sel2], [in_y0, in_y1, in_y2]
    cand, in_z = [cand0, cand1, cand2], [in_z0, in_z1, in_z2]
    pieces = broadcast_pieces(rows)
    band, plane = lax.axis_index("band"), lax.axis_index("plane")
    y = lax.rem(band, NY)
    zh = lax.rem(band // NY, NZ)
    x = band // (NY * NZ)

    def at_band(bx, bz, by):
        return {"band": (bx * NZ + bz) * NY + by}

    def x_peer(d):
        return lax.rem(x + d, NX)

    def y_peer(d):
        return lax.rem(y + d, NY)

    def p_peer(d):
        return lax.rem(plane + d, n_plane)

    bits = [lax.rem(plane // (1 << k), 2) for k in range(n_plane.bit_length() - 1)]
    owners = []
    for flip in sorted(range(1, n_plane), key=lambda f: (-(f >> 1), f)):
        t = 0
        for k, bit in enumerate(bits):
            t = t + (1 << k) * (1 - bit if flip >> k & 1 else bit)
        owners.append(t)

    barrier = pltpu.get_barrier_semaphore()
    peers = [at_band(x_peer(d), zh, y) for d in far_first(NX)]
    peers += [at_band(x, zh, y_peer(d)) for d in far_first(NY)]
    peers += [at_band(x, lax.rem(zh + d, NZ), y) for d in range(1, NZ)]
    peers += [{"plane": p_peer(d)} for d in range(1, n_plane)]
    for peer in peers:
        pl.semaphore_signal(barrier, inc=1, device_id=peer, device_id_type=MESH)

    coul_rows = n // (NX * NY)
    first_row = (y * NX + x) * coul_rows
    coul_tile = pl.multiple_of(first_row // 16 * 16, 16)
    orb_loads = [
        pltpu.make_async_copy(orb_hbm.at[pl.ds(*at)], orb.at[pl.ds(*at)], s_orb.at[p])
        for p, at in enumerate(pieces)
    ]
    loads = [
        pltpu.make_async_copy(coulomb_hbm.at[pl.ds(coul_tile, 16)], coulomb, s_in.at[0]),
        pltpu.make_async_copy(ids_hbm, ids_ref, s_in.at[1]),
        pltpu.make_async_copy(labels_hbm, labels, s_in.at[2]),
        pltpu.make_async_copy(slim_hbm, slim, s_in.at[3]),
        pltpu.make_async_copy(wide_hbm, wide, s_in.at[4]),
    ]
    for load in orb_loads + loads:
        load.start()

    def round_piece(p):
        first, count = pieces[p]
        orb_loads[p].wait()
        orb16[first : first + count, :] = orb[first : first + count, :].astype(BF16)

    round_piece(0)
    pl.semaphore_wait(barrier, len(peers))

    def start(copy):
        copy.start()

    def arrived(region, sem):
        remote(region, region, sem, sem, {"plane": p_peer(1)}).wait_recv()

    def sent(region, sem):
        remote(region, region, sem, sem, {"plane": p_peer(1)}).wait_send()

    def x_copy(p, target, slot):
        first, count = pieces[p]
        chunk = count // NX
        return remote(
            orb16.at[pl.ds(first + target * chunk, chunk)], in_x[p].at[slot],
            s_x.at[p], r_x.at[p], at_band(target, zh, y),
        )

    def send_x(p):
        for d in far_first(NX):
            start(x_copy(p, x_peer(d), x))
        first, count = pieces[p]
        chunk = count // NX
        in_x[p][x] = orb16[pl.ds(first + x * chunk, chunk), :]

    root = [roots_ref[s] for s in range(STEPS)]
    root_y = [lax.rem(r, NY) for r in root]
    root_z = [lax.rem(r // NY, NZ) for r in root]
    root_x = [r // (NY * NZ) for r in root]

    def send_y(p):
        arrived(in_x[p].at[pl.ds(0, NX - 1)], r_x.at[p])
        for s in range(STEPS):
            sel[p][s] = pick(root_x[s], [in_x[p][k] for k in range(NX)])
        chunk = pieces[p][1] // (NX * NY)
        for d in far_first(NY):
            t = y_peer(d)
            start(remote(
                sel[p].at[:, pl.ds(t * chunk, chunk)], in_y[p].at[y],
                s_y.at[p], r_y.at[p], at_band(x, zh, t),
            ))
        in_y[p][y] = sel[p][:, pl.ds(y * chunk, chunk), :]

    def z_copy(p):
        return remote(
            cand[p], in_z[p], s_z.at[p], r_z.at[p], at_band(x, lax.rem(zh + 1, NZ), y)
        )

    def send_z(p):
        arrived(in_y[p].at[pl.ds(0, NY - 1)], r_y.at[p])
        for s in range(STEPS):
            cand[p][s] = pick(root_y[s], [in_y[p][k, s] for k in range(NY)])
        start(z_copy(p))

    def send_gy(p):
        z_copy(p).wait_recv()
        first, count = pieces[p]
        chunk = count // (NX * NY)
        at = pl.ds(first + (x * NY + y) * chunk, chunk)
        for s in range(STEPS):
            shared[s, at, :] = jnp.where(root_z[s] == zh, cand[p][s], in_z[p][s])
        block = shared.at[:, at]
        for d in far_first(NY):
            start(remote(block, block, s_gy.at[p], r_gy.at[p], at_band(x, zh, y_peer(d))))

    def wait_gy(p):
        first, count = pieces[p]
        chunk = count // (NX * NY)
        arrived(shared.at[:, pl.ds(first + x * NY * chunk, (NY - 1) * chunk)], r_gy.at[p])

    def send_gx(p, s):
        first, count = pieces[p]
        block = shared.at[s, pl.ds(first + x * (count // NX), count // NX)]
        for d in far_first(NX):
            start(remote(block, block, s_gx.at[p, s], r_gx.at[p, s], at_band(x_peer(d), zh, y)))

    def wait_gx(p, s):
        first, count = pieces[p]
        arrived(shared.at[s, pl.ds(first, count // NX * (NX - 1))], r_gx.at[p, s])

    def p_copy(target, slot):
        return remote(part.at[target], in_part.at[slot], s_p, r_p, {"plane": target})

    slots = ids_ref.shape[1]
    piece = -(-slots // (128 * PIECES)) * 128

    def add_part(i):
        if i == 0:
            loads[0].wait()
            loads[1].wait()
            loads[2].wait()
        at = slice(i * piece, min((i + 1) * piece, slots))
        ids = ids_ref[pl.ds(plane, 1), at]
        valid = ids >= 0
        id_h = jnp.where(valid, ids // n, -1)
        id_g = jnp.where(valid, lax.rem(ids, n), 0)
        lane = jnp.where(id_g == 0, 0, jnp.where(id_g <= n // 2, 2 * id_g - 1, 2 * (n - id_g)))
        reverse = (jnp.minimum(id_h, n - id_h) >= edge) | (id_h == edge_row)
        lane = jnp.where(reverse, n - 1 - lane, lane)
        iota = lax.broadcasted_iota(jnp.int32, (n, ids.shape[1]), 0)
        hot_h = (labels[:, 0:1] == id_h) | (labels[:, 1:2] == id_h)
        hot_g = jnp.where(iota == lane, 1.0, 0.0).astype(BF16)
        tile = coulomb[:, at].astype(F32)
        own = tile[:coul_rows]
        for k in range(1, 16 // coul_rows):
            inside = first_row - coul_tile == k * coul_rows
            own = jnp.where(inside, tile[k * coul_rows : (k + 1) * coul_rows], own)
        left = jnp.concatenate(
            [jnp.where(hot_h, own[k : k + 1], 0.0).astype(BF16) for k in range(coul_rows)], 0
        )
        flat = lax.dot_general(
            left, hot_g, (((1,), (1,)), ((), ())), preferred_element_type=F32
        )
        flat_sum[...] = flat if i == 0 else flat_sum[...] + flat

    def send_part():
        for k in range(coul_rows):
            for o in range(n_plane):
                at = slice(k * n + o * width, k * n + (o + 1) * width)
                part[o, k * width : (k + 1) * width, :] = flat_sum[at, :].astype(BF16)
        for t in owners:
            start(p_copy(t, plane))
        in_part[plane] = part[plane]

    coul_y, coul_x = rows // NY, rows // (NX * NY)

    def send_dx():
        arrived(in_part.at[pl.ds(0, n_plane - 1)], r_p)
        summed = in_part[0].astype(F32)
        for o in range(1, n_plane):
            summed = summed + in_part[o].astype(F32)
        at = pl.ds(y * coul_y + x * coul_x, coul_x)
        coul16[at, :] = summed.astype(BF16)
        block = coul16.at[at]
        for d in far_first(NX):
            start(remote(block, block, s_dx, r_dx, at_band(x_peer(d), zh, y)))

    def send_dy():
        arrived(coul16.at[pl.ds(y * coul_y, (NX - 1) * coul_x)], r_dx)
        block = coul16.at[pl.ds(y * coul_y, coul_y)]
        for d in far_first(NY):
            start(remote(block, block, s_dy, r_dy, at_band(x, zh, y_peer(d))))

    def wait_dense():
        arrived(coul16.at[pl.ds(0, (NY - 1) * coul_y)], r_dy)
        dense[...] = coul16[...].astype(F32)

    half = width // GROUPS
    block = per_owner * half
    small_block = block - 2 * half
    own_small = lax.rem(plane, period) == period - 1 if period else False
    n_small = n_plane // period if period else 0

    def sized(small, body):
        if not period:
            body(block)
            return
        pl.when(small)(lambda: body(small_block))
        pl.when(jnp.logical_not(small))(lambda: body(block))

    def of_owners(wait):
        every = block * (n_plane - 1) - 2 * half * n_small
        if not period:
            wait(orb16.at[pl.ds(0, every)])
            return
        pl.when(own_small)(lambda: wait(orb16.at[pl.ds(0, every + 2 * half)]))
        pl.when(jnp.logical_not(own_small))(lambda: wait(orb16.at[pl.ds(0, every)]))

    def of_own(wait):
        sized(own_small, lambda count: wait(orb16.at[pl.ds(0, count * (n_plane - 1))]))

    def send_block(from_ref, to_ref, count, sems, target):
        at = pl.ds(0, count)
        start(remote(from_ref.at[at], to_ref.at[at], sems[0], sems[1], {"plane": target}))

    def wait_group(g, s, i):
        if g == 0:
            wait_gx(i, s)
        elif i == 0:
            wait_gx(2, s)

    def forward(g, s):
        both = wide[:n, :]
        first, second = slim[:n_packed, :], slim[n : n + n_packed, :]
        in_first = lax.broadcasted_iota(jnp.int32, (n_packed, n), 1) < labels[:n_packed, 2:3]
        group = 4

        for i in range(half // group):
            wait_group(g, s, i)
            at = slice(g * rows_g + i * group * n, g * rows_g + (i + 1) * group * n)
            pair = (orb[at, :] * shared[s, at, :].astype(F32)).astype(BF16)
            along = dot(pair, both).astype(BF16)
            planes = [along[k * n : (k + 1) * n] for k in range(group)]
            from_first = dot(first, jnp.concatenate([plane_k[:, :n] for plane_k in planes], 1))
            from_second = dot(second, jnp.concatenate([plane_k[:, n:] for plane_k in planes], 1))
            for k in range(group):
                at = slice(k * n, (k + 1) * n)
                packed = jnp.where(in_first, from_first[:, at], from_second[:, at])
                grid_a[pl.ds(i * group + k, n_packed, stride=half), :] = packed
        for t in owners:
            send_f[s, g, t] = grid_a[pl.ds(pl.multiple_of(t * block, block), block), :].astype(BF16)
            small = lax.rem(t, period) == period - 1 if period else False
            sems = (s_f.at[g, s], r_f.at[g, s])
            sized(small, lambda count: send_block(
                send_f.at[s, g, t], recv_f.at[s, g, plane], count, sems, t))
        at = pl.ds(pl.multiple_of(plane * block, block), block)
        recv_f[s, g, plane] = grid_a[at, :].astype(BF16)

    def middle(s):
        for g in range(GROUPS):
            of_own(lambda region: arrived(region, r_f.at[g, s]))
        twin, cas = wide[n : 3 * n, :], slim[4 * n : 5 * n, :]
        pairs = per_owner // 2
        for first_pair in range(0, pairs, 2):
            js = range(first_pair, min(first_pair + 2, pairs))
            at = [slice(j * 2 * half, (j + 1) * 2 * half) for j in js]
            sticks = [recv_f[s, :, :, a, :].reshape(2 * n, n) for a in at]
            if period and js[-1] == pairs - 1:
                sticks[-1] = jnp.where(own_small, jnp.zeros_like(sticks[-1]), sticks[-1])
            spectrum = dot(twin, jnp.concatenate(sticks, 1))
            scaled = []
            for k, j in enumerate(js):
                for h in range(2):
                    coul = dense[pl.ds(2 * j + h, n, stride=width), :]
                    part_h = spectrum[h * n : (h + 1) * n, k * n : (k + 1) * n]
                    scaled.append((part_h * coul).astype(BF16))
            back = dot(cas, jnp.concatenate(scaled, 1))
            for k in range(len(js)):
                two = [
                    back[:, (2 * k + h) * n : (2 * k + h + 1) * n].reshape(n_plane, GROUPS, half, n)
                    for h in range(2)
                ]
                for g in range(GROUPS):
                    for q in range(n_plane):
                        both = jnp.concatenate([two[0][q, g], two[1][q, g]], 0)
                        send_b[s, g, q, at[k], :] = both.astype(BF16)
        for g in range(GROUPS):
            def send_all(count):
                for t in owners:
                    sems = (s_b.at[g, s], r_b.at[g, s])
                    send_block(send_b.at[s, g, t], recv_b.at[s, g, plane], count, sems, t)

            sized(own_small, send_all)
            recv_b[s, g, plane] = send_b[s, g, plane]

    def inverse(g, s):
        of_owners(lambda region: arrived(region, r_b.at[g, s]))
        first, second = wide[3 * n :, :n], wide[3 * n :, n:]
        both = slim[2 * n : 4 * n, :]
        in_first = lax.broadcasted_iota(jnp.int32, (n, n), 1) < labels[:, 2:3]
        grid_b[: n_packed * half, :] = recv_b[s, g].reshape(n_packed * half, n).astype(F32)
        group = 4

        for i in range(half // group):
            packed = [grid_b[pl.ds(i * group + k, n, stride=half), :] for k in range(group)]
            own = [jnp.where(in_first, one, 0.0).astype(BF16) for one in packed]
            other = [jnp.where(in_first, 0.0, one).astype(BF16) for one in packed]
            from_first = dot(first, jnp.concatenate(own, 1))
            from_second = dot(second, jnp.concatenate(other, 1))
            inverse_y = []
            for k in range(group):
                at = slice(k * n, (k + 1) * n)
                inverse_y.append(jnp.concatenate([from_first[:, at], from_second[:, at]], 1).astype(BF16))
            at = slice(g * rows_g + i * group * n, g * rows_g + (i + 1) * group * n)
            term = dot(jnp.concatenate(inverse_y, 0), both) * shared[s, at, :].astype(F32)
            if s == 0:
                total[at, :] = term
            else:
                out_ref[at, :] = (total[at, :] + term).astype(BF16)

    send_x(0)
    round_piece(1)
    send_x(1)
    round_piece(2)
    send_x(2)
    add_part(0)
    add_part(1)
    send_y(0)
    send_y(1)
    for i in range(2, PIECES):
        add_part(i)
    send_z(0)
    send_y(2)
    send_z(1)
    send_part()
    send_gy(0)
    send_z(2)
    send_gy(1)
    loads[3].wait()
    loads[4].wait()
    wait_gy(0)
    send_gx(0, 0)
    wait_gy(1)
    send_gx(1, 0)
    send_gy(2)
    send_gx(0, 1)
    send_gx(1, 1)
    send_dx()
    forward(0, 0)
    wait_gy(2)
    send_gx(2, 0)
    send_gx(2, 1)
    send_dy()
    forward(0, 1)
    forward(1, 0)
    forward(1, 1)
    for p, (_, count) in enumerate(pieces):
        sent(in_x[p].at[pl.ds(0, NX - 1)], s_x.at[p])
        sent(in_y[p].at[pl.ds(0, NY - 1)], s_y.at[p])
        sent(in_z[p], s_z.at[p])
        sent(shared.at[:, pl.ds(0, (NY - 1) * (count // (NX * NY)))], s_gy.at[p])
        for s in range(STEPS):
            sent(shared.at[s, pl.ds(0, (NX - 1) * (count // NX))], s_gx.at[p, s])
    sent(in_part.at[pl.ds(0, n_plane - 1)], s_p)
    grid_b[n_packed * half :, :] = jnp.zeros(((n - n_packed) * half, n), F32)
    for q in range(n_plane):
        if period and q % period == period - 1:
            recv_b[:, :, q, small_block:, :] = jnp.zeros((STEPS, GROUPS, 2 * half, n), BF16)
    wait_dense()
    middle(0)
    sent(coul16.at[pl.ds(0, (NY - 1) * coul_y)], s_dy)
    sent(coul16.at[pl.ds(0, (NX - 1) * coul_x)], s_dx)
    middle(1)
    for g in range(GROUPS):
        for s in range(STEPS):
            of_owners(lambda region: sent(region, s_f.at[g, s]))
    inverse(0, 0)
    inverse(1, 0)
    inverse(0, 1)
    inverse(1, 1)
    for g in range(GROUPS):
        for s in range(STEPS):
            of_own(lambda region: sent(region, s_b.at[g, s]))


def on_device(orbitals, coulomb, stick_lists, roots):
    _, width, n, _ = orbitals.shape
    n_plane = n // width
    rows = width * n
    rows_g = rows // GROUPS
    counts = [count for _, count in broadcast_pieces(rows)]
    coul_block = n // (NX * NY) * width
    per_owner = packing(n, n_plane)[1]
    wide, slim, labels = tables(n, n_plane)
    hbm = pl.BlockSpec(memory_space=pl.ANY)
    vmem = pl.BlockSpec(memory_space=pltpu.VMEM)
    dma = pltpu.SemaphoreType.DMA

    def pair_of_sems(*shape):
        return [dma(shape), dma(shape)]

    gs = (GROUPS, STEPS)
    spectra = pltpu.VMEM((STEPS, GROUPS, n_plane, per_owner * width // GROUPS, n), BF16)
    out = pl.pallas_call(
        functools.partial(kernel, n, n_plane),
        out_shape=jax.ShapeDtypeStruct((rows, n), BF16),
        in_specs=[pl.BlockSpec(memory_space=pltpu.SMEM)] + [hbm] * 6,
        out_specs=vmem,
        scratch_shapes=[
            pltpu.VMEM((rows, n), F32),
            pltpu.VMEM(wide.shape, BF16),
            pltpu.VMEM(slim.shape, BF16),
            pltpu.VMEM(labels.shape, jnp.int32),
            pltpu.VMEM((16, coulomb.shape[1]), BF16),
            pltpu.VMEM(stick_lists.shape, jnp.int32),
            pltpu.VMEM((rows, n), BF16),
            *[pltpu.VMEM((NX, count // NX, n), BF16) for count in counts],
            *[pltpu.VMEM((STEPS, count // NX, n), BF16) for count in counts],
            *[pltpu.VMEM((NY, STEPS, count // (NX * NY), n), BF16) for count in counts],
            *[pltpu.VMEM((STEPS, count // (NX * NY), n), BF16) for count in counts * 2],
            pltpu.VMEM((STEPS, rows, n), BF16),
            pltpu.VMEM((n // (NX * NY) * n, n), F32),
            pltpu.VMEM((n_plane, coul_block, n), BF16),
            pltpu.VMEM((n_plane, coul_block, n), BF16),
            pltpu.VMEM((rows, n), BF16),
            pltpu.VMEM((rows, n), F32),
            pltpu.VMEM((rows_g, n), F32),
            pltpu.VMEM((rows_g, n), F32),
            spectra, spectra, spectra, spectra,
            pltpu.VMEM((rows, n), F32),
            dma((len(counts),)),
            dma((5,)),
            *pair_of_sems(len(counts)),
            *pair_of_sems(len(counts)),
            *pair_of_sems(len(counts)),
            *pair_of_sems(len(counts)),
            *pair_of_sems(len(counts), STEPS),
            dma, dma, dma, dma, dma, dma,
            *pair_of_sems(*gs),
            *pair_of_sems(*gs),
        ],
        compiler_params=pltpu.CompilerParams(
            collective_id=0, has_side_effects=True, vmem_limit_bytes=57 * 1024 * 1024
        ),
        name="exchange",
    )(
        roots, orbitals.reshape(rows, n),
        wide, slim, labels, coulomb, stick_lists,
    )
    return out.reshape(1, width, n, n)


def solution(mesh):
    in_specs = (P("band", "plane", None, None), P(None, "plane"), P(), P())
    out_specs = P("band", "plane", None, None)
    return jax.shard_map(
        on_device, mesh=mesh, in_specs=in_specs, out_specs=out_specs, check_vma=False
    )
```

```python
import functools
import math

import jax
import jax.numpy as jnp
import numpy as np
from jax import lax
from jax.experimental import pallas as pl
from jax.experimental.pallas import tpu as pltpu
from jax.sharding import PartitionSpec as P

NX, NZ, NY = 4, 2, 8
STICKS = 12288
GROUPS = 2
STEPS = 2
PIECES = 3
MESH = pl.DeviceIdType.MESH
F32, BF16 = jnp.float32, jnp.bfloat16


def cas_table(n):
    k = np.arange(n)
    angles = 2.0 * math.pi / n * ((k[:, None] * k[None, :]) % n)
    return np.asarray(np.cos(angles) + np.sin(angles), np.float32)


def pair_table(n, width):
    cas = cas_table(n)
    half = width // GROUPS
    table = np.zeros((2, n, GROUPS, n // width, 2, half), np.float32)
    by_x = cas.reshape(n, n // width, GROUPS, half).transpose(0, 2, 1, 3)
    for h in range(2):
        table[h, :, :, :, h, :] = by_x
    return table.reshape(2 * n, 2 * n)


def packing(n, n_plane):
    signed = np.minimum(np.arange(n), n - np.arange(n))
    squares = signed[:, None] ** 2 + signed[None, :] ** 2
    kept = (squares <= np.sort(squares.reshape(-1))[STICKS - 1]).sum(1)
    best = None
    for t in range(1, n // 2 + 1):
        for extra in ([], [n - t + 1]):
            second = [h for h in range(n) if kept[h] and (signed[h] >= t or h in extra)]
            firsts = [h for h in range(n) if kept[h] and h not in second]
            free, mate = sorted(firsts, key=lambda h: -kept[h]), {}
            for h in sorted(second, key=lambda h: -kept[h]):
                host = next((f for f in free if kept[f] + kept[h] <= n), None)
                if host is None:
                    break
                free.remove(host)
                mate[host] = h
            else:
                if best is None or len(firsts) < len(best[0]):
                    best = firsts, mate, t, extra
    firsts, mate, t, extra = best
    pairs = -(-len(firsts) // 2)
    per_owner = -(-pairs // n_plane) * 2
    n_small = per_owner // 2 * n_plane - pairs
    period = n_plane // n_small if n_small and n_plane % n_small == 0 else 0
    table = -np.ones((per_owner * n_plane, 3), np.int64)
    left = list(firsts)
    for owner in range(n_plane):
        count = per_owner - 2 if period and owner % period == period - 1 else per_owner
        for k in range(min(count, len(left))):
            h = left.pop(0)
            table[owner * per_owner + k] = h, mate.get(h, -1), kept[h]
    return table, per_owner, period, t, (extra or [-1])[0]


def tables(n, n_plane):
    width = n // n_plane
    cas = cas_table(n)
    rows, per_owner = packing(n, n_plane)[:2]
    order = sorted(range(n), key=lambda g: (min(g, n - g), g > n // 2))
    both = np.concatenate([cas[:, order], cas[:, order[::-1]]], 1)
    first, second = np.zeros((n, n), np.float32), np.zeros((n, n), np.float32)
    for row, (h, other, _) in enumerate(rows):
        if h >= 0:
            first[row] = cas[h]
        if other >= 0:
            second[row] = cas[other]
    wide = np.concatenate([both, pair_table(n, width), np.concatenate([first.T, second.T], 1) / n], 0)
    slim = np.concatenate([first, second, both.T / n, cas / n], 0)
    labels = np.full((n, 128), -7, np.int32)
    for row, (h, other, length) in enumerate(rows):
        place = row // per_owner * width + row % per_owner
        labels[place, 0] = h if h >= 0 else -7
        labels[place, 1] = other if other >= 0 else -7
    labels[:, 2] = n
    labels[: len(rows), 2] = np.where(rows[:, 2] < 0, n, rows[:, 2])
    return jnp.asarray(wide).astype(BF16), jnp.asarray(slim).astype(BF16), jnp.asarray(labels)


def dot(a, b):
    return jnp.dot(a, b, preferred_element_type=F32)


def broadcast_pieces(rows):
    return [(0, rows // 4), (rows // 4, rows // 4), (rows // 2, rows // 2)]


def far_first(count):
    return sorted(range(1, count), key=lambda d: -min(d, count - d))


def pick(index, values):
    out = values[0]
    for k in range(1, len(values)):
        out = jnp.where(index == k, values[k], out)
    return out


def remote(src, dst, send_sem, recv_sem, device):
    return pltpu.make_async_remote_copy(
        src_ref=src, dst_ref=dst, send_sem=send_sem, recv_sem=recv_sem,
        device_id=device, device_id_type=MESH,
    )


def kernel(
    n, n_plane,
    roots_ref, orb_hbm, wide_hbm, slim_hbm, labels_hbm, coulomb_hbm, ids_hbm, out_ref,
    orb, wide, slim, labels, coulomb, ids_ref,
    orb16, in_x0, in_x1, in_x2, sel0, sel1, sel2, in_y0, in_y1, in_y2,
    cand0, cand1, cand2, in_z0, in_z1, in_z2, shared,
    flat_sum, part, in_part, coul16, dense, grid_a, grid_b, send_f, recv_f, send_b, recv_b, total,
    s_orb, s_in, s_x, r_x, s_y, r_y, s_z, r_z, s_gy, r_gy, s_gx, r_gx,
    s_p, r_p, s_dy, r_dy, s_dx, r_dx, s_f, r_f, s_b, r_b,
):
    width = n // n_plane
    rows = width * n
    rows_g = rows // GROUPS
    _, per_owner, period, edge, edge_row = packing(n, n_plane)
    n_packed = per_owner * n_plane
    in_x, sel, in_y = [in_x0, in_x1, in_x2], [sel0, sel1, sel2], [in_y0, in_y1, in_y2]
    cand, in_z = [cand0, cand1, cand2], [in_z0, in_z1, in_z2]
    pieces = broadcast_pieces(rows)
    band, plane = lax.axis_index("band"), lax.axis_index("plane")
    y = lax.rem(band, NY)
    zh = lax.rem(band // NY, NZ)
    x = band // (NY * NZ)

    def at_band(bx, bz, by):
        return {"band": (bx * NZ + bz) * NY + by}

    def x_peer(d):
        return lax.rem(x + d, NX)

    def y_peer(d):
        return lax.rem(y + d, NY)

    def p_peer(d):
        return lax.rem(plane + d, n_plane)

    bits = [lax.rem(plane // (1 << k), 2) for k in range(n_plane.bit_length() - 1)]
    owners = []
    for flip in sorted(range(1, n_plane), key=lambda f: (-(f >> 1), f)):
        t = 0
        for k, bit in enumerate(bits):
            t = t + (1 << k) * (1 - bit if flip >> k & 1 else bit)
        owners.append(t)

    barrier = pltpu.get_barrier_semaphore()
    peers = [at_band(x_peer(d), zh, y) for d in far_first(NX)]
    peers += [at_band(x, zh, y_peer(d)) for d in far_first(NY)]
    peers += [at_band(x, lax.rem(zh + d, NZ), y) for d in range(1, NZ)]
    peers += [{"plane": p_peer(d)} for d in range(1, n_plane)]
    for peer in peers:
        pl.semaphore_signal(barrier, inc=1, device_id=peer, device_id_type=MESH)

    coul_rows = n // (NX * NY)
    first_row = (y * NX + x) * coul_rows
    coul_tile = pl.multiple_of(first_row // 16 * 16, 16)
    orb_loads = [
        pltpu.make_async_copy(orb_hbm.at[pl.ds(*at)], orb.at[pl.ds(*at)], s_orb.at[p])
        for p, at in enumerate(pieces)
    ]
    loads = [
        pltpu.make_async_copy(coulomb_hbm.at[pl.ds(coul_tile, 16)], coulomb, s_in.at[0]),
        pltpu.make_async_copy(ids_hbm, ids_ref, s_in.at[1]),
        pltpu.make_async_copy(labels_hbm, labels, s_in.at[2]),
        pltpu.make_async_copy(slim_hbm, slim, s_in.at[3]),
        pltpu.make_async_copy(wide_hbm, wide, s_in.at[4]),
    ]
    for load in orb_loads + loads:
        load.start()

    def round_piece(p):
        first, count = pieces[p]
        orb_loads[p].wait()
        orb16[first : first + count, :] = orb[first : first + count, :].astype(BF16)

    round_piece(0)
    pl.semaphore_wait(barrier, len(peers))

    def start(copy):
        copy.start()

    def arrived(region, sem):
        remote(region, region, sem, sem, {"plane": p_peer(1)}).wait_recv()

    def sent(region, sem):
        remote(region, region, sem, sem, {"plane": p_peer(1)}).wait_send()

    def x_copy(p, target, slot):
        first, count = pieces[p]
        chunk = count // NX
        return remote(
            orb16.at[pl.ds(first + target * chunk, chunk)], in_x[p].at[slot],
            s_x.at[p], r_x.at[p], at_band(target, zh, y),
        )

    def send_x(p):
        for d in far_first(NX):
            start(x_copy(p, x_peer(d), x))
        first, count = pieces[p]
        chunk = count // NX
        in_x[p][x] = orb16[pl.ds(first + x * chunk, chunk), :]

    root = [roots_ref[s] for s in range(STEPS)]
    root_y = [lax.rem(r, NY) for r in root]
    root_z = [lax.rem(r // NY, NZ) for r in root]
    root_x = [r // (NY * NZ) for r in root]

    def send_y(p):
        arrived(in_x[p].at[pl.ds(0, NX - 1)], r_x.at[p])
        for s in range(STEPS):
            sel[p][s] = pick(root_x[s], [in_x[p][k] for k in range(NX)])
        chunk = pieces[p][1] // (NX * NY)
        for d in far_first(NY):
            t = y_peer(d)
            start(remote(
                sel[p].at[:, pl.ds(t * chunk, chunk)], in_y[p].at[y],
                s_y.at[p], r_y.at[p], at_band(x, zh, t),
            ))
        in_y[p][y] = sel[p][:, pl.ds(y * chunk, chunk), :]

    def z_copy(p):
        return remote(
            cand[p], in_z[p], s_z.at[p], r_z.at[p], at_band(x, lax.rem(zh + 1, NZ), y)
        )

    def send_z(p):
        arrived(in_y[p].at[pl.ds(0, NY - 1)], r_y.at[p])
        for s in range(STEPS):
            cand[p][s] = pick(root_y[s], [in_y[p][k, s] for k in range(NY)])
        start(z_copy(p))

    def send_gy(p):
        z_copy(p).wait_recv()
        first, count = pieces[p]
        chunk = count // (NX * NY)
        at = pl.ds(first + (x * NY + y) * chunk, chunk)
        for s in range(STEPS):
            shared[s, at, :] = jnp.where(root_z[s] == zh, cand[p][s], in_z[p][s])
        block = shared.at[:, at]
        for d in far_first(NY):
            start(remote(block, block, s_gy.at[p], r_gy.at[p], at_band(x, zh, y_peer(d))))

    def wait_gy(p):
        first, count = pieces[p]
        chunk = count // (NX * NY)
        arrived(shared.at[:, pl.ds(first + x * NY * chunk, (NY - 1) * chunk)], r_gy.at[p])

    def send_gx(p, s):
        first, count = pieces[p]
        block = shared.at[s, pl.ds(first + x * (count // NX), count // NX)]
        for d in far_first(NX):
            start(remote(block, block, s_gx.at[p, s], r_gx.at[p, s], at_band(x_peer(d), zh, y)))

    def wait_gx(p, s):
        first, count = pieces[p]
        arrived(shared.at[s, pl.ds(first, count // NX * (NX - 1))], r_gx.at[p, s])

    def p_copy(target, slot):
        return remote(part.at[target], in_part.at[slot], s_p, r_p, {"plane": target})

    slots = ids_ref.shape[1]
    piece = -(-slots // (128 * PIECES)) * 128

    def add_part(i):
        if i == 0:
            loads[0].wait()
            loads[1].wait()
            loads[2].wait()
        at = slice(i * piece, min((i + 1) * piece, slots))
        ids = ids_ref[pl.ds(plane, 1), at]
        valid = ids >= 0
        id_h = jnp.where(valid, ids // n, -1)
        id_g = jnp.where(valid, lax.rem(ids, n), 0)
        lane = jnp.where(id_g == 0, 0, jnp.where(id_g <= n // 2, 2 * id_g - 1, 2 * (n - id_g)))
        reverse = (jnp.minimum(id_h, n - id_h) >= edge) | (id_h == edge_row)
        lane = jnp.where(reverse, n - 1 - lane, lane)
        iota = lax.broadcasted_iota(jnp.int32, (n, ids.shape[1]), 0)
        hot_h = (labels[:, 0:1] == id_h) | (labels[:, 1:2] == id_h)
        hot_g = jnp.where(iota == lane, 1.0, 0.0).astype(BF16)
        tile = coulomb[:, at].astype(F32)
        own = tile[:coul_rows]
        for k in range(1, 16 // coul_rows):
            inside = first_row - coul_tile == k * coul_rows
            own = jnp.where(inside, tile[k * coul_rows : (k + 1) * coul_rows], own)
        left = jnp.concatenate(
            [jnp.where(hot_h, own[k : k + 1], 0.0).astype(BF16) for k in range(coul_rows)], 0
        )
        flat = lax.dot_general(
            left, hot_g, (((1,), (1,)), ((), ())), preferred_element_type=F32
        )
        flat_sum[...] = flat if i == 0 else flat_sum[...] + flat

    def send_part():
        for k in range(coul_rows):
            for o in range(n_plane):
                at = slice(k * n + o * width, k * n + (o + 1) * width)
                part[o, k * width : (k + 1) * width, :] = flat_sum[at, :].astype(BF16)
        for t in owners:
            start(p_copy(t, plane))
        in_part[plane] = part[plane]

    coul_y, coul_x = rows // NY, rows // (NX * NY)

    def send_dx():
        arrived(in_part.at[pl.ds(0, n_plane - 1)], r_p)
        summed = in_part[0].astype(F32)
        for o in range(1, n_plane):
            summed = summed + in_part[o].astype(F32)
        at = pl.ds(y * coul_y + x * coul_x, coul_x)
        coul16[at, :] = summed.astype(BF16)
        block = coul16.at[at]
        for d in far_first(NX):
            start(remote(block, block, s_dx, r_dx, at_band(x_peer(d), zh, y)))

    def send_dy():
        arrived(coul16.at[pl.ds(y * coul_y, (NX - 1) * coul_x)], r_dx)
        block = coul16.at[pl.ds(y * coul_y, coul_y)]
        for d in far_first(NY):
            start(remote(block, block, s_dy, r_dy, at_band(x, zh, y_peer(d))))

    def wait_dense():
        arrived(coul16.at[pl.ds(0, (NY - 1) * coul_y)], r_dy)
        dense[...] = coul16[...].astype(F32)

    half = width // GROUPS
    block = per_owner * half
    small_block = block - 2 * half
    own_small = lax.rem(plane, period) == period - 1 if period else False
    n_small = n_plane // period if period else 0

    def sized(small, body):
        if not period:
            body(block)
            return
        pl.when(small)(lambda: body(small_block))
        pl.when(jnp.logical_not(small))(lambda: body(block))

    def of_owners(wait):
        every = block * (n_plane - 1) - 2 * half * n_small
        if not period:
            wait(orb16.at[pl.ds(0, every)])
            return
        pl.when(own_small)(lambda: wait(orb16.at[pl.ds(0, every + 2 * half)]))
        pl.when(jnp.logical_not(own_small))(lambda: wait(orb16.at[pl.ds(0, every)]))

    def of_own(wait):
        sized(own_small, lambda count: wait(orb16.at[pl.ds(0, count * (n_plane - 1))]))

    def send_block(from_ref, to_ref, count, sems, target):
        at = pl.ds(0, count)
        start(remote(from_ref.at[at], to_ref.at[at], sems[0], sems[1], {"plane": target}))

    def wait_group(g, s, i):
        if g == 0:
            wait_gx(i, s)
        elif i == 0:
            wait_gx(2, s)

    def forward(g, s):
        both = wide[:n, :]
        first, second = slim[:n_packed, :], slim[n : n + n_packed, :]
        in_first = lax.broadcasted_iota(jnp.int32, (n_packed, n), 1) < labels[:n_packed, 2:3]
        group = 4

        for i in range(half // group):
            wait_group(g, s, i)
            at = slice(g * rows_g + i * group * n, g * rows_g + (i + 1) * group * n)
            pair = (orb[at, :] * shared[s, at, :].astype(F32)).astype(BF16)
            along = dot(pair, both).astype(BF16)
            planes = [along[k * n : (k + 1) * n] for k in range(group)]
            from_first = dot(first, jnp.concatenate([plane_k[:, :n] for plane_k in planes], 1))
            from_second = dot(second, jnp.concatenate([plane_k[:, n:] for plane_k in planes], 1))
            for k in range(group):
                at = slice(k * n, (k + 1) * n)
                packed = jnp.where(in_first, from_first[:, at], from_second[:, at])
                grid_a[pl.ds(i * group + k, n_packed, stride=half), :] = packed
        for t in owners:
            send_f[s, g, t] = grid_a[pl.ds(pl.multiple_of(t * block, block), block), :].astype(BF16)
            small = lax.rem(t, period) == period - 1 if period else False
            sems = (s_f.at[g, s], r_f.at[g, s])
            sized(small, lambda count: send_block(
                send_f.at[s, g, t], recv_f.at[s, g, plane], count, sems, t))
        at = pl.ds(pl.multiple_of(plane * block, block), block)
        recv_f[s, g, plane] = grid_a[at, :].astype(BF16)

    def middle(s):
        for g in range(GROUPS):
            of_own(lambda region: arrived(region, r_f.at[g, s]))
        twin, cas = wide[n : 3 * n, :], slim[4 * n : 5 * n, :]
        pairs = per_owner // 2
        for first_pair in range(0, pairs, 2):
            js = range(first_pair, min(first_pair + 2, pairs))
            at = [slice(j * 2 * half, (j + 1) * 2 * half) for j in js]
            sticks = [recv_f[s, :, :, a, :].reshape(2 * n, n) for a in at]
            if period and js[-1] == pairs - 1:
                sticks[-1] = jnp.where(own_small, jnp.zeros_like(sticks[-1]), sticks[-1])
            spectrum = dot(twin, jnp.concatenate(sticks, 1))
            scaled = []
            for k, j in enumerate(js):
                for h in range(2):
                    coul = dense[pl.ds(2 * j + h, n, stride=width), :]
                    part_h = spectrum[h * n : (h + 1) * n, k * n : (k + 1) * n]
                    scaled.append((part_h * coul).astype(BF16))
            back = dot(cas, jnp.concatenate(scaled, 1))
            for k in range(len(js)):
                two = [
                    back[:, (2 * k + h) * n : (2 * k + h + 1) * n].reshape(n_plane, GROUPS, half, n)
                    for h in range(2)
                ]
                for g in range(GROUPS):
                    for q in range(n_plane):
                        both = jnp.concatenate([two[0][q, g], two[1][q, g]], 0)
                        send_b[s, g, q, at[k], :] = both.astype(BF16)
        for g in range(GROUPS):
            def send_all(count):
                for t in owners:
                    sems = (s_b.at[g, s], r_b.at[g, s])
                    send_block(send_b.at[s, g, t], recv_b.at[s, g, plane], count, sems, t)

            sized(own_small, send_all)
            recv_b[s, g, plane] = send_b[s, g, plane]

    def inverse(g, s):
        of_owners(lambda region: arrived(region, r_b.at[g, s]))
        first, second = wide[3 * n :, :n], wide[3 * n :, n:]
        both = slim[2 * n : 4 * n, :]
        in_first = lax.broadcasted_iota(jnp.int32, (n, n), 1) < labels[:, 2:3]
        grid_b[: n_packed * half, :] = recv_b[s, g].reshape(n_packed * half, n).astype(F32)
        group = 4

        for i in range(half // group):
            packed = [grid_b[pl.ds(i * group + k, n, stride=half), :] for k in range(group)]
            own = [jnp.where(in_first, one, 0.0).astype(BF16) for one in packed]
            other = [jnp.where(in_first, 0.0, one).astype(BF16) for one in packed]
            from_first = dot(first, jnp.concatenate(own, 1))
            from_second = dot(second, jnp.concatenate(other, 1))
            inverse_y = []
            for k in range(group):
                at = slice(k * n, (k + 1) * n)
                inverse_y.append(jnp.concatenate([from_first[:, at], from_second[:, at]], 1).astype(BF16))
            at = slice(g * rows_g + i * group * n, g * rows_g + (i + 1) * group * n)
            term = dot(jnp.concatenate(inverse_y, 0), both) * shared[s, at, :].astype(F32)
            if s == 0:
                total[at, :] = term
            else:
                out_ref[at, :] = (total[at, :] + term).astype(BF16)

    send_x(0)
    round_piece(1)
    send_x(1)
    round_piece(2)
    send_x(2)
    add_part(0)
    send_y(0)
    send_y(1)
    add_part(1)
    send_z(0)
    send_y(2)
    send_z(1)
    for i in range(2, PIECES):
        add_part(i)
    send_gy(0)
    send_part()
    send_gy(1)
    send_z(2)
    loads[3].wait()
    loads[4].wait()
    wait_gy(0)
    send_gx(0, 0)
    wait_gy(1)
    send_gx(1, 0)
    send_gy(2)
    send_gx(0, 1)
    send_gx(1, 1)
    send_dx()
    forward(0, 0)
    wait_gy(2)
    send_gx(2, 0)
    send_gx(2, 1)
    send_dy()
    forward(0, 1)
    forward(1, 0)
    forward(1, 1)
    for p, (_, count) in enumerate(pieces):
        sent(in_x[p].at[pl.ds(0, NX - 1)], s_x.at[p])
        sent(in_y[p].at[pl.ds(0, NY - 1)], s_y.at[p])
        sent(in_z[p], s_z.at[p])
        sent(shared.at[:, pl.ds(0, (NY - 1) * (count // (NX * NY)))], s_gy.at[p])
        for s in range(STEPS):
            sent(shared.at[s, pl.ds(0, (NX - 1) * (count // NX))], s_gx.at[p, s])
    sent(in_part.at[pl.ds(0, n_plane - 1)], s_p)
    grid_b[n_packed * half :, :] = jnp.zeros(((n - n_packed) * half, n), F32)
    for q in range(n_plane):
        if period and q % period == period - 1:
            recv_b[:, :, q, small_block:, :] = jnp.zeros((STEPS, GROUPS, 2 * half, n), BF16)
    wait_dense()
    middle(0)
    sent(coul16.at[pl.ds(0, (NY - 1) * coul_y)], s_dy)
    sent(coul16.at[pl.ds(0, (NX - 1) * coul_x)], s_dx)
    middle(1)
    for g in range(GROUPS):
        for s in range(STEPS):
            of_owners(lambda region: sent(region, s_f.at[g, s]))
    inverse(0, 0)
    inverse(1, 0)
    inverse(0, 1)
    inverse(1, 1)
    for g in range(GROUPS):
        for s in range(STEPS):
            of_own(lambda region: sent(region, s_b.at[g, s]))


def hand_on(from_ref, to_ref, sem):
    copy = pltpu.make_async_copy(from_ref, to_ref, sem)
    copy.start()
    copy.wait()


def on_device(orbitals, coulomb, stick_lists, roots):
    _, width, n, _ = orbitals.shape
    n_plane = n // width
    rows = width * n
    rows_g = rows // GROUPS
    counts = [count for _, count in broadcast_pieces(rows)]
    coul_block = n // (NX * NY) * width
    per_owner = packing(n, n_plane)[1]
    wide, slim, labels = tables(n, n_plane)
    hbm = pl.BlockSpec(memory_space=pl.ANY)
    vmem = pl.BlockSpec(memory_space=pltpu.VMEM)
    dma = pltpu.SemaphoreType.DMA

    def pair_of_sems(*shape):
        return [dma(shape), dma(shape)]

    gs = (GROUPS, STEPS)
    spectra = pltpu.VMEM((STEPS, GROUPS, n_plane, per_owner * width // GROUPS, n), BF16)
    out = pl.pallas_call(
        functools.partial(kernel, n, n_plane),
        out_shape=jax.ShapeDtypeStruct((rows, n), BF16),
        in_specs=[pl.BlockSpec(memory_space=pltpu.SMEM)] + [hbm] * 6,
        out_specs=vmem,
        scratch_shapes=[
            pltpu.VMEM((rows, n), F32),
            pltpu.VMEM(wide.shape, BF16),
            pltpu.VMEM(slim.shape, BF16),
            pltpu.VMEM(labels.shape, jnp.int32),
            pltpu.VMEM((16, coulomb.shape[1]), BF16),
            pltpu.VMEM(stick_lists.shape, jnp.int32),
            pltpu.VMEM((rows, n), BF16),
            *[pltpu.VMEM((NX, count // NX, n), BF16) for count in counts],
            *[pltpu.VMEM((STEPS, count // NX, n), BF16) for count in counts],
            *[pltpu.VMEM((NY, STEPS, count // (NX * NY), n), BF16) for count in counts],
            *[pltpu.VMEM((STEPS, count // (NX * NY), n), BF16) for count in counts * 2],
            pltpu.VMEM((STEPS, rows, n), BF16),
            pltpu.VMEM((n // (NX * NY) * n, n), F32),
            pltpu.VMEM((n_plane, coul_block, n), BF16),
            pltpu.VMEM((n_plane, coul_block, n), BF16),
            pltpu.VMEM((rows, n), BF16),
            pltpu.VMEM((rows, n), F32),
            pltpu.VMEM((rows_g, n), F32),
            pltpu.VMEM((rows_g, n), F32),
            spectra, spectra, spectra, spectra,
            pltpu.VMEM((rows, n), F32),
            dma((len(counts),)),
            dma((5,)),
            *pair_of_sems(len(counts)),
            *pair_of_sems(len(counts)),
            *pair_of_sems(len(counts)),
            *pair_of_sems(len(counts)),
            *pair_of_sems(len(counts), STEPS),
            dma, dma, dma, dma, dma, dma,
            *pair_of_sems(*gs),
            *pair_of_sems(*gs),
        ],
        compiler_params=pltpu.CompilerParams(
            collective_id=0, has_side_effects=True, vmem_limit_bytes=57 * 1024 * 1024
        ),
        name="exchange",
    )(
        roots, orbitals.reshape(rows, n),
        wide, slim, labels, coulomb, stick_lists,
    )
    out = pl.pallas_call(
        hand_on,
        out_shape=jax.ShapeDtypeStruct((rows, n), BF16),
        in_specs=[hbm],
        out_specs=hbm,
        scratch_shapes=[dma],
        compiler_params=pltpu.CompilerParams(vmem_limit_bytes=57 * 1024 * 1024),
        name="hand_on",
    )(out)
    return out.reshape(1, width, n, n)


def solution(mesh):
    in_specs = (P("band", "plane", None, None), P(None, "plane"), P(), P())
    out_specs = P("band", "plane", None, None)
    return jax.shard_map(
        on_device, mesh=mesh, in_specs=in_specs, out_specs=out_specs, check_vma=False
    )
```

```python
import functools
import math

import jax
import jax.numpy as jnp
import numpy as np
from jax import lax
from jax.experimental import pallas as pl
from jax.experimental.pallas import tpu as pltpu
from jax.sharding import PartitionSpec as P

NX, NZ, NY = 4, 2, 8
STICKS = 12288
GROUPS = 2
STEPS = 2
PIECES = 3
MESH = pl.DeviceIdType.MESH
F32, BF16 = jnp.float32, jnp.bfloat16


def cas_table(n):
    k = np.arange(n)
    angles = 2.0 * math.pi / n * ((k[:, None] * k[None, :]) % n)
    return np.asarray(np.cos(angles) + np.sin(angles), np.float32)


def pair_table(n, width):
    cas = cas_table(n)
    half = width // GROUPS
    table = np.zeros((2, n, GROUPS, n // width, 2, half), np.float32)
    by_x = cas.reshape(n, n // width, GROUPS, half).transpose(0, 2, 1, 3)
    for h in range(2):
        table[h, :, :, :, h, :] = by_x
    return table.reshape(2 * n, 2 * n)


def packing(n, n_plane):
    signed = np.minimum(np.arange(n), n - np.arange(n))
    squares = signed[:, None] ** 2 + signed[None, :] ** 2
    kept = (squares <= np.sort(squares.reshape(-1))[STICKS - 1]).sum(1)
    best = None
    for t in range(1, n // 2 + 1):
        for extra in ([], [n - t + 1]):
            second = [h for h in range(n) if kept[h] and (signed[h] >= t or h in extra)]
            firsts = [h for h in range(n) if kept[h] and h not in second]
            free, mate = sorted(firsts, key=lambda h: -kept[h]), {}
            for h in sorted(second, key=lambda h: -kept[h]):
                host = next((f for f in free if kept[f] + kept[h] <= n), None)
                if host is None:
                    break
                free.remove(host)
                mate[host] = h
            else:
                if best is None or len(firsts) < len(best[0]):
                    best = firsts, mate, t, extra
    firsts, mate, t, extra = best
    pairs = -(-len(firsts) // 2)
    per_owner = -(-pairs // n_plane) * 2
    n_small = per_owner // 2 * n_plane - pairs
    period = n_plane // n_small if n_small and n_plane % n_small == 0 else 0
    table = -np.ones((per_owner * n_plane, 3), np.int64)
    left = list(firsts)
    for owner in range(n_plane):
        count = per_owner - 2 if period and owner % period == period - 1 else per_owner
        for k in range(min(count, len(left))):
            h = left.pop(0)
            table[owner * per_owner + k] = h, mate.get(h, -1), kept[h]
    return table, per_owner, period, t, (extra or [-1])[0]


def tables(n, n_plane):
    width = n // n_plane
    cas = cas_table(n)
    rows, per_owner = packing(n, n_plane)[:2]
    order = sorted(range(n), key=lambda g: (min(g, n - g), g > n // 2))
    both = np.concatenate([cas[:, order], cas[:, order[::-1]]], 1)
    first, second = np.zeros((n, n), np.float32), np.zeros((n, n), np.float32)
    for row, (h, other, _) in enumerate(rows):
        if h >= 0:
            first[row] = cas[h]
        if other >= 0:
            second[row] = cas[other]
    wide = np.concatenate([both, pair_table(n, width), np.concatenate([first.T, second.T], 1) / n], 0)
    slim = np.concatenate([first, second, both.T / n, cas / n], 0)
    labels = np.full((n, 128), -7, np.int32)
    for row, (h, other, length) in enumerate(rows):
        place = row // per_owner * width + row % per_owner
        labels[place, 0] = h if h >= 0 else -7
        labels[place, 1] = other if other >= 0 else -7
    labels[:, 2] = n
    labels[: len(rows), 2] = np.where(rows[:, 2] < 0, n, rows[:, 2])
    return jnp.asarray(wide).astype(BF16), jnp.asarray(slim).astype(BF16), jnp.asarray(labels)


def dot(a, b):
    return jnp.dot(a, b, preferred_element_type=F32)


def broadcast_pieces(rows):
    return [(0, rows // 4), (rows // 4, rows // 4), (rows // 2, rows // 2)]


def far_first(count):
    return sorted(range(1, count), key=lambda d: -min(d, count - d))


def pick(index, values):
    out = values[0]
    for k in range(1, len(values)):
        out = jnp.where(index == k, values[k], out)
    return out


def remote(src, dst, send_sem, recv_sem, device):
    return pltpu.make_async_remote_copy(
        src_ref=src, dst_ref=dst, send_sem=send_sem, recv_sem=recv_sem,
        device_id=device, device_id_type=MESH,
    )


def kernel(
    n, n_plane,
    roots_ref, orb_hbm, wide_hbm, slim_hbm, labels_hbm, coulomb_hbm, ids_hbm, out_ref,
    orb, wide, slim, labels, coulomb, ids_ref,
    orb16, in_x0, in_x1, in_x2, sel0, sel1, sel2, in_y0, in_y1, in_y2,
    cand0, cand1, cand2, in_z0, in_z1, in_z2, shared,
    flat_sum, part, in_part, coul16, dense, grid_a, grid_b, send_f, recv_f, send_b, recv_b, total,
    s_orb, s_in, s_x, r_x, s_y, r_y, s_z, r_z, s_gy, r_gy, s_gx, r_gx,
    s_p, r_p, s_dy, r_dy, s_dx, r_dx, s_f, r_f, s_b, r_b,
):
    width = n // n_plane
    rows = width * n
    rows_g = rows // GROUPS
    _, per_owner, period, edge, edge_row = packing(n, n_plane)
    n_packed = per_owner * n_plane
    in_x, sel, in_y = [in_x0, in_x1, in_x2], [sel0, sel1, sel2], [in_y0, in_y1, in_y2]
    cand, in_z = [cand0, cand1, cand2], [in_z0, in_z1, in_z2]
    pieces = broadcast_pieces(rows)
    band, plane = lax.axis_index("band"), lax.axis_index("plane")
    y = lax.rem(band, NY)
    zh = lax.rem(band // NY, NZ)
    x = band // (NY * NZ)

    def at_band(bx, bz, by):
        return {"band": (bx * NZ + bz) * NY + by}

    def x_peer(d):
        return lax.rem(x + d, NX)

    def y_peer(d):
        return lax.rem(y + d, NY)

    def p_peer(d):
        return lax.rem(plane + d, n_plane)

    bits = [lax.rem(plane // (1 << k), 2) for k in range(n_plane.bit_length() - 1)]
    owners = []
    for flip in sorted(range(1, n_plane), key=lambda f: (-(f >> 1), f)):
        t = 0
        for k, bit in enumerate(bits):
            t = t + (1 << k) * (1 - bit if flip >> k & 1 else bit)
        owners.append(t)

    barrier = pltpu.get_barrier_semaphore()
    peers = [at_band(x_peer(d), zh, y) for d in far_first(NX)]
    peers += [at_band(x, zh, y_peer(d)) for d in far_first(NY)]
    peers += [at_band(x, lax.rem(zh + d, NZ), y) for d in range(1, NZ)]
    peers += [{"plane": p_peer(d)} for d in range(1, n_plane)]
    for peer in peers:
        pl.semaphore_signal(barrier, inc=1, device_id=peer, device_id_type=MESH)

    coul_rows = n // (NX * NY)
    first_row = (y * NX + x) * coul_rows
    coul_tile = pl.multiple_of(first_row // 16 * 16, 16)
    orb_loads = [
        pltpu.make_async_copy(orb_hbm.at[pl.ds(*at)], orb.at[pl.ds(*at)], s_orb.at[p])
        for p, at in enumerate(pieces)
    ]
    loads = [
        pltpu.make_async_copy(coulomb_hbm.at[pl.ds(coul_tile, 16)], coulomb, s_in.at[0]),
        pltpu.make_async_copy(ids_hbm, ids_ref, s_in.at[1]),
        pltpu.make_async_copy(labels_hbm, labels, s_in.at[2]),
        pltpu.make_async_copy(slim_hbm, slim, s_in.at[3]),
        pltpu.make_async_copy(wide_hbm, wide, s_in.at[4]),
    ]
    for load in orb_loads + loads:
        load.start()

    def round_piece(p):
        first, count = pieces[p]
        orb_loads[p].wait()
        orb16[first : first + count, :] = orb[first : first + count, :].astype(BF16)

    round_piece(0)
    pl.semaphore_wait(barrier, len(peers))

    def start(copy):
        copy.start()

    def arrived(region, sem):
        remote(region, region, sem, sem, {"plane": p_peer(1)}).wait_recv()

    def sent(region, sem):
        remote(region, region, sem, sem, {"plane": p_peer(1)}).wait_send()

    def x_copy(p, target, slot):
        first, count = pieces[p]
        chunk = count // NX
        return remote(
            orb16.at[pl.ds(first + target * chunk, chunk)], in_x[p].at[slot],
            s_x.at[p], r_x.at[p], at_band(target, zh, y),
        )

    def send_x(p):
        for d in far_first(NX):
            start(x_copy(p, x_peer(d), x))
        first, count = pieces[p]
        chunk = count // NX
        in_x[p][x] = orb16[pl.ds(first + x * chunk, chunk), :]

    root = [roots_ref[s] for s in range(STEPS)]
    root_y = [lax.rem(r, NY) for r in root]
    root_z = [lax.rem(r // NY, NZ) for r in root]
    root_x = [r // (NY * NZ) for r in root]

    def send_y(p):
        arrived(in_x[p].at[pl.ds(0, NX - 1)], r_x.at[p])
        for s in range(STEPS):
            sel[p][s] = pick(root_x[s], [in_x[p][k] for k in range(NX)])
        chunk = pieces[p][1] // (NX * NY)
        for d in far_first(NY):
            t = y_peer(d)
            start(remote(
                sel[p].at[:, pl.ds(t * chunk, chunk)], in_y[p].at[y],
                s_y.at[p], r_y.at[p], at_band(x, zh, t),
            ))
        in_y[p][y] = sel[p][:, pl.ds(y * chunk, chunk), :]

    def z_copy(p):
        return remote(
            cand[p], in_z[p], s_z.at[p], r_z.at[p], at_band(x, lax.rem(zh + 1, NZ), y)
        )

    def send_z(p):
        arrived(in_y[p].at[pl.ds(0, NY - 1)], r_y.at[p])
        for s in range(STEPS):
            cand[p][s] = pick(root_y[s], [in_y[p][k, s] for k in range(NY)])
        start(z_copy(p))

    def send_gy(p):
        z_copy(p).wait_recv()
        first, count = pieces[p]
        chunk = count // (NX * NY)
        at = pl.ds(first + (x * NY + y) * chunk, chunk)
        for s in range(STEPS):
            shared[s, at, :] = jnp.where(root_z[s] == zh, cand[p][s], in_z[p][s])
        block = shared.at[:, at]
        for d in far_first(NY):
            start(remote(block, block, s_gy.at[p], r_gy.at[p], at_band(x, zh, y_peer(d))))

    def wait_gy(p):
        first, count = pieces[p]
        chunk = count // (NX * NY)
        arrived(shared.at[:, pl.ds(first + x * NY * chunk, (NY - 1) * chunk)], r_gy.at[p])

    def send_gx(p, s):
        first, count = pieces[p]
        block = shared.at[s, pl.ds(first + x * (count // NX), count // NX)]
        for d in far_first(NX):
            start(remote(block, block, s_gx.at[p, s], r_gx.at[p, s], at_band(x_peer(d), zh, y)))

    def wait_gx(p, s):
        first, count = pieces[p]
        arrived(shared.at[s, pl.ds(first, count // NX * (NX - 1))], r_gx.at[p, s])

    def p_copy(target, slot):
        return remote(part.at[target], in_part.at[slot], s_p, r_p, {"plane": target})

    slots = ids_ref.shape[1]
    piece = -(-slots // (128 * PIECES)) * 128

    def add_part(i):
        if i == 0:
            loads[0].wait()
            loads[1].wait()
            loads[2].wait()
        at = slice(i * piece, min((i + 1) * piece, slots))
        ids = ids_ref[pl.ds(plane, 1), at]
        valid = ids >= 0
        id_h = jnp.where(valid, ids // n, -1)
        id_g = jnp.where(valid, lax.rem(ids, n), 0)
        lane = jnp.where(id_g == 0, 0, jnp.where(id_g <= n // 2, 2 * id_g - 1, 2 * (n - id_g)))
        reverse = (jnp.minimum(id_h, n - id_h) >= edge) | (id_h == edge_row)
        lane = jnp.where(reverse, n - 1 - lane, lane)
        iota = lax.broadcasted_iota(jnp.int32, (n, ids.shape[1]), 0)
        hot_h = (labels[:, 0:1] == id_h) | (labels[:, 1:2] == id_h)
        hot_g = jnp.where(iota == lane, 1.0, 0.0).astype(BF16)
        tile = coulomb[:, at].astype(F32)
        own = tile[:coul_rows]
        for k in range(1, 16 // coul_rows):
            inside = first_row - coul_tile == k * coul_rows
            own = jnp.where(inside, tile[k * coul_rows : (k + 1) * coul_rows], own)
        left = jnp.concatenate(
            [jnp.where(hot_h, own[k : k + 1], 0.0).astype(BF16) for k in range(coul_rows)], 0
        )
        flat = lax.dot_general(
            left, hot_g, (((1,), (1,)), ((), ())), preferred_element_type=F32
        )
        flat_sum[...] = flat if i == 0 else flat_sum[...] + flat

    def send_part():
        for k in range(coul_rows):
            for o in range(n_plane):
                at = slice(k * n + o * width, k * n + (o + 1) * width)
                part[o, k * width : (k + 1) * width, :] = flat_sum[at, :].astype(BF16)
        for t in owners:
            start(p_copy(t, plane))
        in_part[plane] = part[plane]

    coul_y, coul_x = rows // NY, rows // (NX * NY)

    def send_dx():
        arrived(in_part.at[pl.ds(0, n_plane - 1)], r_p)
        summed = in_part[0].astype(F32)
        for o in range(1, n_plane):
            summed = summed + in_part[o].astype(F32)
        at = pl.ds(y * coul_y + x * coul_x, coul_x)
        coul16[at, :] = summed.astype(BF16)
        block = coul16.at[at]
        for d in far_first(NX):
            start(remote(block, block, s_dx, r_dx, at_band(x_peer(d), zh, y)))

    def send_dy():
        arrived(coul16.at[pl.ds(y * coul_y, (NX - 1) * coul_x)], r_dx)
        block = coul16.at[pl.ds(y * coul_y, coul_y)]
        for d in far_first(NY):
            start(remote(block, block, s_dy, r_dy, at_band(x, zh, y_peer(d))))

    def wait_dense():
        arrived(coul16.at[pl.ds(0, (NY - 1) * coul_y)], r_dy)
        dense[...] = coul16[...].astype(F32)

    half = width // GROUPS
    block = per_owner * half
    small_block = block - 2 * half
    own_small = lax.rem(plane, period) == period - 1 if period else False
    n_small = n_plane // period if period else 0

    def sized(small, body):
        if not period:
            body(block)
            return
        pl.when(small)(lambda: body(small_block))
        pl.when(jnp.logical_not(small))(lambda: body(block))

    def of_owners(wait, times=1):
        every = times * (block * (n_plane - 1) - 2 * half * n_small)
        if not period:
            wait(orb16.at[pl.ds(0, every)])
            return
        pl.when(own_small)(lambda: wait(orb16.at[pl.ds(0, every + times * 2 * half)]))
        pl.when(jnp.logical_not(own_small))(lambda: wait(orb16.at[pl.ds(0, every)]))

    def of_own(wait, times=1):
        sized(own_small, lambda count: wait(orb16.at[pl.ds(0, times * count * (n_plane - 1))]))

    def send_block(from_ref, to_ref, count, sems, target):
        at = pl.ds(0, count)
        start(remote(from_ref.at[at], to_ref.at[at], sems[0], sems[1], {"plane": target}))

    def wait_group(g, s, i):
        if g == 0:
            wait_gx(i, s)
        elif i == 0:
            wait_gx(2, s)

    def forward(g, s):
        both = wide[:n, :]
        first, second = slim[:n_packed, :], slim[n : n + n_packed, :]
        in_first = lax.broadcasted_iota(jnp.int32, (n_packed, n), 1) < labels[:n_packed, 2:3]
        group = 4

        for i in range(half // group):
            wait_group(g, s, i)
            at = slice(g * rows_g + i * group * n, g * rows_g + (i + 1) * group * n)
            pair = (orb[at, :] * shared[s, at, :].astype(F32)).astype(BF16)
            along = dot(pair, both).astype(BF16)
            planes = [along[k * n : (k + 1) * n] for k in range(group)]
            from_first = dot(first, jnp.concatenate([plane_k[:, :n] for plane_k in planes], 1))
            from_second = dot(second, jnp.concatenate([plane_k[:, n:] for plane_k in planes], 1))
            for k in range(group):
                at = slice(k * n, (k + 1) * n)
                packed = jnp.where(in_first, from_first[:, at], from_second[:, at])
                grid_a[pl.ds(i * group + k, n_packed, stride=half), :] = packed
        for t in owners:
            send_f[s, g, t] = grid_a[pl.ds(pl.multiple_of(t * block, block), block), :].astype(BF16)
            small = lax.rem(t, period) == period - 1 if period else False
            sems = (s_f.at[g, s], r_f.at[g, s])
            sized(small, lambda count: send_block(
                send_f.at[s, g, t], recv_f.at[s, g, plane], count, sems, t))
        at = pl.ds(pl.multiple_of(plane * block, block), block)
        recv_f[s, g, plane] = grid_a[at, :].astype(BF16)

    def middle(s):
        for g in range(GROUPS):
            of_own(lambda region: arrived(region, r_f.at[g, s]))
        twin, cas = wide[n : 3 * n, :], slim[4 * n : 5 * n, :]
        pairs = per_owner // 2
        for first_pair in range(0, pairs, 2):
            js = range(first_pair, min(first_pair + 2, pairs))
            at = [slice(j * 2 * half, (j + 1) * 2 * half) for j in js]
            sticks = [recv_f[s, :, :, a, :].reshape(2 * n, n) for a in at]
            if period and js[-1] == pairs - 1:
                sticks[-1] = jnp.where(own_small, jnp.zeros_like(sticks[-1]), sticks[-1])
            spectrum = dot(twin, jnp.concatenate(sticks, 1))
            scaled = []
            for k, j in enumerate(js):
                for h in range(2):
                    coul = dense[pl.ds(2 * j + h, n, stride=width), :]
                    part_h = spectrum[h * n : (h + 1) * n, k * n : (k + 1) * n]
                    scaled.append((part_h * coul).astype(BF16))
            back = dot(cas, jnp.concatenate(scaled, 1))
            for k in range(len(js)):
                two = [
                    back[:, (2 * k + h) * n : (2 * k + h + 1) * n].reshape(n_plane, GROUPS, half, n)
                    for h in range(2)
                ]
                for g in range(GROUPS):
                    for q in range(n_plane):
                        both = jnp.concatenate([two[0][q, g], two[1][q, g]], 0)
                        send_b[s, g, q, at[k], :] = both.astype(BF16)
        for g in [None] if s == 0 else range(GROUPS):
            def send_all(count):
                for t in owners:
                    at = pl.ds(0, count)
                    own = send_b.at[s, :, t, at] if g is None else send_b.at[s, g, t, at]
                    there = recv_b.at[s, :, plane, at] if g is None else recv_b.at[s, g, plane, at]
                    k = g or 0
                    start(remote(own, there, s_b.at[k, s], r_b.at[k, s], {"plane": t}))

            sized(own_small, send_all)
        for g in range(GROUPS):
            recv_b[s, g, plane] = send_b[s, g, plane]

    def inverse(g, s):
        if s or g == 0:
            of_owners(lambda region: arrived(region, r_b.at[g, s]), 1 if s else GROUPS)
        first, second = wide[3 * n :, :n], wide[3 * n :, n:]
        both = slim[2 * n : 4 * n, :]
        in_first = lax.broadcasted_iota(jnp.int32, (n, n), 1) < labels[:, 2:3]
        grid_b[: n_packed * half, :] = recv_b[s, g].reshape(n_packed * half, n).astype(F32)
        group = 4

        for i in range(half // group):
            packed = [grid_b[pl.ds(i * group + k, n, stride=half), :] for k in range(group)]
            own = [jnp.where(in_first, one, 0.0).astype(BF16) for one in packed]
            other = [jnp.where(in_first, 0.0, one).astype(BF16) for one in packed]
            from_first = dot(first, jnp.concatenate(own, 1))
            from_second = dot(second, jnp.concatenate(other, 1))
            inverse_y = []
            for k in range(group):
                at = slice(k * n, (k + 1) * n)
                inverse_y.append(jnp.concatenate([from_first[:, at], from_second[:, at]], 1).astype(BF16))
            at = slice(g * rows_g + i * group * n, g * rows_g + (i + 1) * group * n)
            term = dot(jnp.concatenate(inverse_y, 0), both) * shared[s, at, :].astype(F32)
            if s == 0:
                total[at, :] = term
            else:
                out_ref[at, :] = (total[at, :] + term).astype(BF16)

    send_x(0)
    round_piece(1)
    send_x(1)
    round_piece(2)
    send_x(2)
    add_part(0)
    send_y(0)
    send_y(1)
    add_part(1)
    send_z(0)
    send_y(2)
    send_z(1)
    for i in range(2, PIECES):
        add_part(i)
    send_gy(0)
    send_part()
    send_gy(1)
    send_z(2)
    loads[3].wait()
    loads[4].wait()
    wait_gy(0)
    send_gx(0, 0)
    wait_gy(1)
    send_gx(1, 0)
    send_gy(2)
    send_gx(0, 1)
    send_gx(1, 1)
    send_dx()
    forward(0, 0)
    wait_gy(2)
    send_gx(2, 0)
    send_gx(2, 1)
    send_dy()
    forward(0, 1)
    forward(1, 0)
    forward(1, 1)
    for p, (_, count) in enumerate(pieces):
        sent(in_x[p].at[pl.ds(0, NX - 1)], s_x.at[p])
        sent(in_y[p].at[pl.ds(0, NY - 1)], s_y.at[p])
        sent(in_z[p], s_z.at[p])
        sent(shared.at[:, pl.ds(0, (NY - 1) * (count // (NX * NY)))], s_gy.at[p])
        for s in range(STEPS):
            sent(shared.at[s, pl.ds(0, (NX - 1) * (count // NX))], s_gx.at[p, s])
    sent(in_part.at[pl.ds(0, n_plane - 1)], s_p)
    grid_b[n_packed * half :, :] = jnp.zeros(((n - n_packed) * half, n), F32)
    for q in range(n_plane):
        if period and q % period == period - 1:
            recv_b[:, :, q, small_block:, :] = jnp.zeros((STEPS, GROUPS, 2 * half, n), BF16)
    wait_dense()
    middle(0)
    sent(coul16.at[pl.ds(0, (NY - 1) * coul_y)], s_dy)
    sent(coul16.at[pl.ds(0, (NX - 1) * coul_x)], s_dx)
    middle(1)
    for g in range(GROUPS):
        for s in range(STEPS):
            of_owners(lambda region: sent(region, s_f.at[g, s]))
    inverse(0, 0)
    inverse(1, 0)
    inverse(0, 1)
    inverse(1, 1)
    of_own(lambda region: sent(region, s_b.at[0, 0]), GROUPS)
    for g in range(GROUPS):
        of_own(lambda region: sent(region, s_b.at[g, 1]))


def on_device(orbitals, coulomb, stick_lists, roots):
    _, width, n, _ = orbitals.shape
    n_plane = n // width
    rows = width * n
    rows_g = rows // GROUPS
    counts = [count for _, count in broadcast_pieces(rows)]
    coul_block = n // (NX * NY) * width
    per_owner = packing(n, n_plane)[1]
    wide, slim, labels = tables(n, n_plane)
    hbm = pl.BlockSpec(memory_space=pl.ANY)
    vmem = pl.BlockSpec(memory_space=pltpu.VMEM)
    dma = pltpu.SemaphoreType.DMA

    def pair_of_sems(*shape):
        return [dma(shape), dma(shape)]

    gs = (GROUPS, STEPS)
    spectra = pltpu.VMEM((STEPS, GROUPS, n_plane, per_owner * width // GROUPS, n), BF16)
    out = pl.pallas_call(
        functools.partial(kernel, n, n_plane),
        out_shape=jax.ShapeDtypeStruct((rows, n), BF16),
        in_specs=[pl.BlockSpec(memory_space=pltpu.SMEM)] + [hbm] * 6,
        out_specs=vmem,
        scratch_shapes=[
            pltpu.VMEM((rows, n), F32),
            pltpu.VMEM(wide.shape, BF16),
            pltpu.VMEM(slim.shape, BF16),
            pltpu.VMEM(labels.shape, jnp.int32),
            pltpu.VMEM((16, coulomb.shape[1]), BF16),
            pltpu.VMEM(stick_lists.shape, jnp.int32),
            pltpu.VMEM((rows, n), BF16),
            *[pltpu.VMEM((NX, count // NX, n), BF16) for count in counts],
            *[pltpu.VMEM((STEPS, count // NX, n), BF16) for count in counts],
            *[pltpu.VMEM((NY, STEPS, count // (NX * NY), n), BF16) for count in counts],
            *[pltpu.VMEM((STEPS, count // (NX * NY), n), BF16) for count in counts * 2],
            pltpu.VMEM((STEPS, rows, n), BF16),
            pltpu.VMEM((n // (NX * NY) * n, n), F32),
            pltpu.VMEM((n_plane, coul_block, n), BF16),
            pltpu.VMEM((n_plane, coul_block, n), BF16),
            pltpu.VMEM((rows, n), BF16),
            pltpu.VMEM((rows, n), F32),
            pltpu.VMEM((rows_g, n), F32),
            pltpu.VMEM((rows_g, n), F32),
            spectra, spectra, spectra, spectra,
            pltpu.VMEM((rows, n), F32),
            dma((len(counts),)),
            dma((5,)),
            *pair_of_sems(len(counts)),
            *pair_of_sems(len(counts)),
            *pair_of_sems(len(counts)),
            *pair_of_sems(len(counts)),
            *pair_of_sems(len(counts), STEPS),
            dma, dma, dma, dma, dma, dma,
            *pair_of_sems(*gs),
            *pair_of_sems(*gs),
        ],
        compiler_params=pltpu.CompilerParams(
            collective_id=0, has_side_effects=True, vmem_limit_bytes=57 * 1024 * 1024
        ),
        name="exchange",
    )(
        roots, orbitals.reshape(rows, n),
        wide, slim, labels, coulomb, stick_lists,
    )
    return out.reshape(1, width, n, n)


def solution(mesh):
    in_specs = (P("band", "plane", None, None), P(None, "plane"), P(), P())
    out_specs = P("band", "plane", None, None)
    return jax.shard_map(
        on_device, mesh=mesh, in_specs=in_specs, out_specs=out_specs, check_vma=False
    )
```

```python
import functools
import math

import jax
import jax.numpy as jnp
import numpy as np
from jax import lax
from jax.experimental import pallas as pl
from jax.experimental.pallas import tpu as pltpu
from jax.sharding import PartitionSpec as P

NX, NZ, NY = 4, 2, 8
STICKS = 12288
GROUPS = 2
STEPS = 2
PIECES = 3
MESH = pl.DeviceIdType.MESH
F32, BF16 = jnp.float32, jnp.bfloat16


def cas_table(n):
    k = np.arange(n)
    angles = 2.0 * math.pi / n * ((k[:, None] * k[None, :]) % n)
    return np.asarray(np.cos(angles) + np.sin(angles), np.float32)


def pair_table(n, width):
    cas = cas_table(n)
    half = width // GROUPS
    table = np.zeros((2, n, GROUPS, n // width, 2, half), np.float32)
    by_x = cas.reshape(n, n // width, GROUPS, half).transpose(0, 2, 1, 3)
    for h in range(2):
        table[h, :, :, :, h, :] = by_x
    return table.reshape(2 * n, 2 * n)


def packing(n, n_plane):
    signed = np.minimum(np.arange(n), n - np.arange(n))
    squares = signed[:, None] ** 2 + signed[None, :] ** 2
    kept = (squares <= np.sort(squares.reshape(-1))[STICKS - 1]).sum(1)
    best = None
    for t in range(1, n // 2 + 1):
        for extra in ([], [n - t + 1]):
            second = [h for h in range(n) if kept[h] and (signed[h] >= t or h in extra)]
            firsts = [h for h in range(n) if kept[h] and h not in second]
            free, mate = sorted(firsts, key=lambda h: -kept[h]), {}
            for h in sorted(second, key=lambda h: -kept[h]):
                host = next((f for f in free if kept[f] + kept[h] <= n), None)
                if host is None:
                    break
                free.remove(host)
                mate[host] = h
            else:
                if best is None or len(firsts) < len(best[0]):
                    best = firsts, mate, t, extra
    firsts, mate, t, extra = best
    pairs = -(-len(firsts) // 2)
    per_owner = -(-pairs // n_plane) * 2
    n_small = per_owner // 2 * n_plane - pairs
    period = n_plane // n_small if n_small and n_plane % n_small == 0 else 0
    table = -np.ones((per_owner * n_plane, 3), np.int64)
    left = list(firsts)
    for owner in range(n_plane):
        count = per_owner - 2 if period and owner % period == period - 1 else per_owner
        for k in range(min(count, len(left))):
            h = left.pop(0)
            table[owner * per_owner + k] = h, mate.get(h, -1), kept[h]
    return table, per_owner, period, t, (extra or [-1])[0]


def tables(n, n_plane):
    width = n // n_plane
    cas = cas_table(n)
    rows, per_owner = packing(n, n_plane)[:2]
    order = sorted(range(n), key=lambda g: (min(g, n - g), g > n // 2))
    both = np.concatenate([cas[:, order], cas[:, order[::-1]]], 1)
    first, second = np.zeros((n, n), np.float32), np.zeros((n, n), np.float32)
    for row, (h, other, _) in enumerate(rows):
        if h >= 0:
            first[row] = cas[h]
        if other >= 0:
            second[row] = cas[other]
    wide = np.concatenate([both, pair_table(n, width), np.concatenate([first.T, second.T], 1) / n], 0)
    slim = np.concatenate([first, second, both.T / n, cas / n], 0)
    labels = np.full((n, 128), -7, np.int32)
    for row, (h, other, length) in enumerate(rows):
        place = row // per_owner * width + row % per_owner
        labels[place, 0] = h if h >= 0 else -7
        labels[place, 1] = other if other >= 0 else -7
    labels[:, 2] = n
    labels[: len(rows), 2] = np.where(rows[:, 2] < 0, n, rows[:, 2])
    return jnp.asarray(wide).astype(BF16), jnp.asarray(slim).astype(BF16), jnp.asarray(labels)


def dot(a, b):
    return jnp.dot(a, b, preferred_element_type=F32)


def broadcast_pieces(rows):
    return [(0, rows // 4), (rows // 4, rows // 4), (rows // 2, rows // 2)]


def far_first(count):
    return sorted(range(1, count), key=lambda d: -min(d, count - d))


def pick(index, values):
    out = values[0]
    for k in range(1, len(values)):
        out = jnp.where(index == k, values[k], out)
    return out


def remote(src, dst, send_sem, recv_sem, device):
    return pltpu.make_async_remote_copy(
        src_ref=src, dst_ref=dst, send_sem=send_sem, recv_sem=recv_sem,
        device_id=device, device_id_type=MESH,
    )


def kernel(
    n, n_plane,
    roots_ref, orb_hbm, wide_hbm, slim_hbm, labels_hbm, coulomb_hbm, ids_hbm, out_ref,
    orb, wide, slim, labels, coulomb, ids_ref,
    orb16, in_x0, in_x1, in_x2, sel0, sel1, sel2, in_y0, in_y1, in_y2,
    cand0, cand1, cand2, in_z0, in_z1, in_z2, shared,
    flat_sum, part, in_part, coul16, dense, grid_a, grid_b, send_f, recv_f, send_b, recv_b, total,
    s_orb, s_in, s_x, r_x, s_y, r_y, s_z, r_z, s_gy, r_gy, s_gx, r_gx,
    s_p, r_p, s_dy, r_dy, s_dx, r_dx, s_f, r_f, s_b, r_b,
):
    width = n // n_plane
    rows = width * n
    rows_g = rows // GROUPS
    _, per_owner, period, edge, edge_row = packing(n, n_plane)
    n_packed = per_owner * n_plane
    in_x, sel, in_y = [in_x0, in_x1, in_x2], [sel0, sel1, sel2], [in_y0, in_y1, in_y2]
    cand, in_z = [cand0, cand1, cand2], [in_z0, in_z1, in_z2]
    pieces = broadcast_pieces(rows)
    band, plane = lax.axis_index("band"), lax.axis_index("plane")
    y = lax.rem(band, NY)
    zh = lax.rem(band // NY, NZ)
    x = band // (NY * NZ)

    def at_band(bx, bz, by):
        return {"band": (bx * NZ + bz) * NY + by}

    def x_peer(d):
        return lax.rem(x + d, NX)

    def y_peer(d):
        return lax.rem(y + d, NY)

    def p_peer(d):
        return lax.rem(plane + d, n_plane)

    bits = [lax.rem(plane // (1 << k), 2) for k in range(n_plane.bit_length() - 1)]
    owners = []
    for flip in sorted(range(1, n_plane), key=lambda f: (-(f >> 1), f)):
        t = 0
        for k, bit in enumerate(bits):
            t = t + (1 << k) * (1 - bit if flip >> k & 1 else bit)
        owners.append(t)

    orb_loads = [
        pltpu.make_async_copy(orb_hbm.at[pl.ds(*at)], orb.at[pl.ds(*at)], s_orb.at[p])
        for p, at in enumerate(pieces)
    ]
    for load in orb_loads:
        load.start()

    barrier = pltpu.get_barrier_semaphore()
    peers = [at_band(x_peer(d), zh, y) for d in far_first(NX)]
    peers += [at_band(x, zh, y_peer(d)) for d in far_first(NY)]
    peers += [at_band(x, lax.rem(zh + d, NZ), y) for d in range(1, NZ)]
    peers += [{"plane": p_peer(d)} for d in range(1, n_plane)]
    for peer in peers:
        pl.semaphore_signal(barrier, inc=1, device_id=peer, device_id_type=MESH)

    coul_rows = n // (NX * NY)
    first_row = (y * NX + x) * coul_rows
    coul_tile = pl.multiple_of(first_row // 16 * 16, 16)
    loads = [
        pltpu.make_async_copy(coulomb_hbm.at[pl.ds(coul_tile, 16)], coulomb, s_in.at[0]),
        pltpu.make_async_copy(ids_hbm, ids_ref, s_in.at[1]),
        pltpu.make_async_copy(labels_hbm, labels, s_in.at[2]),
        pltpu.make_async_copy(slim_hbm, slim, s_in.at[3]),
        pltpu.make_async_copy(wide_hbm, wide, s_in.at[4]),
    ]
    for load in loads:
        load.start()

    def round_piece(p):
        first, count = pieces[p]
        orb_loads[p].wait()
        orb16[first : first + count, :] = orb[first : first + count, :].astype(BF16)

    round_piece(0)
    pl.semaphore_wait(barrier, len(peers))

    def start(copy):
        copy.start()

    def arrived(region, sem):
        remote(region, region, sem, sem, {"plane": p_peer(1)}).wait_recv()

    def sent(region, sem):
        remote(region, region, sem, sem, {"plane": p_peer(1)}).wait_send()

    def x_copy(p, target, slot):
        first, count = pieces[p]
        chunk = count // NX
        return remote(
            orb16.at[pl.ds(first + target * chunk, chunk)], in_x[p].at[slot],
            s_x.at[p], r_x.at[p], at_band(target, zh, y),
        )

    def send_x(p):
        for d in far_first(NX):
            start(x_copy(p, x_peer(d), x))
        first, count = pieces[p]
        chunk = count // NX
        in_x[p][x] = orb16[pl.ds(first + x * chunk, chunk), :]

    root = [roots_ref[s] for s in range(STEPS)]
    root_y = [lax.rem(r, NY) for r in root]
    root_z = [lax.rem(r // NY, NZ) for r in root]
    root_x = [r // (NY * NZ) for r in root]

    def send_y(p):
        arrived(in_x[p].at[pl.ds(0, NX - 1)], r_x.at[p])
        for s in range(STEPS):
            sel[p][s] = pick(root_x[s], [in_x[p][k] for k in range(NX)])
        chunk = pieces[p][1] // (NX * NY)
        for d in far_first(NY):
            t = y_peer(d)
            start(remote(
                sel[p].at[:, pl.ds(t * chunk, chunk)], in_y[p].at[y],
                s_y.at[p], r_y.at[p], at_band(x, zh, t),
            ))
        in_y[p][y] = sel[p][:, pl.ds(y * chunk, chunk), :]

    def z_copy(p):
        return remote(
            cand[p], in_z[p], s_z.at[p], r_z.at[p], at_band(x, lax.rem(zh + 1, NZ), y)
        )

    def send_z(p):
        arrived(in_y[p].at[pl.ds(0, NY - 1)], r_y.at[p])
        for s in range(STEPS):
            cand[p][s] = pick(root_y[s], [in_y[p][k, s] for k in range(NY)])
        start(z_copy(p))

    def send_gy(p):
        z_copy(p).wait_recv()
        first, count = pieces[p]
        chunk = count // (NX * NY)
        at = pl.ds(first + (x * NY + y) * chunk, chunk)
        for s in range(STEPS):
            shared[s, at, :] = jnp.where(root_z[s] == zh, cand[p][s], in_z[p][s])
        block = shared.at[:, at]
        for d in far_first(NY):
            start(remote(block, block, s_gy.at[p], r_gy.at[p], at_band(x, zh, y_peer(d))))

    def wait_gy(p):
        first, count = pieces[p]
        chunk = count // (NX * NY)
        arrived(shared.at[:, pl.ds(first + x * NY * chunk, (NY - 1) * chunk)], r_gy.at[p])

    def send_gx(p, s):
        first, count = pieces[p]
        block = shared.at[s, pl.ds(first + x * (count // NX), count // NX)]
        for d in far_first(NX):
            start(remote(block, block, s_gx.at[p, s], r_gx.at[p, s], at_band(x_peer(d), zh, y)))

    def wait_gx(p, s):
        first, count = pieces[p]
        arrived(shared.at[s, pl.ds(first, count // NX * (NX - 1))], r_gx.at[p, s])

    def p_copy(target, slot):
        return remote(part.at[target], in_part.at[slot], s_p, r_p, {"plane": target})

    slots = ids_ref.shape[1]
    piece = -(-slots // (128 * PIECES)) * 128

    def add_part(i):
        if i == 0:
            loads[0].wait()
            loads[1].wait()
            loads[2].wait()
        at = slice(i * piece, min((i + 1) * piece, slots))
        ids = ids_ref[pl.ds(plane, 1), at]
        valid = ids >= 0
        id_h = jnp.where(valid, ids // n, -1)
        id_g = jnp.where(valid, lax.rem(ids, n), 0)
        lane = jnp.where(id_g == 0, 0, jnp.where(id_g <= n // 2, 2 * id_g - 1, 2 * (n - id_g)))
        reverse = (jnp.minimum(id_h, n - id_h) >= edge) | (id_h == edge_row)
        lane = jnp.where(reverse, n - 1 - lane, lane)
        iota = lax.broadcasted_iota(jnp.int32, (n, ids.shape[1]), 0)
        hot_h = (labels[:, 0:1] == id_h) | (labels[:, 1:2] == id_h)
        hot_g = jnp.where(iota == lane, 1.0, 0.0).astype(BF16)
        tile = coulomb[:, at].astype(F32)
        own = tile[:coul_rows]
        for k in range(1, 16 // coul_rows):
            inside = first_row - coul_tile == k * coul_rows
            own = jnp.where(inside, tile[k * coul_rows : (k + 1) * coul_rows], own)
        left = jnp.concatenate(
            [jnp.where(hot_h, own[k : k + 1], 0.0).astype(BF16) for k in range(coul_rows)], 0
        )
        flat = lax.dot_general(
            left, hot_g, (((1,), (1,)), ((), ())), preferred_element_type=F32
        )
        flat_sum[...] = flat if i == 0 else flat_sum[...] + flat

    def send_part():
        for k in range(coul_rows):
            for o in range(n_plane):
                at = slice(k * n + o * width, k * n + (o + 1) * width)
                part[o, k * width : (k + 1) * width, :] = flat_sum[at, :].astype(BF16)
        for t in owners:
            start(p_copy(t, plane))
        in_part[plane] = part[plane]

    coul_y, coul_x = rows // NY, rows // (NX * NY)

    def send_dx():
        arrived(in_part.at[pl.ds(0, n_plane - 1)], r_p)
        summed = in_part[0].astype(F32)
        for o in range(1, n_plane):
            summed = summed + in_part[o].astype(F32)
        at = pl.ds(y * coul_y + x * coul_x, coul_x)
        coul16[at, :] = summed.astype(BF16)
        block = coul16.at[at]
        for d in far_first(NX):
            start(remote(block, block, s_dx, r_dx, at_band(x_peer(d), zh, y)))

    def send_dy():
        arrived(coul16.at[pl.ds(y * coul_y, (NX - 1) * coul_x)], r_dx)
        block = coul16.at[pl.ds(y * coul_y, coul_y)]
        for d in far_first(NY):
            start(remote(block, block, s_dy, r_dy, at_band(x, zh, y_peer(d))))

    def wait_dense():
        arrived(coul16.at[pl.ds(0, (NY - 1) * coul_y)], r_dy)
        dense[...] = coul16[...].astype(F32)

    half = width // GROUPS
    block = per_owner * half
    small_block = block - 2 * half
    own_small = lax.rem(plane, period) == period - 1 if period else False
    n_small = n_plane // period if period else 0

    def sized(small, body):
        if not period:
            body(block)
            return
        pl.when(small)(lambda: body(small_block))
        pl.when(jnp.logical_not(small))(lambda: body(block))

    def of_owners(wait, times=1):
        every = times * (block * (n_plane - 1) - 2 * half * n_small)
        if not period:
            wait(orb16.at[pl.ds(0, every)])
            return
        pl.when(own_small)(lambda: wait(orb16.at[pl.ds(0, every + times * 2 * half)]))
        pl.when(jnp.logical_not(own_small))(lambda: wait(orb16.at[pl.ds(0, every)]))

    def of_own(wait, times=1):
        sized(own_small, lambda count: wait(orb16.at[pl.ds(0, times * count * (n_plane - 1))]))

    def send_block(from_ref, to_ref, count, sems, target):
        at = pl.ds(0, count)
        start(remote(from_ref.at[at], to_ref.at[at], sems[0], sems[1], {"plane": target}))

    def wait_group(g, s, i):
        if g == 0:
            wait_gx(i, s)
        elif i == 0:
            wait_gx(2, s)

    def forward(g, s):
        both = wide[:n, :]
        first, second = slim[:n_packed, :], slim[n : n + n_packed, :]
        in_first = lax.broadcasted_iota(jnp.int32, (n_packed, n), 1) < labels[:n_packed, 2:3]
        group = 4

        for i in range(half // group):
            wait_group(g, s, i)
            at = slice(g * rows_g + i * group * n, g * rows_g + (i + 1) * group * n)
            pair = (orb[at, :] * shared[s, at, :].astype(F32)).astype(BF16)
            along = dot(pair, both).astype(BF16)
            planes = [along[k * n : (k + 1) * n] for k in range(group)]
            from_first = dot(first, jnp.concatenate([plane_k[:, :n] for plane_k in planes], 1))
            from_second = dot(second, jnp.concatenate([plane_k[:, n:] for plane_k in planes], 1))
            for k in range(group):
                at = slice(k * n, (k + 1) * n)
                packed = jnp.where(in_first, from_first[:, at], from_second[:, at])
                grid_a[pl.ds(i * group + k, n_packed, stride=half), :] = packed
        for t in owners:
            send_f[s, g, t] = grid_a[pl.ds(pl.multiple_of(t * block, block), block), :].astype(BF16)
            small = lax.rem(t, period) == period - 1 if period else False
            sems = (s_f.at[g, s], r_f.at[g, s])
            sized(small, lambda count: send_block(
                send_f.at[s, g, t], recv_f.at[s, g, plane], count, sems, t))
        at = pl.ds(pl.multiple_of(plane * block, block), block)
        recv_f[s, g, plane] = grid_a[at, :].astype(BF16)

    def middle(s):
        for g in range(GROUPS):
            of_own(lambda region: arrived(region, r_f.at[g, s]))
        twin, cas = wide[n : 3 * n, :], slim[4 * n : 5 * n, :]
        pairs = per_owner // 2
        for first_pair in range(0, pairs, 2):
            js = range(first_pair, min(first_pair + 2, pairs))
            at = [slice(j * 2 * half, (j + 1) * 2 * half) for j in js]
            sticks = [recv_f[s, :, :, a, :].reshape(2 * n, n) for a in at]
            if period and js[-1] == pairs - 1:
                sticks[-1] = jnp.where(own_small, jnp.zeros_like(sticks[-1]), sticks[-1])
            spectrum = dot(twin, jnp.concatenate(sticks, 1))
            scaled = []
            for k, j in enumerate(js):
                for h in range(2):
                    coul = dense[pl.ds(2 * j + h, n, stride=width), :]
                    part_h = spectrum[h * n : (h + 1) * n, k * n : (k + 1) * n]
                    scaled.append((part_h * coul).astype(BF16))
            back = dot(cas, jnp.concatenate(scaled, 1))
            for k in range(len(js)):
                two = [
                    back[:, (2 * k + h) * n : (2 * k + h + 1) * n].reshape(n_plane, GROUPS, half, n)
                    for h in range(2)
                ]
                for g in range(GROUPS):
                    for q in range(n_plane):
                        both = jnp.concatenate([two[0][q, g], two[1][q, g]], 0)
                        send_b[s, g, q, at[k], :] = both.astype(BF16)
        for g in [None] if s == 0 else range(GROUPS):
            def send_all(count):
                for t in owners:
                    at = pl.ds(0, count)
                    own = send_b.at[s, :, t, at] if g is None else send_b.at[s, g, t, at]
                    there = recv_b.at[s, :, plane, at] if g is None else recv_b.at[s, g, plane, at]
                    k = g or 0
                    start(remote(own, there, s_b.at[k, s], r_b.at[k, s], {"plane": t}))

            sized(own_small, send_all)
        for g in range(GROUPS):
            recv_b[s, g, plane] = send_b[s, g, plane]

    def inverse(g, s):
        if s or g == 0:
            of_owners(lambda region: arrived(region, r_b.at[g, s]), 1 if s else GROUPS)
        first, second = wide[3 * n :, :n], wide[3 * n :, n:]
        both = slim[2 * n : 4 * n, :]
        in_first = lax.broadcasted_iota(jnp.int32, (n, n), 1) < labels[:, 2:3]
        grid_b[: n_packed * half, :] = recv_b[s, g].reshape(n_packed * half, n).astype(F32)
        group = 4

        for i in range(half // group):
            packed = [grid_b[pl.ds(i * group + k, n, stride=half), :] for k in range(group)]
            own = [jnp.where(in_first, one, 0.0).astype(BF16) for one in packed]
            other = [jnp.where(in_first, 0.0, one).astype(BF16) for one in packed]
            from_first = dot(first, jnp.concatenate(own, 1))
            from_second = dot(second, jnp.concatenate(other, 1))
            inverse_y = []
            for k in range(group):
                at = slice(k * n, (k + 1) * n)
                inverse_y.append(jnp.concatenate([from_first[:, at], from_second[:, at]], 1).astype(BF16))
            at = slice(g * rows_g + i * group * n, g * rows_g + (i + 1) * group * n)
            term = dot(jnp.concatenate(inverse_y, 0), both) * shared[s, at, :].astype(F32)
            if s == 0:
                total[at, :] = term
            else:
                out_ref[at, :] = (total[at, :] + term).astype(BF16)

    send_x(0)
    round_piece(1)
    send_x(1)
    round_piece(2)
    send_x(2)
    add_part(0)
    send_y(0)
    send_y(1)
    add_part(1)
    send_z(0)
    send_y(2)
    send_z(1)
    for i in range(2, PIECES):
        add_part(i)
    send_gy(0)
    send_part()
    send_gy(1)
    send_z(2)
    loads[3].wait()
    loads[4].wait()
    wait_gy(0)
    send_gx(0, 0)
    wait_gy(1)
    send_gx(1, 0)
    send_gy(2)
    send_gx(0, 1)
    send_gx(1, 1)
    send_dx()
    forward(0, 0)
    wait_gy(2)
    send_gx(2, 0)
    send_gx(2, 1)
    send_dy()
    forward(0, 1)
    forward(1, 0)
    forward(1, 1)
    for p, (_, count) in enumerate(pieces):
        sent(in_x[p].at[pl.ds(0, NX - 1)], s_x.at[p])
        sent(in_y[p].at[pl.ds(0, NY - 1)], s_y.at[p])
        sent(in_z[p], s_z.at[p])
        sent(shared.at[:, pl.ds(0, (NY - 1) * (count // (NX * NY)))], s_gy.at[p])
        for s in range(STEPS):
            sent(shared.at[s, pl.ds(0, (NX - 1) * (count // NX))], s_gx.at[p, s])
    sent(in_part.at[pl.ds(0, n_plane - 1)], s_p)
    grid_b[n_packed * half :, :] = jnp.zeros(((n - n_packed) * half, n), F32)
    for q in range(n_plane):
        if period and q % period == period - 1:
            recv_b[:, :, q, small_block:, :] = jnp.zeros((STEPS, GROUPS, 2 * half, n), BF16)
    wait_dense()
    middle(0)
    sent(coul16.at[pl.ds(0, (NY - 1) * coul_y)], s_dy)
    sent(coul16.at[pl.ds(0, (NX - 1) * coul_x)], s_dx)
    middle(1)
    for g in range(GROUPS):
        for s in range(STEPS):
            of_owners(lambda region: sent(region, s_f.at[g, s]))
    inverse(0, 0)
    inverse(1, 0)
    inverse(0, 1)
    inverse(1, 1)
    of_own(lambda region: sent(region, s_b.at[0, 0]), GROUPS)
    for g in range(GROUPS):
        of_own(lambda region: sent(region, s_b.at[g, 1]))


def on_device(orbitals, coulomb, stick_lists, roots):
    _, width, n, _ = orbitals.shape
    n_plane = n // width
    rows = width * n
    rows_g = rows // GROUPS
    counts = [count for _, count in broadcast_pieces(rows)]
    coul_block = n // (NX * NY) * width
    per_owner = packing(n, n_plane)[1]
    wide, slim, labels = tables(n, n_plane)
    hbm = pl.BlockSpec(memory_space=pl.ANY)
    vmem = pl.BlockSpec(memory_space=pltpu.VMEM)
    dma = pltpu.SemaphoreType.DMA

    def pair_of_sems(*shape):
        return [dma(shape), dma(shape)]

    gs = (GROUPS, STEPS)
    spectra = pltpu.VMEM((STEPS, GROUPS, n_plane, per_owner * width // GROUPS, n), BF16)
    out = pl.pallas_call(
        functools.partial(kernel, n, n_plane),
        out_shape=jax.ShapeDtypeStruct((rows, n), BF16),
        in_specs=[pl.BlockSpec(memory_space=pltpu.SMEM)] + [hbm] * 6,
        out_specs=vmem,
        scratch_shapes=[
            pltpu.VMEM((rows, n), F32),
            pltpu.VMEM(wide.shape, BF16),
            pltpu.VMEM(slim.shape, BF16),
            pltpu.VMEM(labels.shape, jnp.int32),
            pltpu.VMEM((16, coulomb.shape[1]), BF16),
            pltpu.VMEM(stick_lists.shape, jnp.int32),
            pltpu.VMEM((rows, n), BF16),
            *[pltpu.VMEM((NX, count // NX, n), BF16) for count in counts],
            *[pltpu.VMEM((STEPS, count // NX, n), BF16) for count in counts],
            *[pltpu.VMEM((NY, STEPS, count // (NX * NY), n), BF16) for count in counts],
            *[pltpu.VMEM((STEPS, count // (NX * NY), n), BF16) for count in counts * 2],
            pltpu.VMEM((STEPS, rows, n), BF16),
            pltpu.VMEM((n // (NX * NY) * n, n), F32),
            pltpu.VMEM((n_plane, coul_block, n), BF16),
            pltpu.VMEM((n_plane, coul_block, n), BF16),
            pltpu.VMEM((rows, n), BF16),
            pltpu.VMEM((rows, n), F32),
            pltpu.VMEM((rows_g, n), F32),
            pltpu.VMEM((rows_g, n), F32),
            spectra, spectra, spectra, spectra,
            pltpu.VMEM((rows, n), F32),
            dma((len(counts),)),
            dma((5,)),
            *pair_of_sems(len(counts)),
            *pair_of_sems(len(counts)),
            *pair_of_sems(len(counts)),
            *pair_of_sems(len(counts)),
            *pair_of_sems(len(counts), STEPS),
            dma, dma, dma, dma, dma, dma,
            *pair_of_sems(*gs),
            *pair_of_sems(*gs),
        ],
        compiler_params=pltpu.CompilerParams(
            collective_id=0, has_side_effects=True, vmem_limit_bytes=57 * 1024 * 1024
        ),
        name="exchange",
    )(
        roots, orbitals.reshape(rows, n),
        wide, slim, labels, coulomb, stick_lists,
    )
    return out.reshape(1, width, n, n)


def solution(mesh):
    in_specs = (P("band", "plane", None, None), P(None, "plane"), P(), P())
    out_specs = P("band", "plane", None, None)
    return jax.shard_map(
        on_device, mesh=mesh, in_specs=in_specs, out_specs=out_specs, check_vma=False
    )
```
